32 devices in a mesh: section: 2 (over core), row: 4 (over y, x), seq: 4 (over z).
Axes of the slice: x: 2, y: 2, z: 4, core: 2. Of those that a mesh axis runs over, the one named last changes fastest.
Arguments:
- inputs: bfloat16 [16, 1024, 576], P('row', 'seq'), may hold values from -6 to 6
- cotangent: bfloat16 [16, 1024, 576], P('row', 'seq'), may hold values from -6 to 6
- group_ids: int32 [16, 1024], P('row', 'seq'), may hold values from 0 to 2, as said below
- w_query: bfloat16 [2, 576, 576], P('section'), may hold values from -0.25 to 0.25
- w_key: bfloat16 [2, 576, 192], P('section'), may hold values from -0.25 to 0.25
- w_value: bfloat16 [2, 576, 192], P('section'), may hold values from -0.25 to 0.25
- w_out: bfloat16 [2, 576, 576], P('section'), may hold values from -1 to 1
- w_gate: bfloat16 [2, 576, 1536], P('section'), may hold values from -0.25 to 0.25
- w_up: bfloat16 [2, 576, 1536], P('section'), may hold values from -0.25 to 0.25
- w_down: bfloat16 [2, 1536, 576], P('section'), may hold values from -0.15625 to 0.15625
- gain_attn: float32 [2, 576], P('section'), may hold values from 0.5 to 1.5
- gain_mlp: float32 [2, 576], P('section'), may hold values from 0.5 to 1.5
Outputs:
- activations: bfloat16 [2, 16, 1024, 576], P('section', 'row', 'seq')
- input_grads: bfloat16 [2, 16, 1024, 576], P('section', 'row', 'seq')
- grad_query: float32 [2, 576, 576], P('section', 'seq')
- grad_key: float32 [2, 576, 192], P('section', 'seq')
- grad_value: float32 [2, 576, 192], P('section', 'seq')
- grad_out: float32 [2, 576, 576], P('section', 'seq')
- grad_gate: float32 [2, 576, 1536], P('section', 'seq')
- grad_up: float32 [2, 576, 1536], P('section', 'seq')
- grad_down: float32 [2, 1536, 576], P('section', 'seq')
- grad_gain_attn: float32 [2, 576], P('section', 'seq')
- grad_gain_mlp: float32 [2, 576], P('section', 'seq')
The draws below stay inside these ranges and needn't reach their ends.
Inputs may be any that keep to these rules, and one draw needn't show every extreme that they name: `group_ids`: along each row the ids never fall; id 1 begins within the first 256 places and ends within the last 256 places, id 0 comes before it and id 2 after it.
All inputs are finite; a program needn't handle non-finite values.
Results may differ from the reference program's by a relative error of at most 0.04.
Values may be sent and summed in bfloat16 or wider, within the bound.
No kernel may reach another device: no remote copies, remote signals or barrier semaphores. Data moves between devices by JAX's collectives and lax.ppermute only.
A program may use at most 192 MiB of HBM per device.

```python
import jax
import jax.numpy as jnp
from jax import lax

D = 576
HQ = 9
KVH = 3
HD = 64
FF = 1536
SPAN = 256
LEN = 1024
ROWS = 16
LAYERS = 2
KVW = 192


def draw_group_ids(key, part):
    key = jax.random.fold_in(key, 11)
    early_key, late_key = jax.random.split(key)
    opening = jax.random.randint(early_key, (ROWS, 1), 1, SPAN)
    closing = jax.random.randint(late_key, (ROWS, 1), LEN - SPAN + 1, LEN)
    places = jnp.arange(LEN, dtype=jnp.int32)[None, :]
    return (places >= opening).astype(jnp.int32) + (places >= closing).astype(jnp.int32)


def steps_of(stream_key, dims, cuts, smallest, top_value):
    level, own = 1.0, jax.random.fold_in(stream_key, 6)
    for dim, blocks in cuts:
        heights = jnp.exp(jax.random.uniform(jax.random.fold_in(own, dim), (blocks,), jnp.float32, smallest / len(cuts), top_value / len(cuts)))
        level = level * jnp.repeat(heights, dims[dim] // blocks).reshape([-1 if axis == dim else 1 for axis in range(len(dims))])
    return level


def gaussian(rng, dims, deviation, most, cuts=(), kind=jnp.bfloat16):
    values = deviation * jax.random.normal(rng, dims, jnp.float32)
    if cuts:
        values = values * steps_of(rng, dims, cuts, -0.22, 0.18)
    return jnp.clip(values, -most, most).astype(kind)


def setup_inputs(seed: int = 0) -> dict:
    key_of = jax.random.split(jax.random.key(seed), 13)
    return {
        "inputs": gaussian(key_of[0], (ROWS, LEN, D), 1.0, 6.0, ((0, 4), (1, 4))),
        "cotangent": gaussian(key_of[1], (ROWS, LEN, D), 1.0, 6.0, ((0, 4), (1, 4))),
        "group_ids": draw_group_ids(jax.random.fold_in(key_of[12], 71), 0),
        "w_query": gaussian(key_of[3], (LAYERS, D, D), D ** -0.5, 0.25, ((0, 2),)),
        "w_key": gaussian(key_of[4], (LAYERS, D, KVW), D ** -0.5, 0.25, ((0, 2),)),
        "w_value": gaussian(key_of[5], (LAYERS, D, KVW), D ** -0.5, 0.25, ((0, 2),)),
        "w_out": gaussian(key_of[6], (LAYERS, D, D), (D // 16) ** -0.5, 1.0, ((0, 2),)),
        "w_gate": gaussian(key_of[7], (LAYERS, D, FF), D ** -0.5, 0.25, ((0, 2),)),
        "w_up": gaussian(key_of[8], (LAYERS, D, FF), D ** -0.5, 0.25, ((0, 2),)),
        "w_down": gaussian(key_of[9], (LAYERS, FF, D), FF ** -0.5, 0.15625, ((0, 2),)),
        "gain_attn": jnp.clip(1.0 + 0.1 * jax.random.normal(key_of[10], (LAYERS, D), jnp.float32), 0.5, 1.5),
        "gain_mlp": jnp.clip(1.0 + 0.1 * jax.random.normal(key_of[11], (LAYERS, D), jnp.float32), 0.5, 1.5),
    }


EPSILON = 1e-05
PRECISE = lax.Precision.HIGHEST

@jax.custom_vjp
def low(v):
    return lax.optimization_barrier(v.astype(jnp.bfloat16)).astype(jnp.float32)

@jax.custom_vjp
def low_back(v):
    return v

def low_keep(v):
    return (low(v), None)

def low_pass(kept, grad):
    return (grad,)

def back_keep(v):
    return (v, None)

def back_low(kept, grad):
    return (low(grad),)
low.defvjp(low_keep, low_pass)
low_back.defvjp(back_keep, back_low)

def matmul(left_side, right_side):
    return jnp.dot(left_side, right_side, precision=PRECISE)

def rotary(length):
    frequency = 10000.0 ** (-jnp.arange(HD // 2, dtype=jnp.float32) * 2.0 / HD)
    angles = jnp.arange(length, dtype=jnp.float32)[:, None] * frequency[None, :]
    cosine_table = jnp.concatenate([jnp.cos(angles), jnp.cos(angles)], -1)
    sine_table = jnp.concatenate([jnp.sin(angles), jnp.sin(angles)], -1)
    return (cosine_table, sine_table)

def rotate(values, tables):
    cosine_table, sine_table = tables
    half_dim = values.shape[-1] // 2
    turned = jnp.concatenate([-values[..., half_dim:], values[..., :half_dim]], -1)
    return values * cosine_table[:, None, :] + turned * sine_table[:, None, :]

def attention(query, keys, values, doc_row):
    length = query.shape[0]
    block_len = min(length, 1024)
    positions = jnp.arange(length, dtype=jnp.int32)

    def one_block(number):
        offset = number * block_len
        query_rows = lax.dynamic_slice_in_dim(query, offset, block_len, 0)
        row_pos = lax.dynamic_slice_in_dim(positions, offset, block_len, 0)
        row_ids = lax.dynamic_slice_in_dim(doc_row, offset, block_len, 0)
        allowed = (positions[None, :] <= row_pos[:, None]) & (doc_row[None, :] == row_ids[:, None])
        mask = allowed[:, None, None, :]
        scores = low_back(jnp.einsum('nghd,mgd->nghm', query_rows, keys, precision=PRECISE) * HD ** (-0.5))
        masked = jnp.where(mask, scores, -1e+30)
        logsum = jax.nn.logsumexp(masked, axis=-1, keepdims=True)
        attn_probs = jnp.where(mask, jnp.exp(masked - logsum), 0.0)
        return jnp.einsum('nghm,mgd->nghd', low(attn_probs), values, precision=PRECISE)
    blocks = lax.map(jax.checkpoint(one_block), jnp.arange(length // block_len, dtype=jnp.int32))
    return blocks.reshape(length, KVH, HQ // KVH, HD)

def norm_rows(stream, gain):
    return stream * lax.rsqrt(lax.optimization_barrier(jnp.mean(stream * stream, -1, keepdims=True)) + EPSILON) * gain

def layer(stream, params, doc_row, tables):
    w_query, w_key, w_value, w_out, w_gate, w_up, w_down, gain_attn, gain_mlp = params
    length = stream.shape[0]
    normed = low(norm_rows(stream, gain_attn))
    query = low(rotate(low_back(matmul(normed, w_query)).reshape(length, HQ, HD), tables))
    query = query.reshape(length, KVH, HQ // KVH, HD)
    keys = low(rotate(low_back(matmul(normed, w_key)).reshape(length, KVH, HD), tables))
    values = low(low_back(matmul(normed, w_value))).reshape(length, KVH, HD)
    mixed = low(low_back(attention(query, keys, values, doc_row).reshape(length, D)))
    middle = stream + low_back(matmul(mixed, w_out))
    normed_second = low(norm_rows(middle, gain_mlp))
    gate = low_back(matmul(normed_second, w_gate))
    up_proj = low_back(matmul(normed_second, w_up))
    hidden = low(jax.nn.silu(gate) * up_proj)
    return middle + low_back(matmul(hidden, w_down))

def run_section(params, stream, doc_row, tables):
    for number in range(params[0].shape[0]):
        stream = layer(stream, tuple((weight[number] for weight in params)), doc_row, tables)
    return stream

def reference(inputs, cotangent, group_ids, w_query, w_key, w_value, w_out, w_gate, w_up, w_down, gain_attn, gain_mlp):
    params = tuple((weight.astype(jnp.float32) for weight in (w_query, w_key, w_value, w_out, w_gate, w_up, w_down, gain_attn, gain_mlp)))
    half_layers = params[0].shape[0] // 2
    earlier_params = tuple((weight[:half_layers] for weight in params))
    later_params = tuple((weight[half_layers:] for weight in params))
    tables = rotary(inputs.shape[1])

    def one_row(totals, row_data):
        source, target, doc_row = row_data

        def section_fn(section_params, stream):
            return run_section(section_params, stream, doc_row, tables)
        middle_out, back_first = jax.vjp(section_fn, earlier_params, source.astype(jnp.float32))
        passed = middle_out.astype(jnp.bfloat16)
        final_out, back_second = jax.vjp(section_fn, later_params, passed.astype(jnp.float32))
        grads_later, grad_passed = back_second(target.astype(jnp.float32))
        sent_back = grad_passed.astype(jnp.bfloat16)
        grads_earlier, grad_source = back_first(sent_back.astype(jnp.float32))
        whole = tuple((jnp.concatenate([front_part, back_part], 0) for front_part, back_part in zip(grads_earlier, grads_later)))
        totals = tuple((running + added for running, added in zip(totals, whole)))
        section_outs = jnp.stack([passed, final_out.astype(jnp.bfloat16)])
        section_grads = jnp.stack([grad_source.astype(jnp.bfloat16), sent_back])
        return (totals, (section_outs, section_grads))
    zeros = tuple((jnp.zeros_like(weight) for weight in params))
    totals, (section_outs, section_grads) = lax.scan(one_row, zeros, (inputs, cotangent, group_ids))
    return (jnp.swapaxes(section_outs, 0, 1), jnp.swapaxes(section_grads, 0, 1), totals[0], totals[1], totals[2], totals[3], totals[4], totals[5], totals[6], totals[7], totals[8])
```

```python
import jax
import jax.numpy as jnp
from jax import lax
from jax.sharding import PartitionSpec as P

D = 576
HQ = 9
KVH = 3
HD = 64
GROUPS = HQ // KVH
QKW = (HQ + KVH) * HD
KVW = KVH * HD
FF = 1536
CHUNKS = 4
SUB = D // CHUNKS // 2
TILE = FF // 4
EPSILON = 1e-05
MASKED = -1e30
F32 = jnp.float32
BF16 = jnp.bfloat16


def mm(a, b):
    return jnp.dot(a, b, preferred_element_type=F32)


def mm_nt(a, b):
    return lax.dot_general(a, b, (((1,), (1,)), ((), ())), preferred_element_type=F32)


def mm_tn(a, b):
    return lax.dot_general(a, b, (((0,), (0,)), ((), ())), preferred_element_type=F32)


def rotary(positions):
    frequency = 10000.0 ** (-jnp.arange(HD // 2, dtype=F32) * 2.0 / HD)
    angles = positions.astype(F32)[:, None] * frequency[None, :]
    cosine = jnp.concatenate([jnp.cos(angles), jnp.cos(angles)], -1)
    sine = jnp.concatenate([jnp.sin(angles), jnp.sin(angles)], -1)
    return cosine, sine


def rotate(values, tables):
    cosine, sine = tables
    heads = values.reshape(values.shape[0], -1, HD)
    turned = jnp.concatenate([-heads[..., HD // 2 :], heads[..., : HD // 2]], -1)
    return (heads * cosine[:, None] + turned * sine[:, None]).reshape(values.shape)


def unrotate(values, tables):
    cosine, sine = tables
    heads = values.reshape(values.shape[0], -1, HD)
    scaled = heads * sine[:, None]
    turned = jnp.concatenate([scaled[..., HD // 2 :], -scaled[..., : HD // 2]], -1)
    return (heads * cosine[:, None] + turned).reshape(values.shape)


def norm_rows(stream, gain):
    inverse = lax.rsqrt(jnp.mean(stream * stream, -1, keepdims=True) + EPSILON)
    return (stream * inverse * gain).astype(BF16), inverse


def norm_backward(incoming, stream, inverse, gain):
    weighted = incoming * gain
    grad_gain = jnp.sum(incoming * stream * inverse, 0)
    grad_stream = inverse * (
        weighted - stream * inverse * inverse * jnp.mean(weighted * stream, -1, keepdims=True)
    )
    return grad_stream, grad_gain


def project(stream, gain, w_qkv, tables):
    normed, _ = norm_rows(stream, gain)
    raw = mm(normed, w_qkv)
    turned = rotate(raw[:, :QKW], tables).astype(BF16)
    values = raw[:, QKW:].astype(BF16)
    return turned[:, :D], jnp.concatenate([turned[:, D:], values], 1)


def allowed(q_pos, q_ids, k_pos, k_ids):
    return (k_pos[None, :] <= q_pos[:, None]) & (k_ids[None, :] == q_ids[:, None])


def attend(query, kv_all, mask):
    outs, sums = [], []
    for head in range(HQ):
        group = head // GROUPS
        q = query[:, head * HD : (head + 1) * HD]
        k = kv_all[:, group * HD : (group + 1) * HD]
        v = kv_all[:, KVW + group * HD : KVW + (group + 1) * HD]
        scores = jnp.where(mask, mm_nt(q, k) * HD ** (-0.5), MASKED)
        top = jnp.max(scores, -1, keepdims=True)
        weights = jnp.exp(scores - top)
        total = jnp.sum(weights, -1, keepdims=True)
        outs.append(mm(weights.astype(BF16), v) / total)
        sums.append(top + jnp.log(total))
    return jnp.concatenate(outs, 1).astype(BF16), jnp.concatenate(sums, 1)


def attend_backward(query, grad_out, logsum, delta, kv_all, mask):
    grad_q, grad_k, grad_v = [], [0.0] * KVH, [0.0] * KVH
    for head in range(HQ):
        group = head // GROUPS
        q = query[:, head * HD : (head + 1) * HD]
        do = grad_out[:, head * HD : (head + 1) * HD]
        k = kv_all[:, group * HD : (group + 1) * HD]
        v = kv_all[:, KVW + group * HD : KVW + (group + 1) * HD]
        scores = jnp.where(mask, mm_nt(q, k) * HD ** (-0.5), MASKED)
        probs = jnp.exp(scores - logsum[:, head : head + 1])
        grad_scores = (probs * (mm_nt(do, v) - delta[:, head : head + 1])).astype(BF16)
        grad_q.append(mm(grad_scores, k) * HD ** (-0.5))
        grad_k[group] += mm_tn(grad_scores, q) * HD ** (-0.5)
        grad_v[group] += mm_tn(probs.astype(BF16), do)
    return jnp.concatenate(grad_q, 1), jnp.concatenate(grad_k, 1), jnp.concatenate(grad_v, 1)


def finish_forward(stream, attended, params):
    middle = stream + mm(attended, params["w_out"])
    normed, _ = norm_rows(middle, params["gain_mlp"])
    gate = mm(normed, params["w_gate"])
    up = mm(normed, params["w_up"])
    hidden = (gate * jax.nn.sigmoid(gate) * up).astype(BF16)
    return middle, gate, up, middle + mm(hidden, params["w_down"])


def pieces_of(rows, columns_first):
    if columns_first:
        split = rows.reshape(CHUNKS, 2, SUB, 2, 2, TILE)
        return split.transpose(3, 4, 1, 0, 2, 5)
    split = rows.reshape(2, 2, 2, SUB, CHUNKS, TILE)
    return split.transpose(0, 1, 2, 4, 3, 5)


def mlp_backward(grad, middle, gate, up, params):
    branch = grad.astype(BF16)
    normed, inverse = norm_rows(middle, params["gain_mlp"])
    sig = jax.nn.sigmoid(gate)
    hidden = (gate * sig * up).astype(BF16)
    grad_hidden = mm_nt(branch, params["w_down"])
    grad_gate = (grad_hidden * up * sig * (1.0 + gate * (1.0 - sig))).astype(BF16)
    grad_up = (grad_hidden * gate * sig).astype(BF16)
    bundle = jnp.concatenate(
        [
            pieces_of(mm_tn(normed, grad_gate), True),
            pieces_of(mm_tn(normed, grad_up), True),
            pieces_of(mm_tn(branch, hidden), False),
        ],
        -2,
    ).astype(BF16)
    grad_normed = mm_nt(grad_gate, params["w_gate"]) + mm_nt(grad_up, params["w_up"])
    grad_norm, grad_gain = norm_backward(grad_normed, middle, inverse, params["gain_mlp"])
    return bundle, grad + grad_norm, grad_gain


def on_device(
    inputs,
    cotangent,
    group_ids,
    w_query,
    w_key,
    w_value,
    w_out,
    w_gate,
    w_up,
    w_down,
    gain_attn,
    gain_mlp,
):
    core = lax.axis_index("section")
    row = lax.axis_index("row")
    place = lax.axis_index("seq")
    spans = lax.axis_size("seq")
    rows, tokens, _ = inputs.shape
    half = tokens // 2
    chips = spans // rows
    member, wagon = place % rows, place // rows
    own = rows * half
    x_bit, y_bit = row & 1, row >> 1

    def turn(step):
        return [(s, s // rows * rows + (s + step) % rows) for s in range(spans)]

    def trade(blocks, pairs_of, axes):
        out = jnp.zeros_like(blocks)
        out = lax.dynamic_update_index_in_dim(
            out, lax.dynamic_index_in_dim(blocks, member, 0, False), member, 0
        )
        for step in range(1, rows):
            block = lax.dynamic_index_in_dim(blocks, (member + step) % rows, 0, False)
            got = lax.ppermute(block, axes, pairs_of(step))
            out = lax.dynamic_update_index_in_dim(out, got, (member - step) % rows, 0)
        return out

    mine = {
        "w_qkv": jnp.concatenate([w_query[0], w_key[0], w_value[0]], 1),
        "w_out": w_out[0],
        "w_gate": w_gate[0],
        "w_up": w_up[0],
        "w_down": w_down[0],
        "gain_attn": gain_attn,
        "gain_mlp": gain_mlp,
    }
    swap = [(0, 1), (1, 0)]
    theirs = {name: lax.ppermute(value, "section", swap) for name, value in mine.items()}
    layers = [
        {n: jnp.where(core == layer, mine[n], theirs[n]) for n in mine} for layer in range(2)
    ]

    half_in = lax.dynamic_slice_in_dim(inputs, core * half, half, 1)
    ids_row = jnp.pad(group_ids.astype(BF16), ((0, 0), (0, D - tokens)))[:, None]
    packet = jnp.concatenate([half_in, ids_row], 1)
    arrived = trade(packet, turn, "seq")
    stream = arrived[:, :half].reshape(own, D).astype(F32)
    ids = arrived[:, half, :tokens].astype(jnp.int32)
    q_ids = lax.dynamic_slice_in_dim(ids, core * half, half, 1).reshape(own)
    clans = [[b + rows * j for j in range(chips)] for b in range(rows)]
    k_ids = ids.reshape(rows * tokens)
    if chips > 1:
        k_ids = lax.all_gather(k_ids, "seq", axis=0, tiled=True, axis_index_groups=clans)
    length = k_ids.shape[0]
    k_pos = jnp.arange(length, dtype=jnp.int32)
    q_pos = (
        (wagon * rows + jnp.arange(rows, dtype=jnp.int32))[:, None] * tokens
        + core * half
        + jnp.arange(half, dtype=jnp.int32)[None, :]
    ).reshape(own)
    mask = allowed(q_pos, q_ids, k_pos, k_ids)
    tables = rotary(q_pos)
    all_tables = rotary(k_pos)

    half_cot, _ = lax.optimization_barrier(
        (lax.dynamic_slice_in_dim(cotangent, core * half, half, 1), arrived)
    )
    target = trade(half_cot, turn, "seq").reshape(own, D)

    def gather_kv(kv):
        other = lax.ppermute(kv, "section", swap)
        pair = jnp.where(core == 0, jnp.stack([kv, other]), jnp.stack([other, kv]))
        pair = pair.reshape(2, rows, half, 2 * KVW).swapaxes(0, 1).reshape(rows * tokens, 2 * KVW)
        if chips > 1:
            pair = lax.all_gather(pair, "seq", axis=0, tiled=True, axis_index_groups=clans)
        return pair

    def scatter_kv(terms):
        if chips > 1:
            terms = lax.psum_scatter(
                terms.astype(BF16), "seq", scatter_dimension=0, tiled=True, axis_index_groups=clans
            ).astype(F32)
        terms = terms.reshape(rows, 2, half, 2 * KVW)
        away = lax.dynamic_index_in_dim(terms, 1 - core, 1, False).astype(BF16)
        kept = lax.dynamic_index_in_dim(terms, core, 1, False)
        return (kept + lax.ppermute(away, "section", swap).astype(F32)).reshape(own, 2 * KVW)

    saved, streams = [], []
    for layer in range(2):
        params = layers[layer]
        query, kv = project(stream, params["gain_attn"], params["w_qkv"], tables)
        kv_all = gather_kv(kv)
        attended, logsum = attend(query, kv_all, mask)
        middle, gate, up, result = finish_forward(stream, attended, params)
        saved.append((stream, query, kv_all, attended, logsum, middle, gate, up))
        leaving = result.astype(BF16)
        streams.append(leaving)
        stream = leaving.astype(F32)

    def to_owners(outs):
        kept = jnp.where(core == 0, outs[0], outs[1])
        sent = jnp.where(core == 0, outs[1], outs[0])
        got = lax.ppermute(sent, "section", swap)
        pair = jnp.where(core == 0, jnp.stack([kept, got]), jnp.stack([got, kept]))
        blocks = pair.reshape(2, rows, half, D).swapaxes(0, 1).reshape(rows, tokens, D)
        return trade(blocks, turn, "seq")[None]

    activations = to_owners(streams)

    def line(section, r):
        return section * 4 + r

    first_pairs = [(line(0, r), line(0, r ^ 1)) for r in range(4)]
    first_pairs += [(line(1, r), line(1, r ^ 2)) for r in range(4)]
    second_pairs = [(line(0, r), line(0, r ^ 2)) for r in range(4)]
    second_pairs += [(line(1, r), line(1, r ^ 1)) for r in range(4)]

    def relative(pieces, h):
        part = lax.dynamic_index_in_dim(pieces, h, 0, False)
        f_bit = jnp.where(h == 0, x_bit, y_bit)
        g_bit = jnp.where(h == 0, y_bit, x_bit)
        part = jnp.where(f_bit == 1, part[::-1], part)
        part = jnp.where(g_bit == 1, part[:, ::-1], part)
        if chips == 1:
            part = jnp.roll(part, -place, axis=2)
        return part

    def reduce_pieces(pieces):
        kept, sent = relative(pieces, core), relative(pieces, 1 - core)
        got = lax.ppermute(sent, "section", swap)
        out = (kept[1].astype(F32) + got[1]).astype(BF16)
        near = lax.ppermute(out, ("section", "row"), first_pairs)
        out = (kept[0, 1].astype(F32) + got[0, 1] + near[1]).astype(BF16)
        far = lax.ppermute(out, ("section", "row"), second_pairs)
        total = kept[0, 0].astype(F32) + got[0, 0] + near[0] + far
        if chips > 1:
            return lax.psum(total.astype(BF16), "seq")
        total = total.astype(BF16)
        answer = total[0].astype(F32)
        for step in range(1, CHUNKS):
            answer = answer + lax.ppermute(total[step], "seq", turn(step))
        return answer.astype(BF16)

    def whole_grad(pair):
        kept = jnp.where(core == 0, pair[0], pair[1])
        sent = jnp.where(core == 0, pair[1], pair[0])
        got = lax.ppermute(sent, "section", swap)
        both = jnp.stack([jnp.where(core == 0, kept, got), jnp.where(core == 0, got, kept)])
        shares = [both] + [
            lax.ppermute(both, "row", [(r, r ^ d) for r in range(4)]) for d in (1, 2, 3)
        ]
        shares = jnp.take(jnp.stack(shares), jnp.arange(4) ^ row, axis=0)
        shares = shares.reshape((2, 2) + shares.shape[1:])
        return jnp.stack([shares[:, :, 0].swapaxes(0, 1), shares[:, :, 1]]).astype(F32)

    gradient = target.astype(F32)
    input_grads = [None, None]
    mlp_pieces, attn_pieces = [None, None], [None, None]
    for layer in (1, 0):
        params = layers[layer]
        stream, query, kv_all, attended, logsum, middle, gate, up = saved[layer]
        bundle, grad_middle, grad_gain_mlp = mlp_backward(gradient, middle, gate, up, params)
        mlp_pieces[layer] = reduce_pieces(bundle)
        branch = grad_middle.astype(BF16)
        grad_w_out = mm_tn(attended, branch)
        grad_attn = mm_nt(branch, params["w_out"]).astype(BF16)
        delta = (grad_attn.astype(F32) * attended.astype(F32)).reshape(own, HQ, HD).sum(-1)
        grad_q, grad_k, grad_v = attend_backward(query, grad_attn, logsum, delta, kv_all, mask)
        grad_k = unrotate(grad_k, all_tables)
        grad_kv = scatter_kv(jnp.concatenate([grad_k, grad_v], 1)).astype(BF16)
        grad_qkv = jnp.concatenate([unrotate(grad_q, tables).astype(BF16), grad_kv], 1)
        normed, inverse = norm_rows(stream, params["gain_attn"])
        grad_w_qkv = mm_tn(normed, grad_qkv)
        grad_normed = mm_nt(grad_qkv, params["w_qkv"])
        grad_norm, grad_gain_attn = norm_backward(
            grad_normed, stream, inverse, params["gain_attn"]
        )
        wide = jnp.concatenate([grad_w_qkv[:, :QKW], grad_w_out, grad_w_qkv[:, QKW:]], 1)
        gains = jnp.stack([grad_gain_attn, grad_gain_mlp]).reshape(2, CHUNKS, D // CHUNKS)
        gains = jnp.pad(gains.swapaxes(0, 1), ((0, 0), (0, 6), (0, TILE - D // CHUNKS)))
        gains = jnp.broadcast_to(gains, (2, 2, 2) + gains.shape)
        bundle = jnp.concatenate([pieces_of(wide, True), gains], -2).astype(BF16)
        attn_pieces[layer] = reduce_pieces(bundle)
        gradient = (grad_middle + grad_norm).astype(BF16)
        input_grads[layer] = gradient
        gradient = gradient.astype(F32)
    input_grads = to_owners(input_grads)

    mlp = whole_grad(mlp_pieces)
    attn = whole_grad(attn_pieces)

    def rows_of(part):
        if part.ndim == 5:
            return part.transpose(2, 3, 0, 1, 4).reshape(2 * SUB, FF)
        full = part.transpose(3, 2, 4, 0, 1, 5).reshape(D, FF)
        return lax.dynamic_slice_in_dim(full, place * (D // spans), D // spans, 0)

    def down_of(part):
        if part.ndim == 5:
            return part.reshape(D, TILE).T
        full = part.transpose(0, 1, 2, 4, 3, 5).reshape(D, FF)
        return lax.dynamic_slice_in_dim(full, place * (FF // spans), FF // spans, 1).T

    grad_gate = rows_of(mlp[..., :SUB, :])
    grad_up = rows_of(mlp[..., SUB : 2 * SUB, :])
    grad_down = down_of(mlp[..., 2 * SUB :, :])
    wide = rows_of(attn[..., :SUB, :])
    gains = attn[0, 0, 0, ..., SUB : SUB + 2, : D // CHUNKS]
    if gains.ndim == 3:
        gains = gains.swapaxes(0, 1).reshape(2, D)
        gains = lax.dynamic_slice_in_dim(gains, place * (D // spans), D // spans, 1)
    return (
        activations,
        input_grads,
        wide[None, :, :D],
        wide[None, :, D:QKW],
        wide[None, :, QKW + D :],
        wide[None, :, QKW : QKW + D],
        grad_gate[None],
        grad_up[None],
        grad_down[None],
        gains[:1],
        gains[1:],
    )


def solution(mesh):
    weights = P("section", None, None)
    shares = P("section", "seq", None)
    return jax.shard_map(
        on_device,
        mesh=mesh,
        in_specs=(P("row", "seq", None), P("row", "seq", None), P("row", "seq"))
        + (weights,) * 7
        + (P("section", None),) * 2,
        out_specs=(P("section", "row", "seq", None),) * 2
        + (shares,) * 7
        + (P("section", "seq"),) * 2,
        check_vma=False,
    )
```

```python
import functools

import jax
import jax.numpy as jnp
from jax import lax
from jax.experimental import pallas as pl
from jax.experimental.pallas import tpu as pltpu
from jax.sharding import PartitionSpec as P

D = 576
HQ = 9
KVH = 3
HD = 64
GROUPS = HQ // KVH
KVW = KVH * HD
LANES = 128
QKV = 1024
FF = 1536
CHUNKS = 4
SUB = D // CHUNKS // 2
TILE = FF // 4
PACK = 16
SPOTS = {"gate": (0, FF), "up": (FF, FF), "down": (2 * FF, FF), "out": (3 * FF, D)}
WIDE = 3 * FF + D
ROW_STEP = 256
KEY_STEP = 256
SCALE = HD**-0.5
EPSILON = 1e-05
MASKED = -1e30
F32 = jnp.float32
BF16 = jnp.bfloat16
VMEM = pl.BlockSpec(memory_space=pltpu.VMEM)
SMEM = pl.BlockSpec(memory_space=pltpu.SMEM)
ANY = pl.BlockSpec(memory_space=pl.ANY)
SWAP = [(0, 1), (1, 0)]


def mm(a, b):
    return jnp.dot(a, b, preferred_element_type=F32)


def mm_nt(a, b):
    return lax.dot_general(a, b, (((1,), (1,)), ((), ())), preferred_element_type=F32)


def mm_tn(a, b):
    return lax.dot_general(a, b, (((0,), (0,)), ((), ())), preferred_element_type=F32)


def shape(dims, kind=BF16):
    return jax.ShapeDtypeStruct(tuple(dims), kind)


def call(body, ins, specs, outs, scratch, flops, out_specs=None, after=()):
    moved = sum(a.size * a.dtype.itemsize for a in list(ins) + list(outs))
    return pl.pallas_call(
        lambda *refs: body(*refs[len(after) :]),
        out_shape=tuple(outs),
        in_specs=[ANY] * len(after) + list(specs),
        out_specs=tuple(out_specs or [VMEM] * len(outs)),
        scratch_shapes=list(scratch),
        compiler_params=pltpu.CompilerParams(vmem_limit_bytes=56 * 1024 * 1024),
        cost_estimate=pl.CostEstimate(
            flops=int(flops), bytes_accessed=int(moved), transcendentals=0
        ),
    )(*after, *ins)


def lane_of(dims):
    return lax.broadcasted_iota(jnp.int32, dims, len(dims) - 1)


def roll(value, by):
    return pltpu.roll(value, by, value.ndim - 1)


def low_half(dims):
    return lane_of(dims) < HD


def halves(value):
    first = (lane_of(value.shape) & (HD - 1)) < HD // 2
    return jnp.where(first, roll(value, LANES - HD // 2), roll(value, HD // 2))


def tiles_of(count, step):
    step = min(count, step)
    return [(start, step) for start in range(0, count, step)]


def norm_inverse(stream):
    return lax.rsqrt(jnp.mean(stream * stream, -1, keepdims=True) + EPSILON)


def norm_back(incoming, stream, inverse, gain):
    weighted = incoming * gain
    slope = jnp.mean(weighted * stream, -1, keepdims=True)
    grad_gain = jnp.sum(incoming * (stream * inverse), 0, keepdims=True)
    return inverse * (weighted - stream * (inverse * inverse * slope)), grad_gain


def start_copy(layer, core, mine, theirs, target, sem):
    @pl.when(core == layer)
    def _():
        pltpu.make_async_copy(mine, target, sem).start()

    @pl.when(core != layer)
    def _():
        pltpu.make_async_copy(theirs, target, sem).start()


class Weights:
    def __init__(self, layer, core, mine, theirs, targets, sems):
        self.pending = {}
        for number, (name, target) in enumerate(targets.items()):
            if name in ("qkv", "gains"):
                lines = pl.ds(0, D) if name == "qkv" else pl.ds(D, PACK)
                pair = mine["qkv"].at[lines], theirs["qkv"].at[lines]
            else:
                first, width = SPOTS[name]
                pair = mine[name], theirs["big"].at[:, first : first + width]
            start_copy(layer, core, *pair, target, sems.at[number])
            self.pending[name] = (pair[0], target, sems.at[number])

    def wait(self, *names):
        for name in names:
            pltpu.make_async_copy(*self.pending.pop(name)).wait()


def gain_row(lines, kind):
    parts = lines[...].astype(F32)
    parts = [parts[3 * kind + i : 3 * kind + i + 1, :D] for i in range(3)]
    return parts[0] + parts[1] + parts[2]


def project_rows(stream, gain, w_ref, cos, sin, q_ref, kv_ref, start, count):
    normed = (stream * norm_inverse(stream) * gain).astype(BF16)
    raw = mm(normed, w_ref[...])
    low = low_half((count, LANES))
    tiles = []
    for t in range(6):
        tile = raw[:, t * LANES : (t + 1) * LANES]
        tiles.append(tile * cos + halves(tile) * sin)
    rows = pl.ds(start, count)
    for head in range(HQ):
        tile = tiles[head // 2]
        tile = roll(tile, HD) if head % 2 else tile
        q_ref[head, rows, :] = jnp.where(low, tile * SCALE, 0.0).astype(BF16)
    kv_ref[rows, 0:LANES] = jnp.where(low, roll(tiles[4], HD), roll(tiles[5], HD)).astype(BF16)
    kv_ref[rows, LANES : 2 * LANES] = jnp.where(
        low, roll(tiles[5], HD), raw[:, 6 * LANES : 7 * LANES]
    ).astype(BF16)
    kv_ref[rows, 2 * LANES :] = raw[:, 7 * LANES :].astype(BF16)


def place_keys(core, own, other, kz, vz):
    for part, index in ((own, core), (other, 1 - core)):
        blocks, half, _ = part.shape
        low = low_half((blocks, half, LANES))
        tiles = [part[:, :, t * LANES : (t + 1) * LANES].astype(F32) for t in range(3)]
        turned = [roll(tile, HD) for tile in tiles]
        for target, heads in (
            (kz, (tiles[0], turned[0], tiles[1])),
            (vz, (turned[1], tiles[2], turned[2])),
        ):
            for group in range(KVH):
                value = jnp.where(low, heads[group], 1.0).astype(BF16)
                target[group, :, pl.ds(index, 1)] = value[:, None]


def key_rows(ref, group, start, count):
    _, _, _, half, _ = ref.shape
    span = 2 * half
    part = ref[group, start // span : (start + count) // span]
    return part.reshape(count, LANES)


def places(core, wagon, rows, tokens, start, dims, axis):
    half = tokens // 2
    local = lax.broadcasted_iota(jnp.int32, dims, axis) + start
    block, inside = local // half, local % half
    return (wagon * rows + block) * tokens + core * half + inside


def opening(place, docs):
    first, second = docs[0], docs[1]
    return jnp.where(place < first, 0, jnp.where(place < second, first, second))


def query_blocks(geometry):
    rows, tokens, chips = geometry
    half = tokens // 2
    if chips == 1:
        return [(b * half, half, (b + 1) * tokens) for b in range(rows)]
    return [(0, rows * half, chips * rows * tokens)]


def attend(geometry, core, wagon, docs, q_ref, kz, vz, heads_out, q_out):
    rows, tokens, _ = geometry
    for start, count, keys in query_blocks(geometry):
        place = places(core, wagon, rows, tokens, start, (count, 1), 0)
        key_place = lane_of((1, keys))
        allowed = (key_place <= place) & (key_place >= opening(place, docs))
        bias = jnp.where(allowed, 0.0, MASKED)
        low = low_half((GROUPS * count, LANES))
        lane = lane_of((GROUPS * count, LANES))
        for group in range(KVH):
            heads = slice(group * GROUPS, (group + 1) * GROUPS)
            q = q_ref[heads, start : start + count, :].reshape(GROUPS * count, LANES)
            scores = mm_nt(q, key_rows(kz, group, 0, keys))
            scores = scores.reshape(GROUPS, count, keys) + bias[None]
            scores = scores.reshape(GROUPS * count, keys)
            top = jnp.max(scores, -1, keepdims=True)
            weights = jnp.exp(scores - top).astype(BF16)
            out = mm(weights, key_rows(vz, group, 0, keys))
            total = jnp.where(low, 1.0, out)
            lse = -(top + jnp.log(total))
            high = lse.astype(BF16).astype(F32)
            rest = lse - high
            middle = rest.astype(BF16).astype(F32)
            tail = jnp.where(
                lane == HD,
                high,
                jnp.where(lane == HD + 1, middle, jnp.where(lane == HD + 2, rest - middle, 0.0)),
            )
            q_aug = jnp.where(low, q.astype(F32), tail).astype(BF16)
            q_out[heads, start : start + count, :] = q_aug.reshape(GROUPS, count, LANES)
            out = jnp.where(low, out / jnp.where(low, roll(out, HD), 1.0), 0.0)
            heads_out[heads, start : start + count, :] = out.reshape(GROUPS, count, LANES)


def attend_back(geometry, core, wagon, docs, q_ref, do_ref, kz, vz, dq, dk, dv):
    rows, tokens, _ = geometry
    span = tokens
    dk[...] = jnp.zeros_like(dk)
    dv[...] = jnp.zeros_like(dv)
    for start, count, keys in query_blocks(geometry):
        width = GROUPS * count
        lane = lane_of((1, width)) % count
        half = tokens // 2
        local = lane + start
        place = (wagon * rows + local // half) * tokens + core * half + local % half
        first = opening(place, docs)
        for key_start, key_count in tiles_of(keys, KEY_STEP):
            key_place = key_start + lax.broadcasted_iota(jnp.int32, (key_count, 1), 0)
            allowed = (key_place <= place) & (key_place >= first)
            blocks = slice(key_start // span, (key_start + key_count) // span)
            for group in range(KVH):
                heads = slice(group * GROUPS, (group + 1) * GROUPS)
                q = q_ref[heads, start : start + count, :].reshape(width, LANES)
                do = do_ref[heads, start : start + count, :].reshape(width, LANES)
                k = key_rows(kz, group, key_start, key_count)
                v = key_rows(vz, group, key_start, key_count)
                probs = jnp.where(allowed, jnp.exp(mm_nt(k, q)), 0.0)
                slopes = (probs * mm_nt(v, do)).astype(BF16)
                part = (key_count // span, 2, half, LANES)
                dv[group, blocks] += mm(probs.astype(BF16), do).reshape(part)
                dk[group, blocks] += mm(slopes, q).reshape(part)
                back = mm_tn(slopes, k).reshape(GROUPS, count, LANES)
                if key_start == 0:
                    dq[heads, start : start + count, :] = back
                else:
                    dq[heads, start : start + count, :] += back


def pack_heads(ref, rows, tile):
    count = rows.size
    low = low_half((count, LANES))
    first = ref[2 * tile, rows, :]
    if 2 * tile + 1 == HQ:
        return jnp.where(low, first, 0.0)
    return jnp.where(low, first, roll(ref[2 * tile + 1, rows, :], HD))


def piece_bits(h, row):
    x_bit, y_bit = row & 1, row >> 1
    return (x_bit, y_bit) if h == 0 else (y_bit, x_bit)


def store_piece(place, chips, core, row, h, f, g, chunk, value, kept, sent):
    f_bit, g_bit = piece_bits(h, row)
    spot = lax.rem(chunk - place + CHUNKS, CHUNKS) if chips == 1 else chunk
    value = value.astype(BF16)

    @pl.when(core == h)
    def _():
        kept[f ^ f_bit, g ^ g_bit, spot] = value

    @pl.when(core != h)
    def _():
        sent[f ^ f_bit, g ^ g_bit, spot] = value


def pack_kernel(geometry, where, inputs, cotangent, ids, wq, wk, wv, gains, *refs):
    rows, tokens, _ = geometry
    half = tokens // 2
    core, member = where[0], where[3]
    outs, w_ref, (counts, sems) = refs[: 2 * rows], refs[2 * rows], refs[2 * rows + 1 :]
    mine = pl.ds(pl.multiple_of(core * half, half), half)
    copies = []
    for step in range(rows):
        target = lax.rem(member + step, rows)
        docs = ids[pl.ds(target, 1), :]
        first = jnp.sum((docs < 1).astype(F32), -1, keepdims=True)
        second = jnp.sum((docs < 2).astype(F32), -1, keepdims=True)
        lane = lane_of((PACK, half))
        value = jnp.where(lane == 0, first, jnp.where(lane == 1, second, 0.0))
        counts[step] = value.astype(BF16)
        copies += [
            (inputs.at[target, :, mine], outs[step].at[pl.ds(0, D)]),
            (counts.at[step], outs[step].at[pl.ds(D, PACK)]),
            (cotangent.at[target, :, mine], outs[rows + step]),
        ]
    copies = [pltpu.make_async_copy(a, b, sems.at[i]) for i, (a, b) in enumerate(copies)]
    for copy in copies:
        copy.start()
    one = lax.broadcasted_iota(jnp.int32, (KVW, KVW), 0) == lane_of((KVW, KVW))
    one = jnp.where(one, 1.0, 0.0).astype(BF16)
    keys, values = mm_tn(wk[...], one), mm_tn(wv[...], one)
    queries = wq[...].astype(F32)
    zeros = jnp.zeros((D, HD), F32)
    w_ref[:D] = jnp.concatenate([queries, keys, zeros, values], 1).astype(BF16)
    lines = []
    for kind in range(2):
        rest = gains[kind : kind + 1, :]
        for _ in range(3):
            part = rest.astype(BF16).astype(F32)
            lines.append(part)
            rest = rest - part
    lines = jnp.concatenate(lines + [jnp.zeros((PACK - 6, D), F32)], 0)
    lines = jnp.concatenate([lines, jnp.zeros((PACK, QKV - D), F32)], 1)
    w_ref[D:] = lines.astype(BF16)
    for copy in copies:
        copy.wait()


def join_kernel(*refs):
    parts, out, sems = refs[:4], refs[4], refs[5]
    copies = [
        pltpu.make_async_copy(part, out.at[:, first : first + width], sems.at[i])
        for i, (part, (first, width)) in enumerate(zip(parts, SPOTS.values()))
    ]
    for copy in copies:
        copy.start()
    for copy in copies:
        copy.wait()


def unpack(block, half):
    return block[:D].T if half % LANES == 0 else block[:half]


def project_kernel(geometry, where, *refs):
    rows, tokens, _ = geometry
    half = tokens // 2
    packets, refs = refs[:rows], refs[rows:]
    mine, theirs, cos, sin, x_ref, q_ref, kv_ref, w_ref, lines, sems = refs
    core, member = where[0], where[3]
    weights = Weights(
        0, core, {"qkv": mine}, {"qkv": theirs}, {"qkv": w_ref, "gains": lines}, sems
    )
    for step in range(rows):
        x_ref[lax.rem(member - step + rows, rows)] = unpack(packets[step][...], half)
    weights.wait("qkv", "gains")
    gain = gain_row(lines, 0)
    for start, count in tiles_of(rows * half, max(ROW_STEP, half)):
        stream = x_ref[start // half : (start + count) // half].reshape(count, D).astype(F32)
        rows_of = slice(start, start + count)
        project_rows(
            stream, gain, w_ref, cos[rows_of], sin[rows_of], q_ref, kv_ref, start, count
        )


def store_blocks(geometry, where, target, start, value):
    rows, tokens, _ = geometry
    half = tokens // 2
    for block in range(start // half, (start + value.shape[0]) // half):
        part = value[block * half - start : (block + 1) * half - start]
        part = part.T if half % LANES == 0 else part
        target[lax.rem(block - where[3] + rows, rows)] = part


def forward_kernel(layer, geometry, where, docs, *refs):
    x_ref, q_ref, own, other, wg, wu, wd, wo, big, wq, wq2, cos, sin = refs[:13]
    outs = refs[13:]
    q_aug, att, middle_ref, gate_ref, up_ref, y_ref, blocks_ref = outs[:7]
    if layer == 0:
        q_next, kv_next = outs[7:9]
        outs = outs[9:]
    else:
        outs = outs[7:]
    kz, vz, heads, wo_v, wg_v, wu_v, wd_v, lines, sems = outs[:9]
    core, wagon = where[0], where[4]
    mine = {"gate": wg, "up": wu, "down": wd, "out": wo, "qkv": wq}
    theirs = {"big": big, "qkv": wq2}
    names = {"out": wo_v, "gains": lines, "gate": wg_v, "up": wu_v, "down": wd_v}
    weights = Weights(layer, core, mine, theirs, names, sems)
    if layer == 0:
        wq_v, lines_next, sems_next = outs[9:]
        following = Weights(1, core, mine, theirs, {"qkv": wq_v, "gains": lines_next}, sems_next)
    place_keys(core, own, other, kz, vz)
    attend(geometry, core, wagon, docs, q_ref, kz, vz, heads, q_aug)
    weights.wait("out", "gains", "gate", "up", "down")
    gain_mlp = gain_row(lines, 1)
    if layer == 0:
        following.wait("qkv", "gains")
        gain_next = gain_row(lines_next, 0)
    tokens = x_ref.shape[0]
    half = geometry[1] // 2
    for start, count in tiles_of(tokens, max(ROW_STEP, half)):
        rows = pl.ds(start, count)
        for tile in range(4):
            att[rows, tile * LANES : (tile + 1) * LANES] = pack_heads(heads, rows, tile).astype(
                BF16
            )
        att[rows, 4 * LANES :] = heads[HQ - 1, rows, :HD].astype(BF16)
        middle = x_ref[rows, :].astype(F32) + mm(att[rows, :], wo_v[...])
        normed = (middle * norm_inverse(middle) * gain_mlp).astype(BF16)
        gate, up = mm(normed, wg_v[...]), mm(normed, wu_v[...])
        middle_ref[rows, :] = middle
        gate_ref[rows, :] = gate.astype(BF16)
        up_ref[rows, :] = up.astype(BF16)
        hidden = (gate * jax.nn.sigmoid(gate) * up).astype(BF16)
        result = (middle + mm_nt(hidden, wd_v[...])).astype(BF16)
        y_ref[rows, :] = result
        store_blocks(geometry, where, blocks_ref, start, result)
        if layer == 0:
            project_rows(
                result.astype(F32),
                gain_next,
                wq_v,
                cos[rows, :],
                sin[rows, :],
                q_next,
                kv_next,
                start,
                count,
            )


def feed_kernel(layer, geometry, where, *refs):
    rows_in, tokens_in, chips = geometry
    half = tokens_in // 2
    core, row, place, member = where[0], where[1], where[2], where[3]
    if layer == 1:
        packets, refs = refs[:rows_in], refs[rows_in:]
    else:
        grad_ref, refs = refs[0], refs[1:]
    middle_ref, gate_ref, up_ref, wd, big, wq, wq2 = refs[:7]
    refs = refs[7:]
    if layer == 1:
        grad_ref, refs = refs[0], refs[1:]
    dgate, dup, kept, sent, normed, hidden, downs, wd_v, lines, sems = refs
    weights = Weights(
        layer,
        core,
        {"down": wd, "qkv": wq},
        {"big": big, "qkv": wq2},
        {"down": wd_v, "gains": lines},
        sems,
    )
    if layer == 1:
        for step in range(rows_in):
            spot = lax.rem(member - step + rows_in, rows_in)
            grad_ref[spot] = unpack(packets[step][...], half)
    weights.wait("down", "gains")
    gain_mlp = gain_row(lines, 1)
    tokens = middle_ref.shape[0]
    for start, count in tiles_of(tokens, max(ROW_STEP, half)):
        rows = pl.ds(start, count)
        if layer == 1:
            branch = grad_ref[start // half : (start + count) // half].reshape(count, D)
        else:
            branch = grad_ref[rows, :]
        middle = middle_ref[rows, :]
        normed[rows, :] = (middle * norm_inverse(middle) * gain_mlp).astype(BF16)
        gate, up = gate_ref[rows, :].astype(F32), up_ref[rows, :].astype(F32)
        sig = jax.nn.sigmoid(gate)
        lifted = gate * sig
        grad_hidden = mm(branch, wd_v[...])
        hidden[rows, :] = (lifted * up).astype(BF16)
        dgate[rows, :] = (grad_hidden * up * (sig + lifted * (1.0 - sig))).astype(BF16)
        dup[rows, :] = (grad_hidden * lifted).astype(BF16)
    branch = grad_ref[...].reshape(tokens, D)
    for chunk in range(CHUNKS):
        downs[chunk] = mm_tn(branch, hidden[:, chunk * TILE : (chunk + 1) * TILE])
    for h in range(2):
        for f in range(2):
            columns = slice((2 * h + f) * TILE, (2 * h + f + 1) * TILE)
            gates = mm_tn(normed[...], dgate[:, columns])
            ups = mm_tn(normed[...], dup[:, columns])
            for g in range(2):
                for chunk in range(CHUNKS):
                    lines_of = slice((2 * chunk + g) * SUB, (2 * chunk + g + 1) * SUB)
                    spots = pl.ds(((2 * h + f) * 2 + g) * SUB, SUB)
                    value = jnp.concatenate(
                        [gates[lines_of], ups[lines_of], downs[chunk, spots, :]], 0
                    )
                    store_piece(place, chips, core, row, h, f, g, chunk, value, kept, sent)


def middle_kernel(layer, geometry, where, *refs):
    grad_ref, middle_ref, dgate, dup, att, wg, wu, wo, big, wq, wq2 = refs[:11]
    dm_ref, gain_out, do_heads, wg_v, wu_v, wo_v, lines, sems = refs[11:]
    weights = Weights(
        layer,
        where[0],
        {"gate": wg, "up": wu, "out": wo, "qkv": wq},
        {"big": big, "qkv": wq2},
        {"gate": wg_v, "up": wu_v, "out": wo_v, "gains": lines},
        sems,
    )
    weights.wait("gate", "up", "out", "gains")
    gain_mlp = gain_row(lines, 1)
    tokens = middle_ref.shape[0]
    grad_gain = jnp.zeros((1, D), F32)
    for start, count in tiles_of(tokens, ROW_STEP):
        rows = pl.ds(start, count)
        middle = middle_ref[rows, :]
        grad_normed = mm_nt(dgate[rows, :], wg_v[...]) + mm_nt(dup[rows, :], wu_v[...])
        back, more = norm_back(grad_normed, middle, norm_inverse(middle), gain_mlp)
        grad_gain = grad_gain + more
        dm = grad_ref[rows, :].astype(F32) + back
        dm_ref[rows, :] = dm
        grad_att = mm_nt(dm.astype(BF16), wo_v[...]).astype(BF16).astype(F32)
        low = low_half((count, LANES))
        lane = lane_of((count, LANES))
        for head in range(HQ):
            if head < HQ - 1:
                tile = slice(head // 2 * LANES, (head // 2 + 1) * LANES)
                do = grad_att[:, tile]
                out = att[rows, tile].astype(F32)
            else:
                pad = jnp.zeros((count, HD), F32)
                do = jnp.concatenate([grad_att[:, 4 * LANES :], pad], 1)
                out = jnp.concatenate([att[rows, 4 * LANES :].astype(F32), pad], 1)
            if head % 2:
                do, out = roll(do, HD), roll(out, HD)
            do = jnp.where(low, do, 0.0)
            delta = -jnp.sum(do * out, -1, keepdims=True)
            high = delta.astype(BF16).astype(F32)
            do = jnp.where(lane == HD, high, jnp.where(lane == HD + 1, delta - high, do))
            do_heads[head, rows, :] = do.astype(BF16)
    gain_out[...] = grad_gain


def attend_back_kernel(geometry, where, docs, *refs):
    q_aug, do_heads, own, other, cos, sin = refs[:6]
    dq_out, kept, sent = refs[6:9]
    kz, vz, dq, dk, dv = refs[9:]
    core, wagon = where[0], where[4]
    place_keys(core, own, other, kz, vz)
    attend_back(geometry, core, wagon, docs, q_aug, do_heads, kz, vz, dq, dk, dv)
    for start, count in tiles_of(q_aug.shape[1], ROW_STEP):
        rows = pl.ds(start, count)
        for tile in range(5):
            value = pack_heads(dq, rows, tile) * SCALE
            value = value * cos[rows, :] - halves(value) * sin[rows, :]
            dq_out[rows, tile * LANES : (tile + 1) * LANES] = value.astype(BF16)
    _, blocks, _, half, _ = dk.shape
    low = low_half((blocks, half, LANES))
    for target, index in ((kept, core), (sent, 1 - core)):

        def pick(ref, group):
            return ref[group, :, pl.ds(index, 1)].reshape(blocks, half, LANES)

        def join(first, second):
            return jnp.where(low, first, roll(second, HD)).astype(target.dtype)

        target[:, :, 0:LANES] = join(pick(dk, 0), pick(dk, 1))
        target[:, :, LANES : 2 * LANES] = join(pick(dk, 2), pick(dv, 0))
        target[:, :, 2 * LANES :] = join(pick(dv, 1), pick(dv, 2))


def input_back_kernel(layer, geometry, where, *refs):
    rows_in, tokens_in, chips = geometry
    dm_ref, att, x_ref, dq, dkv, dkv2, gain_mlp, wq, wq2, cos, sin = refs[:11]
    dx_ref, blocks_ref, kept, sent, dqkv, normed, da, wq_v, lines, sems = refs[11:]
    core, row, place = where[0], where[1], where[2]
    weights = Weights(
        layer, core, {"qkv": wq}, {"qkv": wq2}, {"qkv": wq_v, "gains": lines}, sems
    )
    weights.wait("qkv", "gains")
    gain = gain_row(lines, 0)
    tokens = x_ref.shape[0]
    half = tokens_in // 2
    grad_gain = jnp.zeros((1, D), F32)
    for start, count in tiles_of(tokens, max(ROW_STEP, half)):
        rows = pl.ds(start, count)
        low = low_half((count, LANES))
        grads = [
            dkv[rows, t * LANES : (t + 1) * LANES]
            + dkv2[rows, t * LANES : (t + 1) * LANES].astype(F32)
            for t in range(3)
        ]
        for tile in range(4):
            lanes = slice(tile * LANES, (tile + 1) * LANES)
            dqkv[rows, lanes] = dq[rows, lanes]
        turned = roll(grads[0], HD)

        def unrotate(value):
            return value * cos[rows, :] - halves(value) * sin[rows, :]

        last = dq[rows, 4 * LANES :].astype(F32)
        dqkv[rows, 4 * LANES : 5 * LANES] = jnp.where(low, last, unrotate(turned)).astype(BF16)
        keys = unrotate(jnp.where(low, turned, roll(grads[1], HD)))
        dqkv[rows, 5 * LANES : 6 * LANES] = keys.astype(BF16)
        dqkv[rows, 6 * LANES : 7 * LANES] = jnp.where(low, 0.0, grads[1]).astype(BF16)
        dqkv[rows, 7 * LANES :] = grads[2].astype(BF16)
        stream = x_ref[rows, :].astype(F32)
        inverse = norm_inverse(stream)
        normed[rows, :] = (stream * inverse * gain).astype(BF16)
        grad_normed = mm_nt(dqkv[rows, :], wq_v[...])
        back, more = norm_back(grad_normed, stream, inverse, gain)
        grad_gain = grad_gain + more
        dm = dm_ref[rows, :]
        dx = (dm + back).astype(BF16)
        dx_ref[rows, :] = dx
        store_blocks(geometry, where, blocks_ref, start, dx)
        da[rows, 0:D] = dm.astype(BF16)
        da[rows, D:] = jnp.zeros((count, 2 * TILE - D), BF16)
    pad = jnp.zeros((1, 2 * TILE - D), F32)
    lines = []
    for vector in (grad_gain, gain_mlp[...]):
        wide = jnp.concatenate([vector, pad], 1)
        lines += [wide[:, :TILE], wide[:, TILE:]]
    lines = jnp.concatenate(lines + [jnp.zeros((4, TILE), F32)], 0)
    for h in range(2):
        for f in range(2):
            if h == 0:
                value = mm_tn(normed[...], dqkv[:, f * TILE : (f + 1) * TILE])
            else:
                value = mm_tn(att[...], da[:, f * TILE : (f + 1) * TILE])
            if h == 1 and f == 1:
                more = mm_tn(normed[...], dqkv[:, 6 * LANES :])
                value = jnp.concatenate(
                    [
                        value[:, :LANES],
                        value[:, LANES : 2 * LANES] + more[:, :LANES],
                        more[:, LANES:],
                    ],
                    1,
                )
            for g in range(2):
                for chunk in range(CHUNKS):
                    part = value[(2 * chunk + g) * SUB : (2 * chunk + g + 1) * SUB]
                    part = jnp.concatenate([part, lines], 0)
                    store_piece(place, chips, core, row, h, f, g, chunk, part, kept, sent)


def pair_kernel(rows, kept, got, *refs):
    outs, sems = refs[:rows], refs[rows]
    copies = []
    for step in range(rows):
        for half, part in ((0, kept), (1, got)):
            sem = sems.at[2 * step + half]
            copies.append(pltpu.make_async_copy(part.at[step], outs[step].at[half], sem))
    for copy in copies:
        copy.start()
    for copy in copies:
        copy.wait()


def owners_kernel(geometry, where, *refs):
    rows, tokens, _ = geometry
    half = tokens // 2
    core, member = where[0], where[3]
    sets = [refs[i : i + rows] for i in range(0, len(refs) - 2, rows)]
    out, sems = refs[-2:]

    def move(blocks):
        copies = []
        for step, block in enumerate(blocks):
            target = lax.rem(member - step + rows, rows)
            for side, index in ((0, core), (1, 1 - core)):
                lanes = pl.ds(pl.multiple_of(index * half, half), half)
                sem = sems.at[2 * step + side]
                copies.append(
                    pltpu.make_async_copy(block.at[side], out.at[target, :, lanes], sem)
                )
        for copy in copies:
            copy.start()
        for copy in copies:
            copy.wait()

    if len(sets) == 1:
        move(sets[0])
    else:
        for number in range(2):

            @pl.when(core == number)
            def _():
                move(sets[number])


def gather_kernel(where, *refs):
    mlp, attn = refs[:4], refs[4:8]
    wq, wk, wv, wo, wg, wu, wd, g1, g2 = refs[8:17]
    wide = refs[17]
    core, row, place = where[0], where[1], where[2]
    for step in range(4):
        peer = row ^ step
        x_bit, y_bit = peer & 1, peer >> 1
        for kind in range(2):
            h = core if kind == 0 else 1 - core
            f = jnp.where(h == 0, x_bit, y_bit)
            g = jnp.where(h == 0, y_bit, x_bit)
            part = mlp[step][kind].astype(F32)
            rows = pl.ds(pl.multiple_of(g * SUB, 8), SUB)
            tile = 2 * h + f
            columns = pl.ds(pl.multiple_of(tile * TILE, LANES), TILE)
            wg[0, rows, columns] = part[:SUB]
            wu[0, rows, columns] = part[SUB : 2 * SUB]
            wd[0, pl.ds(pl.multiple_of((2 * tile + g) * SUB, 8), SUB), :] = part[2 * SUB :]
            part = attn[step][kind].astype(F32)
            wide[rows, columns] = part[:SUB]
    wq[0] = wide[:, :D]
    wk[0] = wide[:, D : D + KVW]
    wo[0] = wide[:, 2 * TILE : 2 * TILE + D]
    wv[0] = wide[:, 2 * TILE + D :]
    lines = attn[0][0, SUB:, :].astype(F32)
    for kind, out in ((0, g1), (1, g2)):
        whole = jnp.concatenate(
            [lines[2 * kind : 2 * kind + 1], lines[2 * kind + 1 : 2 * kind + 2]], 1
        )
        for chunk in range(CHUNKS):

            @pl.when(place == chunk)
            def _():
                out[...] = whole[:, chunk * 2 * SUB : (chunk + 1) * 2 * SUB]


def rotary(place):
    frequency = 10000.0 ** (-jnp.arange(HD // 2, dtype=F32) * 2.0 / HD)
    angles = place.astype(F32)[:, None] * frequency[None, :]
    cosine, sine = jnp.cos(angles), jnp.sin(angles)
    return jnp.concatenate([cosine] * 4, 1), jnp.concatenate([-sine, sine] * 2, 1)


def on_device(
    inputs,
    cotangent,
    group_ids,
    w_query,
    w_key,
    w_value,
    w_out,
    w_gate,
    w_up,
    w_down,
    gain_attn,
    gain_mlp,
):
    core = lax.axis_index("section")
    row = lax.axis_index("row")
    place = lax.axis_index("seq")
    spans = lax.axis_size("seq")
    rows, tokens, _ = inputs.shape
    half = tokens // 2
    chips = spans // rows
    member, wagon = place % rows, place // rows
    own = rows * half
    blocks = chips * rows
    length = blocks * tokens
    geometry = (rows, tokens, chips)
    flipped = half % LANES == 0
    where = jnp.stack([core, row, place, member, wagon]).astype(jnp.int32)
    clans = [[b + rows * j for j in range(chips)] for b in range(rows)]

    def turn(step):
        return [(s, s // rows * rows + (s + step) % rows) for s in range(spans)]

    def sems(count):
        return pltpu.SemaphoreType.DMA((count,))

    def vmem(*dims, kind=BF16):
        return pltpu.VMEM(dims, kind)

    def flip(array):
        return jnp.swapaxes(array, -1, -2)

    gains = jnp.concatenate([gain_attn, gain_mlp], 0)
    pack_ins = [
        where,
        flip(inputs),
        flip(cotangent),
        group_ids,
        w_query[0],
        flip(w_key[0]),
        flip(w_value[0]),
        gains,
    ]
    if flipped:
        packed = call(
            functools.partial(pack_kernel, geometry),
            pack_ins,
            [SMEM] + [ANY] * 2 + [VMEM] * 5,
            [shape((D + PACK, half))] * rows + [shape((D, half))] * rows + [shape((D + PACK, QKV))],
            [vmem(rows, PACK, half), sems(3 * rows)],
            0,
        )
        packets, shares, w_qkv = packed[:rows], packed[rows : 2 * rows], packed[-1]
    else:
        packets, shares = [], []
        below = [jnp.sum((group_ids < i).astype(F32), 1) for i in (1, 2)]
        counts = jnp.pad(jnp.stack(below, 1), ((0, 0), (0, D - 2))).astype(BF16)
        counts = jnp.pad(counts[:, None], ((0, 0), (0, PACK - 1), (0, 0)))
        for step in range(rows):
            target = (member + step) % rows
            for array, outs in ((inputs, packets), (cotangent, shares)):
                part = lax.dynamic_index_in_dim(array, target, 0, False)
                part = lax.dynamic_slice_in_dim(part, core * half, half, 0)
                outs.append(part)
            line = lax.dynamic_index_in_dim(counts, target, 0, False)
            packets[-1] = jnp.concatenate([packets[-1], line], 0)
        w_qkv = jnp.concatenate(
            [w_query[0], w_key[0], jnp.zeros((D, HD), BF16), w_value[0]], 1
        )
        parts, rest = [], gains
        for _ in range(3):
            parts.append(rest.astype(BF16))
            rest = rest - parts[-1].astype(F32)
        lines = jnp.stack(parts, 1).reshape(6, D)
        w_qkv = jnp.concatenate([w_qkv, jnp.pad(lines, ((0, PACK - 6), (0, QKV - D)))], 0)
    packets = [packets[0]] + [
        lax.ppermute(packets[step], "seq", turn(step)) for step in range(1, rows)
    ]
    w_qkv = [w_qkv, lax.ppermute(w_qkv, "section", SWAP)]
    mine = {"gate": w_gate[0], "up": w_up[0], "down": flip(w_down[0]), "out": w_out[0]}
    big = call(
        join_kernel,
        list(mine.values()),
        [ANY] * 4,
        [shape((D, WIDE))],
        [sems(4)],
        0,
        after=w_qkv[:1],
    )[0]
    big = lax.ppermute(big, "section", SWAP)
    if flipped:
        docs = sum(packet[D, :2].astype(F32) for packet in packets)
    else:
        docs = sum(packet[half, :2].astype(F32) for packet in packets)
    if chips > 1:
        docs = lax.psum(docs, "seq", axis_index_groups=clans)
    docs = docs.astype(jnp.int32)
    local = jnp.arange(own, dtype=jnp.int32)
    tables = rotary((wagon * rows + local // half) * tokens + core * half + local % half)

    x_in, query, kv = call(
        functools.partial(project_kernel, geometry),
        [where, *packets, *w_qkv, *tables],
        [SMEM] + [VMEM] * rows + [ANY] * 2 + [VMEM] * 2,
        [shape((rows, half, D)), shape((HQ, own, LANES)), shape((own, 2 * KVW))],
        [vmem(D, QKV), vmem(PACK, QKV), sems(2)],
        2 * own * D * QKV,
    )
    x_in = x_in.reshape(own, D)

    def exchange(kv):
        kv = kv.reshape(rows, half, 2 * KVW)
        if chips > 1:
            kv = lax.all_gather(kv, "seq", axis=0, tiled=True, axis_index_groups=clans)
        return kv, lax.ppermute(kv, "section", SWAP)

    key_scratch = [vmem(KVH, blocks, 2, half, LANES)] * 2
    head_scratch = [vmem(HQ, own, LANES, kind=F32)]
    weight = {"gate": vmem(D, FF), "up": vmem(D, FF), "down": vmem(D, FF), "out": vmem(D, D)}
    lines_scratch = vmem(PACK, QKV)
    attn_flops = 4 * HQ * own * length * LANES
    feed_flops = 2 * own * D * (D + 3 * FF)
    flat = shape((own, D))
    wide = shape((own, FF))
    heads = shape((HQ, own, LANES))
    sent_blocks = shape((rows, D, half) if flipped else (rows, half, D))

    def forward(layer, x, query, kv):
        outs = [heads, flat, shape((own, D), F32), wide, wide, flat, sent_blocks]
        scratch = key_scratch + head_scratch
        scratch += [weight["out"], weight["gate"], weight["up"], weight["down"]]
        scratch += [lines_scratch, sems(5)]
        if layer == 0:
            outs += [heads, shape((own, 2 * KVW))]
            scratch += [vmem(D, QKV), lines_scratch, sems(2)]
        return call(
            functools.partial(forward_kernel, layer, geometry),
            [where, docs, x, query, *kv, *mine.values(), big, *w_qkv, *tables],
            [SMEM] * 2 + [VMEM] * 4 + [ANY] * 7 + [VMEM] * 2,
            outs,
            scratch,
            attn_flops + feed_flops,
        )

    kv0 = exchange(kv)
    q0, att0, middle0, gate0, up0, y0, blocks0, query, kv = forward(0, x_in, query, kv0)
    shares = [shares[0]] + [
        lax.ppermute(shares[step], "seq", turn(step)) for step in range(1, rows)
    ]
    kv1 = exchange(kv)
    q1, att1, middle1, gate1, up1, y1, blocks1 = forward(1, y0, query, kv1)
    mlp_pieces = shape((2, 2, CHUNKS, 3 * SUB, TILE))
    attn_pieces = shape((2, 2, CHUNKS, SUB + 8, TILE))

    def feed(layer, grads, middle, gate, up, after):
        outs = [shape((rows, half, D))] if layer == 1 else []
        return call(
            functools.partial(feed_kernel, layer, geometry),
            [where, *grads, middle, gate, up, mine["down"], big, *w_qkv],
            [SMEM] + [VMEM] * (len(grads) + 3) + [ANY] * 4,
            outs + [wide, wide, mlp_pieces, mlp_pieces],
            [vmem(own, D), vmem(own, FF), vmem(CHUNKS, D, TILE, kind=F32)]
            + [weight["down"], lines_scratch, sems(2)],
            8 * own * D * FF,
            after=after,
        )

    def spread(layer, grad, middle, dgate, dup, att, after):
        return call(
            functools.partial(middle_kernel, layer, geometry),
            [where, grad, middle, dgate, dup, att, mine["gate"], mine["up"], mine["out"]]
            + [big, *w_qkv],
            [SMEM] + [VMEM] * 5 + [ANY] * 6,
            [shape((own, D), F32), shape((1, D), F32), heads],
            [weight["gate"], weight["up"], weight["out"], lines_scratch, sems(4)],
            2 * own * D * (D + 2 * FF),
            after=after,
        )

    def attention_back(q_aug, do_heads, kv, after):
        dq, dkv, dkv_sent = call(
            functools.partial(attend_back_kernel, geometry),
            [where, docs, q_aug, do_heads, *kv, *tables],
            [SMEM] * 2 + [VMEM] * 6,
            [
                shape((own, 5 * LANES)),
                shape((blocks, half, 2 * KVW), F32),
                shape((blocks, half, 2 * KVW)),
            ],
            key_scratch
            + head_scratch
            + [vmem(KVH, blocks, 2, half, LANES, kind=F32)] * 2,
            3 * attn_flops,
            after=after,
        )
        dkv_got = lax.ppermute(dkv_sent, "section", SWAP)
        if chips > 1:
            dkv = lax.psum_scatter(
                (dkv + dkv_got).astype(BF16),
                "seq",
                scatter_dimension=0,
                tiled=True,
                axis_index_groups=clans,
            ).astype(F32)
            dkv_got = jnp.zeros(dkv.shape, BF16)
        return dq, dkv.reshape(own, 2 * KVW), dkv_got.reshape(own, 2 * KVW)

    def input_back(layer, dm, att, x, dq, dkv, dkv_got, gain_grad, after):
        return call(
            functools.partial(input_back_kernel, layer, geometry),
            [where, dm, att, x, dq, dkv, dkv_got, gain_grad, *w_qkv, *tables],
            [SMEM] + [VMEM] * 7 + [ANY] * 2 + [VMEM] * 2,
            [flat, sent_blocks, attn_pieces, attn_pieces],
            [vmem(own, QKV), vmem(own, D), vmem(own, 2 * TILE), vmem(D, QKV)]
            + [lines_scratch, sems(2)],
            4 * own * D * QKV + 2 * own * D * D,
            after=after,
        )

    def line(section, r):
        return section * 4 + r

    first_pairs = [(line(0, r), line(0, r ^ 1)) for r in range(4)]
    first_pairs += [(line(1, r), line(1, r ^ 2)) for r in range(4)]
    second_pairs = [(line(0, r), line(0, r ^ 2)) for r in range(4)]
    second_pairs += [(line(1, r), line(1, r ^ 1)) for r in range(4)]

    def sum_cores(kept, sent):
        got = lax.ppermute(sent, "section", SWAP)
        return (kept[1].astype(F32) + got[1]).astype(BF16), (kept, got)

    def sum_first(out, held):
        kept, got = held
        near = lax.ppermute(out, ("section", "row"), first_pairs)
        out = (kept[0, 1].astype(F32) + got[0, 1] + near[1]).astype(BF16)
        return out, (kept, got, near)

    def sum_second(out, held):
        kept, got, near = held
        far = lax.ppermute(out, ("section", "row"), second_pairs)
        total = (kept[0, 0].astype(F32) + got[0, 0] + near[0] + far).astype(BF16)
        if chips > 1:
            return [lax.psum(total, "seq")]
        return [total[step] for step in range(CHUNKS)]

    def sum_seq(parts):
        if chips > 1:
            return parts[0]
        answer = parts[0].astype(F32)
        for step in range(1, CHUNKS):
            answer = answer + lax.ppermute(parts[step], "seq", turn(step))
        return answer.astype(BF16)

    def pairs_of(layer, kept):
        got = lax.ppermute(kept, "section", [(1 - layer, layer)])
        pairs = call(
            functools.partial(pair_kernel, rows),
            [kept, got],
            [ANY] * 2,
            [shape((2,) + kept.shape[1:])] * rows,
            [sems(2 * rows)],
            0,
        )
        base = layer * spans
        return [pairs[0]] + [
            lax.ppermute(
                pairs[step], ("section", "seq"), [(base + s, base + t) for s, t in turn(step)]
            )
            for step in range(1, rows)
        ]

    def to_owners(sets):
        if flipped:
            out = call(
                functools.partial(owners_kernel, geometry),
                [where, *sets[0], *sets[1]],
                [SMEM] + [ANY] * (2 * rows),
                [shape((rows, D, tokens))],
                [sems(2 * rows)],
                0,
            )[0]
            return flip(out)[None]
        out = jnp.zeros((rows, 2, half, D), BF16)
        for step in range(rows):
            pair = jnp.where(core == 0, sets[0][step], sets[1][step])
            pair = jnp.where(core == 0, pair, pair[::-1])
            out = lax.dynamic_update_index_in_dim(out, pair, (member - step) % rows, 0)
        return out.reshape(1, rows, tokens, D)

    grad1, dgate, dup, kept, sent = feed(1, shares, middle1, gate1, up1, [])
    grad1 = grad1.reshape(own, D)
    out, held_m1 = sum_cores(kept, sent)
    ys0 = pairs_of(0, blocks0)
    dm, gain_grad, do_heads = spread(1, grad1, middle1, dgate, dup, att1, [])
    dq, dkv, dkv_got = attention_back(q1, do_heads, kv1, [out, ys0[3]])
    ys1 = pairs_of(1, blocks1)
    out, held_m1 = sum_first(out, held_m1)
    dx1, blocks1, kept, sent = input_back(
        1, dm, att1, y0, dq, dkv, dkv_got, gain_grad, [out, ys1[1]]
    )
    parts_m1 = sum_second(out, held_m1)
    dgate, dup, kept_m0, sent_m0 = feed(0, [dx1], middle0, gate0, up0, [parts_m1[0]])
    out_a1, held_a1 = sum_cores(kept, sent)
    mlp1 = sum_seq(parts_m1)
    dm, gain_grad, do_heads = spread(0, dx1, middle0, dgate, dup, att0, [out_a1, mlp1])
    out_m0, held_m0 = sum_cores(kept_m0, sent_m0)
    out_a1, held_a1 = sum_first(out_a1, held_a1)
    dq, dkv, dkv_got = attention_back(q0, do_heads, kv0, [out_m0, out_a1])
    dxs1 = pairs_of(1, blocks1)
    parts_a1 = sum_second(out_a1, held_a1)
    out_m0, held_m0 = sum_first(out_m0, held_m0)
    dx0, blocks0, kept, sent = input_back(
        0, dm, att0, x_in, dq, dkv, dkv_got, gain_grad, [out_m0, parts_a1[0], dxs1[1]]
    )
    attn1 = sum_seq(parts_a1)
    mlp0 = sum_seq(sum_second(out_m0, held_m0))
    attn0 = sum_seq(sum_second(*sum_first(*sum_cores(kept, sent))))
    activations = to_owners([ys0, ys1])
    input_grads = to_owners([pairs_of(0, blocks0), dxs1])

    def all_shares(pair):
        kept = jnp.where(core == 0, pair[0], pair[1])
        sent = jnp.where(core == 0, pair[1], pair[0])
        both = jnp.stack([kept, lax.ppermute(sent, "section", SWAP)])
        return [both] + [
            lax.ppermute(both, "row", [(r, r ^ step) for r in range(4)]) for step in range(1, 4)
        ]

    mlp = all_shares([mlp0, mlp1])
    attn = all_shares([attn0, attn1])
    share = D // spans
    if chips == 1:
        grads = call(
            gather_kernel,
            [where, *mlp, *attn],
            [SMEM] + [VMEM] * 8,
            [shape((1, share, width), F32) for width in (D, KVW, KVW, D, FF, FF)]
            + [shape((1, D, TILE), F32)]
            + [shape((1, share), F32)] * 2,
            [vmem(2 * SUB, FF, kind=F32)],
            0,
        )
        grads = list(grads)
        grads[6] = flip(grads[6])
        return (activations, input_grads) + tuple(grads)

    def ordered(parts):
        parts = jnp.stack(parts).astype(F32)
        parts = jnp.take(parts, jnp.arange(4) ^ row, axis=0)
        parts = jnp.take(parts, jnp.arange(2) ^ core, axis=1)
        parts = parts.reshape((2, 2) + parts.shape[1:])
        return jnp.stack([parts[:, :, 0].swapaxes(0, 1), parts[:, :, 1]])

    def rows_of(part):
        full = part.transpose(3, 2, 4, 0, 1, 5).reshape(D, FF)
        return lax.dynamic_slice_in_dim(full, place * share, share, 0)[None]

    mlp, attn = ordered(mlp), ordered(attn)
    downs = mlp[..., 2 * SUB :, :].transpose(0, 1, 2, 4, 3, 5).reshape(D, FF)
    downs = lax.dynamic_slice_in_dim(downs, place * (FF // spans), FF // spans, 1).T[None]
    full = rows_of(attn[..., :SUB, :])
    lines = attn[0, 0, 0, 0, SUB : SUB + 4].reshape(2, 2 * TILE)[:, :D]
    lines = lax.dynamic_slice_in_dim(lines, place * share, share, 1)
    return (
        activations,
        input_grads,
        full[..., :D],
        full[..., D : D + KVW],
        full[..., 2 * TILE + D :],
        full[..., 2 * TILE : 2 * TILE + D],
        rows_of(mlp[..., :SUB, :]),
        rows_of(mlp[..., SUB : 2 * SUB, :]),
        downs,
        lines[:1],
        lines[1:],
    )


def solution(mesh):
    weights = P("section", None, None)
    shares = P("section", "seq", None)
    return jax.shard_map(
        on_device,
        mesh=mesh,
        in_specs=(P("row", "seq", None), P("row", "seq", None), P("row", "seq"))
        + (weights,) * 7
        + (P("section", None),) * 2,
        out_specs=(P("section", "row", "seq", None),) * 2
        + (shares,) * 7
        + (P("section", "seq"),) * 2,
        check_vma=False,
    )
```

```python
import functools

import jax
import jax.numpy as jnp
from jax import lax
from jax.experimental import pallas as pl
from jax.experimental.pallas import tpu as pltpu
from jax.sharding import PartitionSpec as P

D = 576
HQ = 9
KVH = 3
HD = 64
GROUPS = HQ // KVH
KVW = KVH * HD
LANES = 128
QKV = 1024
FF = 1536
CHUNKS = 4
SUB = D // CHUNKS // 2
TILE = FF // 4
PACK = 16
ROW_STEP = 256
KEY_STEP = 256
SCALE = HD**-0.5
EPSILON = 1e-05
MASKED = -1e30
F32 = jnp.float32
BF16 = jnp.bfloat16
VMEM = pl.BlockSpec(memory_space=pltpu.VMEM)
SMEM = pl.BlockSpec(memory_space=pltpu.SMEM)
ANY = pl.BlockSpec(memory_space=pl.ANY)
SWAP = [(0, 1), (1, 0)]


def mm(a, b):
    return jnp.dot(a, b, preferred_element_type=F32)


def mm_nt(a, b):
    return lax.dot_general(a, b, (((1,), (1,)), ((), ())), preferred_element_type=F32)


def mm_tn(a, b):
    return lax.dot_general(a, b, (((0,), (0,)), ((), ())), preferred_element_type=F32)


def shape(dims, kind=BF16):
    return jax.ShapeDtypeStruct(tuple(dims), kind)


def call(body, ins, specs, outs, scratch, flops, stack=()):
    moved = sum(a.size * a.dtype.itemsize for a in list(ins) + list(outs))
    inner, piled = len(ins), len(stack)
    piles = [shape((piled, *stack[0].shape), stack[0].dtype)] if piled else []

    def strip(*refs):
        mid = piled + inner
        if not piled:
            return body(*refs)
        pile, sems = refs[mid], refs[-1]
        copies = [
            pltpu.make_async_copy(source, pile.at[i], sems.at[i])
            for i, source in enumerate(refs[:piled])
        ]
        for copy in copies:
            copy.start()
        body(*refs[piled:mid], *refs[mid + 1 : -1])
        for copy in copies:
            copy.wait()

    return pl.pallas_call(
        strip,
        out_shape=tuple(piles) + tuple(outs),
        in_specs=[ANY] * piled + list(specs),
        out_specs=tuple([VMEM] * (len(piles) + len(outs))),
        scratch_shapes=list(scratch) + [pltpu.SemaphoreType.DMA((piled,))] * len(piles),
        compiler_params=pltpu.CompilerParams(vmem_limit_bytes=56 * 1024 * 1024),
        cost_estimate=pl.CostEstimate(
            flops=int(flops), bytes_accessed=int(moved), transcendentals=0
        ),
    )(*stack, *ins)


def hold(value, *others):
    return lax.optimization_barrier((value, others))[0]


def lane_of(dims):
    return lax.broadcasted_iota(jnp.int32, dims, len(dims) - 1)


def roll(value, by):
    return pltpu.roll(value, by, value.ndim - 1)


def low_half(dims):
    return lane_of(dims) < HD


def halves(value):
    first = (lane_of(value.shape) & (HD - 1)) < HD // 2
    return jnp.where(first, roll(value, LANES - HD // 2), roll(value, HD // 2))


def tiles_of(count, step):
    step = min(count, step)
    return [(start, step) for start in range(0, count, step)]


def norm_inverse(stream):
    return lax.rsqrt(jnp.mean(stream * stream, -1, keepdims=True) + EPSILON)


def norm_back(incoming, stream, inverse, gain):
    weighted = incoming * gain
    slope = jnp.mean(weighted * stream, -1, keepdims=True)
    grad_gain = jnp.sum(incoming * (stream * inverse), 0, keepdims=True)
    return inverse * (weighted - stream * (inverse * inverse * slope)), grad_gain


def start_copy(layer, core, mine, theirs, target, sem):
    @pl.when(core == layer)
    def _():
        pltpu.make_async_copy(mine, target, sem).start()

    @pl.when(core != layer)
    def _():
        pltpu.make_async_copy(theirs, target, sem).start()


class Weights:
    def __init__(self, layer, core, mine, theirs, targets, sems):
        self.pending = {}
        for number, (name, target) in enumerate(targets.items()):
            if name in ("qkv", "gains"):
                lines = pl.ds(0, D) if name == "qkv" else pl.ds(D, PACK)
                pair = mine["qkv"].at[lines], theirs["qkv"].at[lines]
            else:
                pair = mine[name], theirs[name]
            start_copy(layer, core, *pair, target, sems.at[number])
            self.pending[name] = (pair[0], target, sems.at[number])

    def wait(self, *names):
        for name in names:
            pltpu.make_async_copy(*self.pending.pop(name)).wait()


def gain_row(lines, kind):
    parts = lines[...].astype(F32)
    parts = [parts[3 * kind + i : 3 * kind + i + 1, :D] for i in range(3)]
    return parts[0] + parts[1] + parts[2]


def project_rows(stream, gain, w_ref, cos, sin, q_ref, kv_ref, start, count):
    normed = (stream * norm_inverse(stream) * gain).astype(BF16)
    raw = mm(normed, w_ref[...])
    low = low_half((count, LANES))
    tiles = []
    for t in range(6):
        tile = raw[:, t * LANES : (t + 1) * LANES]
        tiles.append(tile * cos + halves(tile) * sin)
    rows = pl.ds(start, count)
    for head in range(HQ):
        tile = tiles[head // 2]
        tile = roll(tile, HD) if head % 2 else tile
        q_ref[head, rows, :] = jnp.where(low, tile * SCALE, 0.0).astype(BF16)
    kv_ref[rows, 0:LANES] = jnp.where(low, roll(tiles[4], HD), roll(tiles[5], HD)).astype(BF16)
    kv_ref[rows, LANES : 2 * LANES] = jnp.where(
        low, roll(tiles[5], HD), raw[:, 6 * LANES : 7 * LANES]
    ).astype(BF16)
    kv_ref[rows, 2 * LANES :] = raw[:, 7 * LANES :].astype(BF16)


def place_keys(core, own, other, kz, vz):
    for part, index in ((own, core), (other, 1 - core)):
        blocks, half, _ = part.shape
        low = low_half((blocks, half, LANES))
        tiles = [part[:, :, t * LANES : (t + 1) * LANES].astype(F32) for t in range(3)]
        turned = [roll(tile, HD) for tile in tiles]
        for target, heads in (
            (kz, (tiles[0], turned[0], tiles[1])),
            (vz, (turned[1], tiles[2], turned[2])),
        ):
            for group in range(KVH):
                value = jnp.where(low, heads[group], 1.0).astype(BF16)
                target[group, :, pl.ds(index, 1)] = value[:, None]


def key_rows(ref, group, start, count):
    _, _, _, half, _ = ref.shape
    span = 2 * half
    part = ref[group, start // span : (start + count) // span]
    return part.reshape(count, LANES)


def places(core, wagon, rows, tokens, start, dims, axis):
    half = tokens // 2
    local = lax.broadcasted_iota(jnp.int32, dims, axis) + start
    block, inside = local // half, local % half
    return (wagon * rows + block) * tokens + core * half + inside


def opening(place, docs):
    first, second = docs[0], docs[1]
    return jnp.where(place < first, 0, jnp.where(place < second, first, second))


def query_blocks(geometry):
    rows, tokens, chips = geometry
    half = tokens // 2
    if chips == 1:
        return [(b * half, half, (b + 1) * tokens) for b in range(rows)]
    return [(0, rows * half, chips * rows * tokens)]


def attend(geometry, core, wagon, docs, q_ref, kz, vz, heads_out, q_out):
    rows, tokens, _ = geometry
    for start, count, keys in query_blocks(geometry):
        place = places(core, wagon, rows, tokens, start, (count, 1), 0)
        key_place = lane_of((1, keys))
        allowed = (key_place <= place) & (key_place >= opening(place, docs))
        bias = jnp.where(allowed, 0.0, MASKED)
        low = low_half((GROUPS * count, LANES))
        lane = lane_of((GROUPS * count, LANES))
        for group in range(KVH):
            heads = slice(group * GROUPS, (group + 1) * GROUPS)
            q = q_ref[heads, start : start + count, :].reshape(GROUPS * count, LANES)
            scores = mm_nt(q, key_rows(kz, group, 0, keys))
            scores = scores.reshape(GROUPS, count, keys) + bias[None]
            scores = scores.reshape(GROUPS * count, keys)
            top = jnp.max(scores, -1, keepdims=True)
            weights = jnp.exp(scores - top).astype(BF16)
            out = mm(weights, key_rows(vz, group, 0, keys))
            total = jnp.where(low, 1.0, out)
            lse = -(top + jnp.log(total))
            high = lse.astype(BF16).astype(F32)
            rest = lse - high
            middle = rest.astype(BF16).astype(F32)
            tail = jnp.where(
                lane == HD,
                high,
                jnp.where(lane == HD + 1, middle, jnp.where(lane == HD + 2, rest - middle, 0.0)),
            )
            q_aug = jnp.where(low, q.astype(F32), tail).astype(BF16)
            q_out[heads, start : start + count, :] = q_aug.reshape(GROUPS, count, LANES)
            out = jnp.where(low, out / jnp.where(low, roll(out, HD), 1.0), 0.0)
            heads_out[heads, start : start + count, :] = out.reshape(GROUPS, count, LANES)


def attend_back(geometry, core, wagon, docs, q_ref, do_ref, kz, vz, dq, dk, dv):
    rows, tokens, _ = geometry
    span = tokens
    dk[...] = jnp.zeros_like(dk)
    dv[...] = jnp.zeros_like(dv)
    for start, count, keys in query_blocks(geometry):
        width = GROUPS * count
        lane = lane_of((1, width)) % count
        half = tokens // 2
        local = lane + start
        place = (wagon * rows + local // half) * tokens + core * half + local % half
        first = opening(place, docs)
        for key_start, key_count in tiles_of(keys, KEY_STEP):
            key_place = key_start + lax.broadcasted_iota(jnp.int32, (key_count, 1), 0)
            allowed = (key_place <= place) & (key_place >= first)
            blocks = slice(key_start // span, (key_start + key_count) // span)
            for group in range(KVH):
                heads = slice(group * GROUPS, (group + 1) * GROUPS)
                q = q_ref[heads, start : start + count, :].reshape(width, LANES)
                do = do_ref[heads, start : start + count, :].reshape(width, LANES)
                k = key_rows(kz, group, key_start, key_count)
                v = key_rows(vz, group, key_start, key_count)
                probs = jnp.where(allowed, jnp.exp(mm_nt(k, q)), 0.0)
                slopes = (probs * mm_nt(v, do)).astype(BF16)
                part = (key_count // span, 2, half, LANES)
                dv[group, blocks] += mm(probs.astype(BF16), do).reshape(part)
                dk[group, blocks] += mm(slopes, q).reshape(part)
                back = mm_tn(slopes, k).reshape(GROUPS, count, LANES)
                if key_start == 0:
                    dq[heads, start : start + count, :] = back
                else:
                    dq[heads, start : start + count, :] += back


def pack_heads(ref, rows, tile):
    count = rows.size
    low = low_half((count, LANES))
    first = ref[2 * tile, rows, :]
    if 2 * tile + 1 == HQ:
        return jnp.where(low, first, 0.0)
    return jnp.where(low, first, roll(ref[2 * tile + 1, rows, :], HD))


def piece_bits(h, row):
    x_bit, y_bit = row & 1, row >> 1
    return (x_bit, y_bit) if h == 0 else (y_bit, x_bit)


def store_piece(place, turned, core, row, h, f, g, chunk, value, kept, sent):
    f_bit, g_bit = piece_bits(h, row)
    spot = lax.rem(chunk - place + CHUNKS, CHUNKS) if turned else chunk
    value = value.astype(BF16)

    @pl.when(core == h)
    def _():
        kept[f ^ f_bit, g ^ g_bit, spot] = value

    @pl.when(core != h)
    def _():
        sent[f ^ f_bit, g ^ g_bit, spot] = value


def pack_kernel(geometry, where, inputs, cotangent, ids, wq, wk, wv, gain1, gain2, *refs):
    rows, tokens, _ = geometry
    half = tokens // 2
    core, member = where[0], where[3]
    outs, w_ref, (counts, sems) = refs[: 2 * rows], refs[2 * rows], refs[2 * rows + 1 :]
    mine = pl.ds(pl.multiple_of(core * half, half), half)
    copies = []
    for step in range(rows):
        target = lax.rem(member + step, rows)
        docs = ids[pl.ds(target, 1), :]
        first = jnp.sum((docs < 1).astype(F32), -1, keepdims=True)
        second = jnp.sum((docs < 2).astype(F32), -1, keepdims=True)
        lane = lane_of((PACK, half))
        value = jnp.where(lane == 0, first, jnp.where(lane == 1, second, 0.0))
        counts[step] = value.astype(BF16)
        copies += [
            (inputs.at[target, :, mine], outs[step].at[pl.ds(0, D)]),
            (counts.at[step], outs[step].at[pl.ds(D, PACK)]),
            (cotangent.at[target, :, mine], outs[rows + step]),
        ]
    copies = [pltpu.make_async_copy(a, b, sems.at[i]) for i, (a, b) in enumerate(copies)]
    for copy in copies:
        copy.start()
    one = lax.broadcasted_iota(jnp.int32, (KVW, KVW), 0) == lane_of((KVW, KVW))
    one = jnp.where(one, 1.0, 0.0).astype(BF16)
    keys, values = mm_tn(wk[...], one), mm_tn(wv[...], one)
    queries = wq[...].astype(F32)
    zeros = jnp.zeros((D, HD), F32)
    w_ref[:D] = jnp.concatenate([queries, keys, zeros, values], 1).astype(BF16)
    lines = []
    for gain in (gain1, gain2):
        rest = gain[...]
        for _ in range(3):
            part = rest.astype(BF16).astype(F32)
            lines.append(part)
            rest = rest - part
    lines = jnp.concatenate(lines + [jnp.zeros((PACK - 6, D), F32)], 0)
    lines = jnp.concatenate([lines, jnp.zeros((PACK, QKV - D), F32)], 1)
    w_ref[D:] = lines.astype(BF16)
    for copy in copies:
        copy.wait()


def unpack(block, half):
    return block[:D].T if half % LANES == 0 else block[:half]


def project_kernel(geometry, where, *refs):
    rows, tokens, _ = geometry
    half = tokens // 2
    packets, refs = refs[:rows], refs[rows:]
    mine, theirs, cos, sin, x_ref, q_ref, kv_ref, w_ref, lines, sems = refs
    core, member = where[0], where[3]
    weights = Weights(
        0, core, {"qkv": mine}, {"qkv": theirs}, {"qkv": w_ref, "gains": lines}, sems
    )
    for step in range(rows):
        x_ref[lax.rem(member - step + rows, rows)] = unpack(packets[step][...], half)
    weights.wait("qkv", "gains")
    gain = gain_row(lines, 0)
    for start, count in tiles_of(rows * half, max(ROW_STEP, half)):
        stream = x_ref[start // half : (start + count) // half].reshape(count, D).astype(F32)
        rows_of = slice(start, start + count)
        project_rows(
            stream, gain, w_ref, cos[rows_of], sin[rows_of], q_ref, kv_ref, start, count
        )


def store_blocks(geometry, where, target, start, value):
    rows, tokens, _ = geometry
    half = tokens // 2
    for block in range(start // half, (start + value.shape[0]) // half):
        part = value[block * half - start : (block + 1) * half - start]
        part = part.T if half % LANES == 0 else part
        spot = lax.rem(block - where[3] + rows, rows)
        target[spot] = part


def forward_kernel(layer, geometry, where, docs, *refs):
    x_ref, q_ref, own, other, cos, sin = refs[:6]
    wg, wg2, wu, wu2, wd, wd2, wo, wo2, wq, wq2 = refs[6:16]
    refs = refs[16:]
    if layer == 1:
        earlier, refs = refs[0], refs[1:]
    q_aug, att, middle_ref, gate_ref, up_ref, y_ref = refs[:6]
    outs = refs[6:]
    if layer == 0:
        blocks_ref, q_next, kv_next = outs[:3]
        outs = outs[3:]
    else:
        pair_refs, blocks_ref = outs[: geometry[0]], outs[geometry[0]]
        outs = outs[geometry[0] + 1 :]
    kz, vz, heads, wo_v, wg_v, wu_v, wd_v, lines, sems = outs[:9]
    core, wagon = where[0], where[4]
    mine = {"gate": wg, "up": wu, "down": wd, "out": wo, "qkv": wq}
    theirs = {"gate": wg2, "up": wu2, "down": wd2, "out": wo2, "qkv": wq2}
    names = {"out": wo_v, "gains": lines, "gate": wg_v, "up": wu_v, "down": wd_v}
    weights = Weights(layer, core, mine, theirs, names, sems)
    if layer == 0:
        wq_v, lines_next, sems_next = outs[9:]
        following = Weights(1, core, mine, theirs, {"qkv": wq_v, "gains": lines_next}, sems_next)
    place_keys(core, own, other, kz, vz)
    attend(geometry, core, wagon, docs, q_ref, kz, vz, heads, q_aug)
    weights.wait("out", "gains", "gate", "up", "down")
    gain_mlp = gain_row(lines, 1)
    if layer == 0:
        following.wait("qkv", "gains")
        gain_next = gain_row(lines_next, 0)
    tokens = x_ref.shape[0]
    half = geometry[1] // 2
    for start, count in tiles_of(tokens, max(ROW_STEP, half)):
        rows = pl.ds(start, count)
        for tile in range(4):
            att[rows, tile * LANES : (tile + 1) * LANES] = pack_heads(heads, rows, tile).astype(
                BF16
            )
        att[rows, 4 * LANES :] = heads[HQ - 1, rows, :HD].astype(BF16)
        middle = x_ref[rows, :].astype(F32) + mm(att[rows, :], wo_v[...])
        normed = (middle * norm_inverse(middle) * gain_mlp).astype(BF16)
        gate, up = mm(normed, wg_v[...]), mm(normed, wu_v[...])
        middle_ref[rows, :] = middle
        gate_ref[rows, :] = gate.astype(BF16)
        up_ref[rows, :] = up.astype(BF16)
        hidden = (gate * jax.nn.sigmoid(gate) * up).astype(BF16)
        result = (middle + mm_nt(hidden, wd_v[...])).astype(BF16)
        y_ref[rows, :] = result
        store_blocks(geometry, where, blocks_ref, start, result)
        if layer == 0:
            project_rows(
                result.astype(F32),
                gain_next,
                wq_v,
                cos[rows, :],
                sin[rows, :],
                q_next,
                kv_next,
                start,
                count,
            )
    if layer == 1:
        for step, pair in enumerate(pair_refs):
            pair[pl.ds(core, 1)] = earlier[pl.ds(step, 1)]
            pair[pl.ds(1 - core, 1)] = blocks_ref[pl.ds(step, 1)]


def feed_kernel(layer, geometry, where, *refs):
    rows_in, tokens_in, chips = geometry
    half = tokens_in // 2
    core, row, place, member = where[0], where[1], where[2], where[3]
    if layer == 1:
        packets, refs = refs[:rows_in], refs[rows_in:]
    else:
        grad_ref, refs = refs[0], refs[1:]
    middle_ref, gate_ref, up_ref, wd, wd2, wq, wq2 = refs[:7]
    refs = refs[7:]
    if layer == 1:
        grad_ref, refs = refs[0], refs[1:]
    dgate, dup, kept, sent, normed, hidden, downs, wd_v, lines, sems = refs
    weights = Weights(
        layer,
        core,
        {"down": wd, "qkv": wq},
        {"down": wd2, "qkv": wq2},
        {"down": wd_v, "gains": lines},
        sems,
    )
    if layer == 1:
        for step in range(rows_in):
            spot = lax.rem(member - step + rows_in, rows_in)
            grad_ref[spot] = unpack(packets[step][...], half)
    weights.wait("down", "gains")
    gain_mlp = gain_row(lines, 1)
    tokens = middle_ref.shape[0]
    for start, count in tiles_of(tokens, max(ROW_STEP, half)):
        rows = pl.ds(start, count)
        if layer == 1:
            branch = grad_ref[start // half : (start + count) // half].reshape(count, D)
        else:
            branch = grad_ref[rows, :]
        middle = middle_ref[rows, :]
        normed[rows, :] = (middle * norm_inverse(middle) * gain_mlp).astype(BF16)
        gate, up = gate_ref[rows, :].astype(F32), up_ref[rows, :].astype(F32)
        sig = jax.nn.sigmoid(gate)
        lifted = gate * sig
        grad_hidden = mm(branch, wd_v[...])
        hidden[rows, :] = (lifted * up).astype(BF16)
        dgate[rows, :] = (grad_hidden * up * (sig + lifted * (1.0 - sig))).astype(BF16)
        dup[rows, :] = (grad_hidden * lifted).astype(BF16)
    branch = grad_ref[...].reshape(tokens, D)
    for chunk in range(CHUNKS):
        downs[chunk] = mm_tn(branch, hidden[:, chunk * TILE : (chunk + 1) * TILE])
    for h in range(2):
        for f in range(2):
            columns = slice((2 * h + f) * TILE, (2 * h + f + 1) * TILE)
            gates = mm_tn(normed[...], dgate[:, columns])
            ups = mm_tn(normed[...], dup[:, columns])
            for g in range(2):
                for chunk in range(CHUNKS):
                    lines_of = slice((2 * chunk + g) * SUB, (2 * chunk + g + 1) * SUB)
                    spots = pl.ds(((2 * h + f) * 2 + g) * SUB, SUB)
                    value = jnp.concatenate(
                        [gates[lines_of], ups[lines_of], downs[chunk, spots, :]], 0
                    )
                    store_piece(place, chips == 1, core, row, h, f, g, chunk, value, kept, sent)


def middle_kernel(layer, geometry, where, *refs):
    grad_ref, middle_ref, dgate, dup, att, wg, wg2, wu, wu2, wo, wo2, wq, wq2 = refs[:13]
    dm_ref, gain_out, do_heads, wg_v, wu_v, wo_v, lines, sems = refs[13:]
    weights = Weights(
        layer,
        where[0],
        {"gate": wg, "up": wu, "out": wo, "qkv": wq},
        {"gate": wg2, "up": wu2, "out": wo2, "qkv": wq2},
        {"gate": wg_v, "up": wu_v, "out": wo_v, "gains": lines},
        sems,
    )
    weights.wait("gate", "up", "out", "gains")
    gain_mlp = gain_row(lines, 1)
    tokens = middle_ref.shape[0]
    grad_gain = jnp.zeros((1, D), F32)
    for start, count in tiles_of(tokens, ROW_STEP):
        rows = pl.ds(start, count)
        middle = middle_ref[rows, :]
        grad_normed = mm_nt(dgate[rows, :], wg_v[...]) + mm_nt(dup[rows, :], wu_v[...])
        back, more = norm_back(grad_normed, middle, norm_inverse(middle), gain_mlp)
        grad_gain = grad_gain + more
        dm = grad_ref[rows, :].astype(F32) + back
        dm_ref[rows, :] = dm
        grad_att = mm_nt(dm.astype(BF16), wo_v[...]).astype(BF16).astype(F32)
        low = low_half((count, LANES))
        lane = lane_of((count, LANES))
        for head in range(HQ):
            if head < HQ - 1:
                tile = slice(head // 2 * LANES, (head // 2 + 1) * LANES)
                do = grad_att[:, tile]
                out = att[rows, tile].astype(F32)
            else:
                pad = jnp.zeros((count, HD), F32)
                do = jnp.concatenate([grad_att[:, 4 * LANES :], pad], 1)
                out = jnp.concatenate([att[rows, 4 * LANES :].astype(F32), pad], 1)
            if head % 2:
                do, out = roll(do, HD), roll(out, HD)
            do = jnp.where(low, do, 0.0)
            delta = -jnp.sum(do * out, -1, keepdims=True)
            high = delta.astype(BF16).astype(F32)
            do = jnp.where(lane == HD, high, jnp.where(lane == HD + 1, delta - high, do))
            do_heads[head, rows, :] = do.astype(BF16)
    gain_out[...] = grad_gain


def attend_back_kernel(geometry, where, docs, *refs):
    q_aug, do_heads, own, other, cos, sin = refs[:6]
    dq_out, kept, sent = refs[6:9]
    kz, vz, dq, dk, dv = refs[9:]
    core, wagon = where[0], where[4]
    place_keys(core, own, other, kz, vz)
    attend_back(geometry, core, wagon, docs, q_aug, do_heads, kz, vz, dq, dk, dv)
    for start, count in tiles_of(q_aug.shape[1], ROW_STEP):
        rows = pl.ds(start, count)
        for tile in range(5):
            value = pack_heads(dq, rows, tile) * SCALE
            value = value * cos[rows, :] - halves(value) * sin[rows, :]
            dq_out[rows, tile * LANES : (tile + 1) * LANES] = value.astype(BF16)
    _, blocks, _, half, _ = dk.shape
    low = low_half((blocks, half, LANES))
    for target, index in ((kept, core), (sent, 1 - core)):

        def pick(ref, group):
            return ref[group, :, pl.ds(index, 1)].reshape(blocks, half, LANES)

        def join(first, second):
            return jnp.where(low, first, roll(second, HD)).astype(target.dtype)

        target[:, :, 0:LANES] = join(pick(dk, 0), pick(dk, 1))
        target[:, :, LANES : 2 * LANES] = join(pick(dk, 2), pick(dv, 0))
        target[:, :, 2 * LANES :] = join(pick(dv, 1), pick(dv, 2))


def input_back_kernel(layer, geometry, where, *refs):
    rows_in, tokens_in, chips = geometry
    dm_ref, att, x_ref, dq, dkv, dkv2, gain_mlp, wq, wq2, cos, sin = refs[:11]
    dx_ref, blocks_refs, refs = refs[11], refs[12 : 12 + rows_in], refs[12 + rows_in :]
    kept, sent, blocks_ref, dqkv, normed, da, wq_v, lines, sems = refs
    core, row, place = where[0], where[1], where[2]
    weights = Weights(
        layer, core, {"qkv": wq}, {"qkv": wq2}, {"qkv": wq_v, "gains": lines}, sems
    )
    weights.wait("qkv", "gains")
    gain = gain_row(lines, 0)
    tokens = x_ref.shape[0]
    half = tokens_in // 2
    grad_gain = jnp.zeros((1, D), F32)
    for start, count in tiles_of(tokens, max(ROW_STEP, half)):
        rows = pl.ds(start, count)
        low = low_half((count, LANES))
        grads = [
            dkv[rows, t * LANES : (t + 1) * LANES]
            + dkv2[rows, t * LANES : (t + 1) * LANES].astype(F32)
            for t in range(3)
        ]
        for tile in range(4):
            lanes = slice(tile * LANES, (tile + 1) * LANES)
            dqkv[rows, lanes] = dq[rows, lanes]
        turned = roll(grads[0], HD)

        def unrotate(value):
            return value * cos[rows, :] - halves(value) * sin[rows, :]

        last = dq[rows, 4 * LANES :].astype(F32)
        dqkv[rows, 4 * LANES : 5 * LANES] = jnp.where(low, last, unrotate(turned)).astype(BF16)
        keys = unrotate(jnp.where(low, turned, roll(grads[1], HD)))
        dqkv[rows, 5 * LANES : 6 * LANES] = keys.astype(BF16)
        dqkv[rows, 6 * LANES : 7 * LANES] = jnp.where(low, 0.0, grads[1]).astype(BF16)
        dqkv[rows, 7 * LANES :] = grads[2].astype(BF16)
        stream = x_ref[rows, :].astype(F32)
        inverse = norm_inverse(stream)
        normed[rows, :] = (stream * inverse * gain).astype(BF16)
        grad_normed = mm_nt(dqkv[rows, :], wq_v[...])
        back, more = norm_back(grad_normed, stream, inverse, gain)
        grad_gain = grad_gain + more
        dm = dm_ref[rows, :]
        dx = (dm + back).astype(BF16)
        dx_ref[rows, :] = dx
        store_blocks(geometry, where, blocks_ref, start, dx)
        da[rows, 0:D] = dm.astype(BF16)
        da[rows, D:] = jnp.zeros((count, 2 * TILE - D), BF16)
    for step, block in enumerate(blocks_refs):
        block[...] = blocks_ref[step]
    pad = jnp.zeros((1, 2 * TILE - D), F32)
    lines = []
    for vector in (grad_gain, gain_mlp[...]):
        wide = jnp.concatenate([vector, pad], 1)
        lines += [wide[:, :TILE], wide[:, TILE:]]
    lines = jnp.concatenate(lines + [jnp.zeros((4, TILE), F32)], 0)
    for h in range(2):
        for f in range(2):
            if h == 0:
                value = mm_tn(normed[...], dqkv[:, f * TILE : (f + 1) * TILE])
            else:
                value = mm_tn(att[...], da[:, f * TILE : (f + 1) * TILE])
            if h == 1 and f == 1:
                more = mm_tn(normed[...], dqkv[:, 6 * LANES :])
                value = jnp.concatenate(
                    [
                        value[:, :LANES],
                        value[:, LANES : 2 * LANES] + more[:, :LANES],
                        more[:, LANES:],
                    ],
                    1,
                )
            for g in range(2):
                for chunk in range(CHUNKS):
                    part = value[(2 * chunk + g) * SUB : (2 * chunk + g + 1) * SUB]
                    part = jnp.concatenate([part, lines], 0)
                    store_piece(place, chips == 1, core, row, h, f, g, chunk, part, kept, sent)


def owners_kernel(geometry, where, *refs):
    rows, tokens, _ = geometry
    half = tokens // 2
    core, member = where[0], where[3]
    sets = [refs[i : i + rows + 1] for i in range(0, len(refs) - 2, rows + 1)]
    out, sems = refs[-2:]

    def move(blocks):
        copies = []
        for step in range(rows):
            target = lax.rem(member - step + rows, rows)
            for side, index in ((0, core), (1, 1 - core)):
                lanes = pl.ds(pl.multiple_of(index * half, half), half)
                source = blocks[rows].at[step] if side else blocks[step]
                if len(sets) == 1:
                    source = source.at[side]
                sem = sems.at[2 * step + side]
                copies.append(pltpu.make_async_copy(source, out.at[target, :, lanes], sem))
        for copy in copies:
            copy.start()
        for copy in copies:
            copy.wait()

    if len(sets) == 1:
        move(sets[0])
    else:
        for number in range(2):

            @pl.when(core == number)
            def _():
                move(sets[number])


def gather_kernel(where, *refs):
    mlp0, mlp1, attn = refs[:2], refs[2:4], refs[4:6]
    wq, wk, wv, wo, wg, wu, wd, g1, g2 = refs[6:15]
    wide, share = refs[15:]
    core, row, place = where[0], where[1], where[2]
    for step in range(4):
        peer = row ^ step
        x_bit, y_bit = peer & 1, peer >> 1
        for kind in range(2):
            h = core if kind == 0 else 1 - core
            f = jnp.where(h == 0, x_bit, y_bit)
            g = jnp.where(h == 0, y_bit, x_bit)

            @pl.when(core == 0)
            def _():
                share[...] = mlp0[kind][step]

            @pl.when(core == 1)
            def _():
                share[...] = mlp1[1 - kind][step]

            part = share[...].astype(F32)
            rows = pl.ds(pl.multiple_of(g * SUB, 8), SUB)
            tile = 2 * h + f
            columns = pl.ds(pl.multiple_of(tile * TILE, LANES), TILE)
            wg[0, rows, columns] = part[:SUB]
            wu[0, rows, columns] = part[SUB : 2 * SUB]
            wd[0, pl.ds(pl.multiple_of((2 * tile + g) * SUB, 8), SUB), :] = part[2 * SUB :]
            part = attn[kind][step, core].astype(F32)
            wide[rows, columns] = part[:SUB]
    wq[0] = wide[:, :D]
    wk[0] = wide[:, D : D + KVW]
    wo[0] = wide[:, 2 * TILE : 2 * TILE + D]
    wv[0] = wide[:, 2 * TILE + D :]
    lines = attn[0][0, core].astype(F32)[SUB:]
    for kind, out in ((0, g1), (1, g2)):
        whole = jnp.concatenate(
            [lines[2 * kind : 2 * kind + 1], lines[2 * kind + 1 : 2 * kind + 2]], 1
        )
        for chunk in range(CHUNKS):

            @pl.when(place == chunk)
            def _():
                out[...] = whole[:, chunk * 2 * SUB : (chunk + 1) * 2 * SUB]


def rotary(place):
    frequency = 10000.0 ** (-jnp.arange(HD // 2, dtype=F32) * 2.0 / HD)
    angles = place.astype(F32)[:, None] * frequency[None, :]
    cosine, sine = jnp.cos(angles), jnp.sin(angles)
    return jnp.concatenate([cosine] * 4, 1), jnp.concatenate([-sine, sine] * 2, 1)


def on_device(
    inputs,
    cotangent,
    group_ids,
    w_query,
    w_key,
    w_value,
    w_out,
    w_gate,
    w_up,
    w_down,
    gain_attn,
    gain_mlp,
):
    core = lax.axis_index("section")
    row = lax.axis_index("row")
    place = lax.axis_index("seq")
    spans = lax.axis_size("seq")
    rows, tokens, _ = inputs.shape
    half = tokens // 2
    chips = spans // rows
    member, wagon = place % rows, place // rows
    own = rows * half
    blocks = chips * rows
    length = blocks * tokens
    geometry = (rows, tokens, chips)
    flipped = half % LANES == 0
    where = jnp.stack([core, row, place, member, wagon]).astype(jnp.int32)
    clans = [[b + rows * j for j in range(chips)] for b in range(rows)]

    def turn(step):
        return [(s, s // rows * rows + (s + step) % rows) for s in range(spans)]

    def sems(count):
        return pltpu.SemaphoreType.DMA((count,))

    def vmem(*dims, kind=BF16):
        return pltpu.VMEM(dims, kind)

    def flip(array):
        return jnp.swapaxes(array, -1, -2)

    pack_ins = [
        where,
        flip(inputs),
        flip(cotangent),
        group_ids,
        w_query[0],
        flip(w_key[0]),
        flip(w_value[0]),
        gain_attn,
        gain_mlp,
    ]
    if flipped:
        packed = call(
            functools.partial(pack_kernel, geometry),
            pack_ins,
            [SMEM] + [ANY] * 2 + [VMEM] * 6,
            [shape((D + PACK, half))] * rows + [shape((D, half))] * rows + [shape((D + PACK, QKV))],
            [vmem(rows, PACK, half), sems(3 * rows)],
            0,
        )
        packets, shares, w_qkv = packed[:rows], packed[rows : 2 * rows], packed[-1]
    else:
        packets, shares = [], []
        below = [jnp.sum((group_ids < i).astype(F32), 1) for i in (1, 2)]
        counts = jnp.pad(jnp.stack(below, 1), ((0, 0), (0, D - 2))).astype(BF16)
        counts = jnp.pad(counts[:, None], ((0, 0), (0, PACK - 1), (0, 0)))
        for step in range(rows):
            target = (member + step) % rows
            for array, outs in ((inputs, packets), (cotangent, shares)):
                part = lax.dynamic_index_in_dim(array, target, 0, False)
                part = lax.dynamic_slice_in_dim(part, core * half, half, 0)
                outs.append(part)
            line = lax.dynamic_index_in_dim(counts, target, 0, False)
            packets[-1] = jnp.concatenate([packets[-1], line], 0)
        w_qkv = jnp.concatenate(
            [w_query[0], w_key[0], jnp.zeros((D, HD), BF16), w_value[0]], 1
        )
        parts, rest = [], jnp.concatenate([gain_attn, gain_mlp], 0)
        for _ in range(3):
            parts.append(rest.astype(BF16))
            rest = rest - parts[-1].astype(F32)
        lines = jnp.stack(parts, 1).reshape(6, D)
        w_qkv = jnp.concatenate([w_qkv, jnp.pad(lines, ((0, PACK - 6), (0, QKV - D)))], 0)
    packets = [packets[0]] + [
        lax.ppermute(packets[step], "seq", turn(step)) for step in range(1, rows)
    ]
    w_qkv = [w_qkv, lax.ppermute(w_qkv, "section", SWAP)]
    mine = {"gate": w_gate[0], "up": w_up[0], "down": flip(w_down[0]), "out": w_out[0]}
    gates = dict(zip(mine, [w_qkv[1], *packets[1:4]]))
    pairs = {
        name: (value, lax.ppermute(hold(value, gates[name]), "section", SWAP))
        for name, value in mine.items()
    }
    pairs["qkv"] = w_qkv

    def weights_of(*names):
        return [side for name in names for side in pairs[name]]

    if flipped:
        docs = sum(packet[D, :2].astype(F32) for packet in packets)
    else:
        docs = sum(packet[half, :2].astype(F32) for packet in packets)
    if chips > 1:
        docs = lax.psum(docs, "seq", axis_index_groups=clans)
    docs = docs.astype(jnp.int32)
    local = jnp.arange(own, dtype=jnp.int32)
    tables = rotary((wagon * rows + local // half) * tokens + core * half + local % half)

    x_in, query, kv = call(
        functools.partial(project_kernel, geometry),
        [where, *packets, *w_qkv, *tables],
        [SMEM] + [VMEM] * rows + [ANY] * 2 + [VMEM] * 2,
        [shape((rows, half, D)), shape((HQ, own, LANES)), shape((own, 2 * KVW))],
        [vmem(D, QKV), vmem(PACK, QKV), sems(2)],
        2 * own * D * QKV,
    )
    x_in = x_in.reshape(own, D)

    def exchange(kv):
        kv = kv.reshape(rows, half, 2 * KVW)
        if chips > 1:
            kv = lax.all_gather(kv, "seq", axis=0, tiled=True, axis_index_groups=clans)
        return kv, lax.ppermute(kv, "section", SWAP)

    key_scratch = [vmem(KVH, blocks, 2, half, LANES)] * 2
    head_scratch = [vmem(HQ, own, LANES, kind=F32)]
    weight = {"gate": vmem(D, FF), "up": vmem(D, FF), "down": vmem(D, FF), "out": vmem(D, D)}
    lines_scratch = vmem(PACK, QKV)
    attn_flops = 4 * HQ * own * length * LANES
    feed_flops = 2 * own * D * (D + 3 * FF)
    flat = shape((own, D))
    wide = shape((own, FF))
    heads = shape((HQ, own, LANES))
    sent_blocks = shape((rows, D, half) if flipped else (rows, half, D))

    def forward(layer, x, query, kv, *earlier):
        outs = [heads, flat, shape((own, D), F32), wide, wide, flat, sent_blocks]
        scratch = key_scratch + head_scratch
        scratch += [weight["out"], weight["gate"], weight["up"], weight["down"]]
        scratch += [lines_scratch, sems(5)]
        if layer == 0:
            outs += [heads, shape((own, 2 * KVW))]
            scratch += [vmem(D, QKV), lines_scratch, sems(2)]
        else:
            scratch = [vmem(*sent_blocks.shape)] + scratch
            outs = outs[:-1] + [shape((2,) + sent_blocks.shape[1:])] * rows
        return call(
            functools.partial(forward_kernel, layer, geometry),
            [where, docs, x, query, *kv, *tables]
            + weights_of("gate", "up", "down", "out", "qkv")
            + list(earlier),
            [SMEM] * 2 + [VMEM] * 6 + [ANY] * 10 + [VMEM] * len(earlier),
            outs,
            scratch,
            attn_flops + feed_flops,
        )

    kv0 = exchange(kv)
    q0, att0, middle0, gate0, up0, y0, blocks0, query, kv = forward(0, x_in, query, kv0)
    shares = [shares[0]] + [
        lax.ppermute(shares[step], "seq", turn(step)) for step in range(1, rows)
    ]
    kv1 = exchange(kv)
    outs = forward(1, y0, query, kv1, blocks0)
    q1, att1, middle1, gate1, up1, y1, *pair_blocks = hold(outs, shares)
    mlp_pieces = shape((2, 2, CHUNKS, 3 * SUB, TILE))
    attn_pieces = shape((2, 2, CHUNKS, SUB + 8, TILE))

    def feed(layer, where, grads, middle, gate, up, **order):
        outs = [shape((rows, half, D))] if layer == 1 else []
        return call(
            functools.partial(feed_kernel, layer, geometry),
            [where, *grads, middle, gate, up] + weights_of("down", "qkv"),
            [SMEM] + [VMEM] * (len(grads) + 3) + [ANY] * 4,
            outs + [wide, wide, mlp_pieces, mlp_pieces],
            [vmem(own, D), vmem(own, FF), vmem(CHUNKS, D, TILE, kind=F32)]
            + [weight["down"], lines_scratch, sems(2)],
            8 * own * D * FF,
            **order,
        )

    def spread(layer, where, grad, middle, dgate, dup, att, **order):
        return call(
            functools.partial(middle_kernel, layer, geometry),
            [where, grad, middle, dgate, dup, att] + weights_of("gate", "up", "out", "qkv"),
            [SMEM] + [VMEM] * 5 + [ANY] * 8,
            [shape((own, D), F32), shape((1, D), F32), heads],
            [weight["gate"], weight["up"], weight["out"], lines_scratch, sems(4)],
            2 * own * D * (D + 2 * FF),
            **order,
        )

    def attention_back(where, q_aug, do_heads, kv, **order):
        return call(
            functools.partial(attend_back_kernel, geometry),
            [where, docs, q_aug, do_heads, *kv, *tables],
            [SMEM] * 2 + [VMEM] * 6,
            [
                shape((own, 5 * LANES)),
                shape((blocks, half, 2 * KVW), F32),
                shape((blocks, half, 2 * KVW)),
            ],
            key_scratch
            + head_scratch
            + [vmem(KVH, blocks, 2, half, LANES, kind=F32)] * 2,
            3 * attn_flops,
            **order,
        )

    def trade_keys(dq, dkv, dkv_sent):
        dkv_got = lax.ppermute(dkv_sent, "section", SWAP)
        if chips > 1:
            dkv = lax.psum_scatter(
                (dkv + dkv_got).astype(BF16),
                "seq",
                scatter_dimension=0,
                tiled=True,
                axis_index_groups=clans,
            ).astype(F32)
            dkv_got = jnp.zeros(dkv.shape, BF16)
        return dq, dkv.reshape(own, 2 * KVW), dkv_got.reshape(own, 2 * KVW)

    def input_back(layer, where, dm, att, x, dq, dkv, dkv_got, gain_grad, **order):
        return call(
            functools.partial(input_back_kernel, layer, geometry),
            [where, dm, att, x, dq, dkv, dkv_got, gain_grad, *w_qkv, *tables],
            [SMEM] + [VMEM] * 7 + [ANY] * 2 + [VMEM] * 2,
            [flat]
            + [shape(sent_blocks.shape[1:])] * rows
            + [attn_pieces, attn_pieces],
            [vmem(*sent_blocks.shape), vmem(own, QKV), vmem(own, D), vmem(own, 2 * TILE), vmem(D, QKV)]
            + [lines_scratch, sems(2)],
            4 * own * D * QKV + 2 * own * D * D,
            **order,
        )

    def line(section, r):
        return section * 4 + r

    first_pairs = [(line(0, r), line(0, r ^ 1)) for r in range(4)]
    first_pairs += [(line(1, r), line(1, r ^ 2)) for r in range(4)]
    second_pairs = [(line(0, r), line(0, r ^ 2)) for r in range(4)]
    second_pairs += [(line(1, r), line(1, r ^ 1)) for r in range(4)]

    def to_core(sent):
        return lax.ppermute(sent, "section", SWAP)

    def sum_cores(kept, got):
        return (kept[1].astype(F32) + got[1]).astype(BF16)

    def to_first(out):
        return lax.ppermute(out, ("section", "row"), first_pairs)

    def sum_first(kept, got, near):
        return (kept[0, 1].astype(F32) + got[0, 1] + near[1]).astype(BF16)

    def to_second(out):
        return lax.ppermute(out, ("section", "row"), second_pairs)

    def sum_second(kept, got, near, far):
        return (kept[0, 0].astype(F32) + got[0, 0] + near[0] + far).astype(BF16)

    def to_seq(total):
        if chips > 1:
            return [lax.psum(total, "seq")]
        return [total[0]] + [
            lax.ppermute(total[step], "seq", turn(step)) for step in range(1, CHUNKS)
        ]

    def sum_seq(first, others):
        return sum((part.astype(F32) for part in others), first.astype(F32)).astype(BF16)

    def to_rows(blocks):
        return list(blocks[:1]) + [
            lax.ppermute(blocks[step], "seq", turn(step)) for step in range(1, rows)
        ]

    def to_owners(sets):
        if flipped:
            return call(
                functools.partial(owners_kernel, geometry),
                [where, *sum(sets, [])],
                [SMEM] + [ANY] * ((rows + 1) * len(sets)),
                [shape((rows, D, tokens))],
                [sems(2 * rows)],
                0,
            )[0]
        out = jnp.zeros((rows, 2, half, D), BF16)
        for step in range(rows):
            if len(sets) == 1:
                pair = [sets[0][step][0], sets[0][rows][step][1]]
            else:
                pair = [
                    jnp.where(core == 0, sets[0][step], sets[1][step]),
                    jnp.where(core == 0, sets[0][rows][step], sets[1][rows][step]),
                ]
            pair = jnp.where(core == 0, jnp.stack(pair), jnp.stack(pair[::-1]))
            out = lax.dynamic_update_index_in_dim(out, pair, (member - step) % rows, 0)
        return flip(out.reshape(rows, tokens, D))

    def to_all(piece):
        return [piece] + [
            lax.ppermute(piece, "row", [(r, r ^ step) for r in range(4)]) for step in range(1, 4)
        ]

    ys = to_rows(pair_blocks)
    grad1, dgate, dup, kept_m1, sent = hold(feed(1, where, shares, middle1, gate1, up1), ys[1])
    grad1 = grad1.reshape(own, D)
    got_m1 = to_core(sent)

    dm, gain_grad, do_heads = hold(
        spread(1, where, grad1, middle1, dgate, dup, att1), ys[2], got_m1
    )

    out = sum_cores(hold(kept_m1, dm), got_m1)
    near_m1 = to_first(out)
    kept_m1, *outs = hold(
        (kept_m1, *attention_back(where, q1, do_heads, kv1)), ys[3], near_m1
    )
    dq, dkv, dkv_got = trade_keys(*outs)

    out = sum_first(kept_m1, got_m1, near_m1)
    far_m1 = to_second(out)
    outs = input_back(
        1, hold(where, out), dm, att1, y0, dq, dkv, dkv_got, gain_grad, stack=ys
    )
    kept_m1, pile, dx1, *blocks1, kept_a1, sent = hold((kept_m1, *outs), far_m1)
    got_a1 = to_core(sent)
    ys.append(to_core(pile))

    total = sum_second(kept_m1, got_m1, near_m1, far_m1)
    parts_m1 = to_seq(total)
    outs = feed(0, hold(where, total), [dx1], middle0, gate0, up0)
    dgate, dup, kept_m0, sent = hold(outs, ys[rows], got_a1, parts_m1)
    got_m0 = to_core(sent)

    mlp1 = to_all(sum_seq(hold(parts_m1[0], dgate), parts_m1[1:]))
    out = sum_cores(hold(kept_a1, dgate), got_a1)
    near_a1 = to_first(out)
    activations = to_owners([ys])
    outs = spread(0, hold(where, out, mlp1[0]), dx1, middle0, dgate, dup, att0)
    dm, gain_grad, do_heads = hold(outs, activations, mlp1, near_a1, got_m0)

    out_a1 = sum_first(hold(kept_a1, dm), got_a1, near_a1)
    far_a1 = to_second(out_a1)
    out_m0 = sum_cores(hold(kept_m0, dm), got_m0)
    near_m0 = to_first(out_m0)
    dxs1 = to_rows(hold(blocks1, dm))
    pile, *outs = attention_back(hold(where, out_a1, out_m0), q0, do_heads, kv0, stack=mlp1)
    kept_a1, kept_m0, pile, *outs = hold(
        (kept_a1, kept_m0, pile, *outs), far_a1, near_m0, dxs1
    )
    mlp1 = lax.ppermute(pile, "section", [(0, 1)]), pile
    dq, dkv, dkv_got = trade_keys(*outs)

    total_a1 = sum_second(kept_a1, got_a1, near_a1, far_a1)
    parts_a1 = to_seq(total_a1)
    out = sum_first(kept_m0, got_m0, near_m0)
    far_m0 = to_second(out)
    outs = input_back(
        0, hold(where, out, total_a1), dm, att0, x_in, dq, dkv, dkv_got, gain_grad, stack=dxs1
    )
    kept_m0, pile, dx0, *blocks0, kept_a0, sent = hold(
        (kept_m0, *outs), far_m0, parts_a1, mlp1[0]
    )

    got_a0 = to_core(sent)
    total = sum_second(kept_m0, got_m0, near_m0, far_m0)
    parts_m0 = to_seq(total)
    out = sum_cores(hold(kept_a0, total), got_a0)
    near_a0 = to_first(out)
    out = sum_first(hold(kept_a0, parts_m0, near_a0), got_a0, near_a0)
    far_a0 = to_second(out)
    piece = sum_seq(hold(parts_m0[0], out), parts_m0[1:])
    mlp0 = to_all(piece)
    total = sum_second(hold(kept_a0, piece), got_a0, near_a0, far_a0)
    parts_a0 = to_seq(total)
    blocks0, pile = hold((blocks0, pile), total)
    dxs1.append(lax.ppermute(pile, "section", [(0, 1)]))
    dxs0 = to_rows(blocks0)
    attn = jnp.stack([sum_seq(p[0], p[1:]) for p in (parts_a0, parts_a1)])
    mlp0 = hold(mlp0, attn)
    attn = to_all(attn)
    mlp0 = jnp.stack(mlp0)
    mlp0 = mlp0, lax.ppermute(mlp0, "section", [(1, 0)])
    dxs0 = hold(dxs0, attn)
    attn = jnp.stack(attn)
    attn = attn, to_core(attn)
    dxs0.append(lax.ppermute(hold(jnp.stack(dxs0), attn[0]), "section", [(1, 0)]))
    input_grads = to_owners([dxs0, dxs1])
    input_grads = flip(input_grads)[None]
    activations = flip(activations)[None]
    share = D // spans
    if chips == 1:
        grads = call(
            gather_kernel,
            [where, *mlp0, *mlp1, *attn],
            [SMEM] + [VMEM] * 6,
            [shape((1, share, width), F32) for width in (D, KVW, KVW, D, FF, FF)]
            + [shape((1, D, TILE), F32)]
            + [shape((1, share), F32)] * 2,
            [vmem(2 * SUB, FF, kind=F32), vmem(3 * SUB, TILE)],
            0,
        )
        grads = list(grads)
        grads[6] = flip(grads[6])
        return (activations, input_grads) + tuple(grads)

    def ordered(parts):
        parts = parts.reshape(2, 4, *parts.shape[1:]).swapaxes(0, 1).astype(F32)
        parts = jnp.take(parts, jnp.arange(4) ^ row, axis=0)
        parts = jnp.take(parts, jnp.arange(2) ^ core, axis=1)
        parts = parts.reshape((2, 2) + parts.shape[1:])
        return jnp.stack([parts[:, :, 0].swapaxes(0, 1), parts[:, :, 1]])

    def rows_of(part):
        full = part.transpose(3, 2, 4, 0, 1, 5).reshape(D, FF)
        return lax.dynamic_slice_in_dim(full, place * share, share, 0)[None]

    mlp1 = jnp.concatenate([mlp1[1], mlp1[0]], 0)
    mlp = ordered(jnp.where(core == 0, jnp.concatenate(mlp0, 0), mlp1))
    attn = ordered(lax.dynamic_index_in_dim(jnp.concatenate(attn, 0), core, 1, False))
    downs = mlp[..., 2 * SUB :, :].transpose(0, 1, 2, 4, 3, 5).reshape(D, FF)
    downs = lax.dynamic_slice_in_dim(downs, place * (FF // spans), FF // spans, 1).T[None]
    full = rows_of(attn[..., :SUB, :])
    lines = attn[0, 0, 0, 0, SUB : SUB + 4].reshape(2, 2 * TILE)[:, :D]
    lines = lax.dynamic_slice_in_dim(lines, place * share, share, 1)
    return (
        activations,
        input_grads,
        full[..., :D],
        full[..., D : D + KVW],
        full[..., 2 * TILE + D :],
        full[..., 2 * TILE : 2 * TILE + D],
        rows_of(mlp[..., :SUB, :]),
        rows_of(mlp[..., SUB : 2 * SUB, :]),
        downs,
        lines[:1],
        lines[1:],
    )


def solution(mesh):
    weights = P("section", None, None)
    shares = P("section", "seq", None)
    return jax.shard_map(
        on_device,
        mesh=mesh,
        in_specs=(P("row", "seq", None), P("row", "seq", None), P("row", "seq"))
        + (weights,) * 7
        + (P("section", None),) * 2,
        out_specs=(P("section", "row", "seq", None),) * 2
        + (shares,) * 7
        + (P("section", "seq"),) * 2,
        check_vma=False,
    )
```

```python
import functools

import jax
import jax.numpy as jnp
from jax import lax
from jax.experimental import pallas as pl
from jax.experimental.pallas import tpu as pltpu
from jax.sharding import PartitionSpec as P

D = 576
HQ = 9
KVH = 3
HD = 64
GROUPS = HQ // KVH
KVW = KVH * HD
LANES = 128
QKV = 1024
FF = 1536
CHUNKS = 4
SUB = D // CHUNKS // 2
TILE = FF // 4
PACK = 16
ROW_STEP = 256
KEY_STEP = 256
SCALE = HD**-0.5
SPARE = 8 * 1024 * 1024
EPSILON = 1e-05
MASKED = -1e30
F32 = jnp.float32
BF16 = jnp.bfloat16
VMEM = pl.BlockSpec(memory_space=pltpu.VMEM)
SMEM = pl.BlockSpec(memory_space=pltpu.SMEM)
ANY = pl.BlockSpec(memory_space=pl.ANY)
SWAP = [(0, 1), (1, 0)]


def mm(a, b):
    return jnp.dot(a, b, preferred_element_type=F32)


def mm_nt(a, b):
    return lax.dot_general(a, b, (((1,), (1,)), ((), ())), preferred_element_type=F32)


def mm_tn(a, b):
    return lax.dot_general(a, b, (((0,), (0,)), ((), ())), preferred_element_type=F32)


def shape(dims, kind=BF16):
    return jax.ShapeDtypeStruct(tuple(dims), kind)


def size_of(array):
    if not jnp.issubdtype(array.dtype, jnp.number):
        return 0
    *lead, rows, columns = (1, 1, *array.shape)
    size = -(-rows // 16) * 16 * -(-columns // LANES) * LANES * array.dtype.itemsize
    for dim in lead:
        size *= dim
    return size


def call(body, ins, specs, outs, scratch, flops, stack=(), room=None):
    moved = sum(a.size * a.dtype.itemsize for a in list(ins) + list(outs))
    inner, piled = len(ins), len(stack)
    held = [a for a, spec in zip(ins, specs) if spec is VMEM] + list(outs) + list(scratch)
    if room is None:
        room = sum(size_of(a) for a in held) + SPARE
        room += sum(size_of(a) for a in stack)
    piles = [shape((piled, *stack[0].shape), stack[0].dtype)] if piled else []

    def strip(*refs):
        mid = piled + inner
        if not piled:
            return body(*refs)
        pile, sems = refs[mid], refs[-1]
        copies = [
            pltpu.make_async_copy(source, pile.at[i], sems.at[i])
            for i, source in enumerate(refs[:piled])
        ]
        for copy in copies:
            copy.start()
        body(*refs[piled:mid], *refs[mid + 1 : -1])
        for copy in copies:
            copy.wait()

    return pl.pallas_call(
        strip,
        out_shape=tuple(piles) + tuple(outs),
        in_specs=[ANY] * piled + list(specs),
        out_specs=tuple([VMEM] * (len(piles) + len(outs))),
        scratch_shapes=list(scratch) + [pltpu.SemaphoreType.DMA((piled,))] * len(piles),
        compiler_params=pltpu.CompilerParams(vmem_limit_bytes=min(room, 56 * 1024 * 1024)),
        cost_estimate=pl.CostEstimate(
            flops=int(flops), bytes_accessed=int(moved), transcendentals=0
        ),
    )(*stack, *ins)


def hold(value, *others):
    return lax.optimization_barrier((value, others))[0]


def lane_of(dims):
    return lax.broadcasted_iota(jnp.int32, dims, len(dims) - 1)


def roll(value, by):
    return pltpu.roll(value, by, value.ndim - 1)


def low_half(dims):
    return lane_of(dims) < HD


def halves(value):
    first = (lane_of(value.shape) & (HD - 1)) < HD // 2
    return jnp.where(first, roll(value, LANES - HD // 2), roll(value, HD // 2))


def tiles_of(count, step):
    step = min(count, step)
    return [(start, step) for start in range(0, count, step)]


def norm_inverse(stream):
    return lax.rsqrt(jnp.mean(stream * stream, -1, keepdims=True) + EPSILON)


def norm_back(incoming, stream, inverse, gain):
    weighted = incoming * gain
    slope = jnp.mean(weighted * stream, -1, keepdims=True)
    grad_gain = jnp.sum(incoming * (stream * inverse), 0, keepdims=True)
    return inverse * (weighted - stream * (inverse * inverse * slope)), grad_gain


def start_copy(layer, core, mine, theirs, target, sem):
    @pl.when(core == layer)
    def _():
        pltpu.make_async_copy(mine, target, sem).start()

    @pl.when(core != layer)
    def _():
        pltpu.make_async_copy(theirs, target, sem).start()


class Weights:
    def __init__(self, layer, core, mine, theirs, targets, sems):
        self.pending = {}
        for number, (name, target) in enumerate(targets.items()):
            if name in ("qkv", "gains"):
                lines = pl.ds(0, D) if name == "qkv" else pl.ds(D, PACK)
                pair = mine["qkv"].at[lines], theirs["qkv"].at[lines]
            else:
                pair = mine[name], theirs[name]
            start_copy(layer, core, *pair, target, sems.at[number])
            self.pending[name] = (pair[0], target, sems.at[number])

    def wait(self, *names):
        for name in names:
            pltpu.make_async_copy(*self.pending.pop(name)).wait()


def gain_row(lines, kind):
    parts = lines[...].astype(F32)
    parts = [parts[3 * kind + i : 3 * kind + i + 1, :D] for i in range(3)]
    return parts[0] + parts[1] + parts[2]


def project_rows(stream, gain, w_ref, cos, sin, q_ref, kv_ref, start, count):
    normed = (stream * norm_inverse(stream) * gain).astype(BF16)
    raw = mm(normed, w_ref[...])
    low = low_half((count, LANES))
    tiles = []
    for t in range(6):
        tile = raw[:, t * LANES : (t + 1) * LANES]
        tiles.append(tile * cos + halves(tile) * sin)
    rows = pl.ds(start, count)
    for head in range(HQ):
        tile = tiles[head // 2]
        tile = roll(tile, HD) if head % 2 else tile
        q_ref[head, rows, :] = jnp.where(low, tile * SCALE, 0.0).astype(BF16)
    kv_ref[rows, 0:LANES] = jnp.where(low, roll(tiles[4], HD), roll(tiles[5], HD)).astype(BF16)
    kv_ref[rows, LANES : 2 * LANES] = jnp.where(
        low, roll(tiles[5], HD), raw[:, 6 * LANES : 7 * LANES]
    ).astype(BF16)
    kv_ref[rows, 2 * LANES :] = raw[:, 7 * LANES :].astype(BF16)


def place_keys(core, own, other, kz, vz):
    for part, index in ((own, core), (other, 1 - core)):
        blocks, half, _ = part.shape
        low = low_half((blocks, half, LANES))
        tiles = [part[:, :, t * LANES : (t + 1) * LANES].astype(F32) for t in range(3)]
        turned = [roll(tile, HD) for tile in tiles]
        for target, heads in (
            (kz, (tiles[0], turned[0], tiles[1])),
            (vz, (turned[1], tiles[2], turned[2])),
        ):
            for group in range(KVH):
                value = jnp.where(low, heads[group], 1.0).astype(BF16)
                target[group, :, pl.ds(index, 1)] = value[:, None]


def key_rows(ref, group, start, count):
    _, _, _, half, _ = ref.shape
    span = 2 * half
    part = ref[group, start // span : (start + count) // span]
    return part.reshape(count, LANES)


def places(core, wagon, rows, tokens, start, dims, axis):
    half = tokens // 2
    local = lax.broadcasted_iota(jnp.int32, dims, axis) + start
    block, inside = local // half, local % half
    return (wagon * rows + block) * tokens + core * half + inside


def opening(place, docs):
    first, second = docs[0], docs[1]
    return jnp.where(place < first, 0, jnp.where(place < second, first, second))


def query_blocks(geometry):
    rows, tokens, chips = geometry
    half = tokens // 2
    if chips == 1:
        return [(b * half, half, (b + 1) * tokens) for b in range(rows)]
    return [(0, rows * half, chips * rows * tokens)]


def attend(geometry, core, wagon, docs, q_ref, kz, vz, heads_out, q_out):
    rows, tokens, _ = geometry
    for start, count, keys in query_blocks(geometry):
        place = places(core, wagon, rows, tokens, start, (count, 1), 0)
        key_place = lane_of((1, keys))
        allowed = (key_place <= place) & (key_place >= opening(place, docs))
        bias = jnp.where(allowed, 0.0, MASKED)
        low = low_half((GROUPS * count, LANES))
        lane = lane_of((GROUPS * count, LANES))
        for group in range(KVH):
            heads = slice(group * GROUPS, (group + 1) * GROUPS)
            q = q_ref[heads, start : start + count, :].reshape(GROUPS * count, LANES)
            scores = mm_nt(q, key_rows(kz, group, 0, keys))
            scores = scores.reshape(GROUPS, count, keys) + bias[None]
            scores = scores.reshape(GROUPS * count, keys)
            top = jnp.max(scores, -1, keepdims=True)
            weights = jnp.exp(scores - top).astype(BF16)
            out = mm(weights, key_rows(vz, group, 0, keys))
            total = jnp.where(low, 1.0, out)
            lse = -(top + jnp.log(total))
            high = lse.astype(BF16).astype(F32)
            rest = lse - high
            middle = rest.astype(BF16).astype(F32)
            tail = jnp.where(
                lane == HD,
                high,
                jnp.where(lane == HD + 1, middle, jnp.where(lane == HD + 2, rest - middle, 0.0)),
            )
            q_aug = jnp.where(low, q.astype(F32), tail).astype(BF16)
            q_out[heads, start : start + count, :] = q_aug.reshape(GROUPS, count, LANES)
            out = jnp.where(low, out / jnp.where(low, roll(out, HD), 1.0), 0.0)
            heads_out[heads, start : start + count, :] = out.reshape(GROUPS, count, LANES)


def attend_back(geometry, core, wagon, docs, q_ref, do_ref, kz, vz, dq, dk, dv):
    rows, tokens, _ = geometry
    span = tokens
    dk[...] = jnp.zeros_like(dk)
    dv[...] = jnp.zeros_like(dv)
    for start, count, keys in query_blocks(geometry):
        width = GROUPS * count
        lane = lane_of((1, width)) % count
        half = tokens // 2
        local = lane + start
        place = (wagon * rows + local // half) * tokens + core * half + local % half
        first = opening(place, docs)
        for key_start, key_count in tiles_of(keys, KEY_STEP):
            key_place = key_start + lax.broadcasted_iota(jnp.int32, (key_count, 1), 0)
            allowed = (key_place <= place) & (key_place >= first)
            blocks = slice(key_start // span, (key_start + key_count) // span)
            for group in range(KVH):
                heads = slice(group * GROUPS, (group + 1) * GROUPS)
                q = q_ref[heads, start : start + count, :].reshape(width, LANES)
                do = do_ref[heads, start : start + count, :].reshape(width, LANES)
                k = key_rows(kz, group, key_start, key_count)
                v = key_rows(vz, group, key_start, key_count)
                probs = jnp.where(allowed, jnp.exp(mm_nt(k, q)), 0.0)
                slopes = (probs * mm_nt(v, do)).astype(BF16)
                part = (key_count // span, 2, half, LANES)
                dv[group, blocks] += mm(probs.astype(BF16), do).reshape(part)
                dk[group, blocks] += mm(slopes, q).reshape(part)
                back = mm_tn(slopes, k).reshape(GROUPS, count, LANES)
                if key_start == 0:
                    dq[heads, start : start + count, :] = back
                else:
                    dq[heads, start : start + count, :] += back


def pack_heads(ref, rows, tile):
    count = rows.size
    low = low_half((count, LANES))
    first = ref[2 * tile, rows, :]
    if 2 * tile + 1 == HQ:
        return jnp.where(low, first, 0.0)
    return jnp.where(low, first, roll(ref[2 * tile + 1, rows, :], HD))


def piece_bits(h, row):
    x_bit, y_bit = row & 1, row >> 1
    return (x_bit, y_bit) if h == 0 else (y_bit, x_bit)


def store_piece(place, turned, core, row, h, f, g, chunk, value, kept, sent):
    f_bit, g_bit = piece_bits(h, row)
    spot = chunk ^ place if turned else chunk
    spot = (spot & 1) * 2 + spot // 2 if turned else spot
    value = value.astype(BF16)

    @pl.when(core == h)
    def _():
        kept[f ^ f_bit, g ^ g_bit, spot] = value

    @pl.when(core != h)
    def _():
        sent[f ^ f_bit, g ^ g_bit, spot] = value


def pack_kernel(geometry, where, inputs, cotangent, ids, wq, wk, wv, gain1, gain2, *refs):
    rows, tokens, _ = geometry
    half = tokens // 2
    core, member = where[0], where[3]
    outs, w_ref, (counts, sems) = refs[: 2 * rows], refs[2 * rows], refs[2 * rows + 1 :]
    mine = pl.ds(pl.multiple_of(core * half, half), half)
    copies = []
    for step in range(rows):
        target = member ^ step
        docs = ids[pl.ds(target, 1), :]
        first = jnp.sum((docs < 1).astype(F32), -1, keepdims=True)
        second = jnp.sum((docs < 2).astype(F32), -1, keepdims=True)
        lane = lane_of((PACK, half))
        value = jnp.where(lane == 0, first, jnp.where(lane == 1, second, 0.0))
        counts[step] = value.astype(BF16)
        copies += [
            (inputs.at[target, :, mine], outs[step].at[pl.ds(0, D)]),
            (counts.at[step], outs[step].at[pl.ds(D, PACK)]),
            (cotangent.at[target, :, mine], outs[rows + step]),
        ]
    copies = [pltpu.make_async_copy(a, b, sems.at[i]) for i, (a, b) in enumerate(copies)]
    for copy in copies:
        copy.start()
    one = lax.broadcasted_iota(jnp.int32, (KVW, KVW), 0) == lane_of((KVW, KVW))
    one = jnp.where(one, 1.0, 0.0).astype(BF16)
    keys, values = mm_tn(wk[...], one), mm_tn(wv[...], one)
    queries = wq[...].astype(F32)
    zeros = jnp.zeros((D, HD), F32)
    w_ref[:D] = jnp.concatenate([queries, keys, zeros, values], 1).astype(BF16)
    lines = []
    for gain in (gain1, gain2):
        rest = gain[...]
        for _ in range(3):
            part = rest.astype(BF16).astype(F32)
            lines.append(part)
            rest = rest - part
    lines = jnp.concatenate(lines + [jnp.zeros((PACK - 6, D), F32)], 0)
    lines = jnp.concatenate([lines, jnp.zeros((PACK, QKV - D), F32)], 1)
    w_ref[D:] = lines.astype(BF16)
    for copy in copies:
        copy.wait()


def unpack(block, half):
    return block[:D].T if half % LANES == 0 else block[:half]


def project_kernel(geometry, where, *refs):
    rows, tokens, _ = geometry
    half = tokens // 2
    packets, refs = refs[:rows], refs[rows:]
    mine, theirs, cos, sin, x_ref, q_ref, kv_ref, w_ref, lines, sems = refs
    core, member = where[0], where[3]
    weights = Weights(
        0, core, {"qkv": mine}, {"qkv": theirs}, {"qkv": w_ref, "gains": lines}, sems
    )
    for step in range(rows):
        x_ref[member ^ step] = unpack(packets[step][...], half)
    weights.wait("qkv", "gains")
    gain = gain_row(lines, 0)
    for start, count in tiles_of(rows * half, max(ROW_STEP, half)):
        stream = x_ref[start // half : (start + count) // half].reshape(count, D).astype(F32)
        rows_of = slice(start, start + count)
        project_rows(
            stream, gain, w_ref, cos[rows_of], sin[rows_of], q_ref, kv_ref, start, count
        )


def store_blocks(geometry, where, target, start, value):
    rows, tokens, _ = geometry
    half = tokens // 2
    for block in range(start // half, (start + value.shape[0]) // half):
        part = value[block * half - start : (block + 1) * half - start]
        part = part.T if half % LANES == 0 else part
        target[block ^ where[3]] = part


def forward_kernel(layer, geometry, where, docs, *refs):
    x_ref, q_ref, own, other, cos, sin = refs[:6]
    wg, wg2, wu, wu2, wd, wd2, wo, wo2, wq, wq2 = refs[6:16]
    refs = refs[16:]
    if layer == 1:
        earlier, refs = refs[0], refs[1:]
    q_aug, att, middle_ref, gate_ref, up_ref, y_ref = refs[:6]
    outs = refs[6:]
    if layer == 0:
        blocks_ref, q_next, kv_next = outs[:3]
        outs = outs[3:]
    else:
        pair_refs, blocks_ref = outs[: geometry[0]], outs[geometry[0]]
        outs = outs[geometry[0] + 1 :]
    kz, vz, heads, wo_v, wg_v, wu_v, wd_v, lines, sems = outs[:9]
    core, wagon = where[0], where[4]
    mine = {"gate": wg, "up": wu, "down": wd, "out": wo, "qkv": wq}
    theirs = {"gate": wg2, "up": wu2, "down": wd2, "out": wo2, "qkv": wq2}
    names = {"out": wo_v, "gains": lines, "gate": wg_v, "up": wu_v, "down": wd_v}
    weights = Weights(layer, core, mine, theirs, names, sems)
    if layer == 0:
        wq_v, lines_next, sems_next = outs[9:]
        following = Weights(1, core, mine, theirs, {"qkv": wq_v, "gains": lines_next}, sems_next)
    place_keys(core, own, other, kz, vz)
    attend(geometry, core, wagon, docs, q_ref, kz, vz, heads, q_aug)
    weights.wait("out", "gains", "gate", "up", "down")
    gain_mlp = gain_row(lines, 1)
    if layer == 0:
        following.wait("qkv", "gains")
        gain_next = gain_row(lines_next, 0)
    tokens = x_ref.shape[0]
    half = geometry[1] // 2
    for start, count in tiles_of(tokens, max(ROW_STEP, half)):
        rows = pl.ds(start, count)
        for tile in range(4):
            att[rows, tile * LANES : (tile + 1) * LANES] = pack_heads(heads, rows, tile).astype(
                BF16
            )
        att[rows, 4 * LANES :] = heads[HQ - 1, rows, :HD].astype(BF16)
        middle = x_ref[rows, :].astype(F32) + mm(att[rows, :], wo_v[...])
        normed = (middle * norm_inverse(middle) * gain_mlp).astype(BF16)
        gate, up = mm(normed, wg_v[...]), mm(normed, wu_v[...])
        middle_ref[rows, :] = middle
        gate_ref[rows, :] = gate.astype(BF16)
        up_ref[rows, :] = up.astype(BF16)
        hidden = (gate * jax.nn.sigmoid(gate) * up).astype(BF16)
        result = (middle + mm_nt(hidden, wd_v[...])).astype(BF16)
        y_ref[rows, :] = result
        store_blocks(geometry, where, blocks_ref, start, result)
        if layer == 0:
            project_rows(
                result.astype(F32),
                gain_next,
                wq_v,
                cos[rows, :],
                sin[rows, :],
                q_next,
                kv_next,
                start,
                count,
            )
    if layer == 1:
        for step, pair in enumerate(pair_refs):
            pair[pl.ds(core, 1)] = earlier[pl.ds(step, 1)]
            pair[pl.ds(1 - core, 1)] = blocks_ref[pl.ds(step, 1)]


def feed_kernel(layer, geometry, where, *refs):
    rows_in, tokens_in, chips = geometry
    half = tokens_in // 2
    core, row, place, member = where[0], where[1], where[2], where[3]
    if layer == 1:
        packets, refs = refs[:rows_in], refs[rows_in:]
    else:
        grad_ref, refs = refs[0], refs[1:]
    middle_ref, gate_ref, up_ref, wd, wd2, wq, wq2 = refs[:7]
    refs = refs[7:]
    if layer == 1:
        grad_ref, refs = refs[0], refs[1:]
    dgate, dup, kept, sent, normed, turned, hidden, downs, wd_v, lines, sems = refs
    weights = Weights(
        layer,
        core,
        {"down": wd, "qkv": wq},
        {"down": wd2, "qkv": wq2},
        {"down": wd_v, "gains": lines},
        sems,
    )
    if layer == 1:
        for step in range(rows_in):
            grad_ref[member ^ step] = unpack(packets[step][...], half)
    weights.wait("down", "gains")
    gain_mlp = gain_row(lines, 1)
    tokens = middle_ref.shape[0]
    for start, count in tiles_of(tokens, max(ROW_STEP, half)):
        rows = pl.ds(start, count)
        if layer == 1:
            branch = grad_ref[start // half : (start + count) // half].reshape(count, D)
        else:
            branch = grad_ref[rows, :]
        middle = middle_ref[rows, :]
        normed[rows, :] = (middle * norm_inverse(middle) * gain_mlp).astype(BF16)
        gate, up = gate_ref[rows, :].astype(F32), up_ref[rows, :].astype(F32)
        sig = jax.nn.sigmoid(gate)
        lifted = gate * sig
        grad_hidden = mm(branch, wd_v[...])
        hidden[rows, :] = (lifted * up).astype(BF16)
        dgate[rows, :] = (grad_hidden * up * (sig + lifted * (1.0 - sig))).astype(BF16)
        dup[rows, :] = (grad_hidden * lifted).astype(BF16)
    turned[...] = grad_ref[...].reshape(tokens, D).T
    for chunk in range(CHUNKS):
        downs[chunk] = mm(turned[...], hidden[:, chunk * TILE : (chunk + 1) * TILE])
    turned[...] = normed[...].T
    for h in range(2):
        for f in range(2):
            columns = slice((2 * h + f) * TILE, (2 * h + f + 1) * TILE)
            gates = mm(turned[...], dgate[:, columns])
            ups = mm(turned[...], dup[:, columns])
            for g in range(2):
                for chunk in range(CHUNKS):
                    lines_of = slice((2 * chunk + g) * SUB, (2 * chunk + g + 1) * SUB)
                    spots = pl.ds(((2 * h + f) * 2 + g) * SUB, SUB)
                    value = jnp.concatenate(
                        [gates[lines_of], ups[lines_of], downs[chunk, spots, :]], 0
                    )
                    store_piece(place, chips == 1, core, row, h, f, g, chunk, value, kept, sent)


def middle_kernel(layer, geometry, where, *refs):
    grad_ref, middle_ref, dgate, dup, att, wg, wg2, wu, wu2, wo, wo2, wq, wq2 = refs[:13]
    dm_ref, gain_out, do_heads, wg_v, wu_v, wo_v, lines, sems = refs[13:]
    weights = Weights(
        layer,
        where[0],
        {"gate": wg, "up": wu, "out": wo, "qkv": wq},
        {"gate": wg2, "up": wu2, "out": wo2, "qkv": wq2},
        {"gate": wg_v, "up": wu_v, "out": wo_v, "gains": lines},
        sems,
    )
    weights.wait("gate", "up", "out", "gains")
    gain_mlp = gain_row(lines, 1)
    tokens = middle_ref.shape[0]
    grad_gain = jnp.zeros((1, D), F32)
    for start, count in tiles_of(tokens, ROW_STEP):
        rows = pl.ds(start, count)
        middle = middle_ref[rows, :]
        grad_normed = mm_nt(dgate[rows, :], wg_v[...]) + mm_nt(dup[rows, :], wu_v[...])
        back, more = norm_back(grad_normed, middle, norm_inverse(middle), gain_mlp)
        grad_gain = grad_gain + more
        dm = grad_ref[rows, :].astype(F32) + back
        dm_ref[rows, :] = dm
        grad_att = mm_nt(dm.astype(BF16), wo_v[...]).astype(BF16).astype(F32)
        low = low_half((count, LANES))
        lane = lane_of((count, LANES))
        for head in range(HQ):
            if head < HQ - 1:
                tile = slice(head // 2 * LANES, (head // 2 + 1) * LANES)
                do = grad_att[:, tile]
                out = att[rows, tile].astype(F32)
            else:
                pad = jnp.zeros((count, HD), F32)
                do = jnp.concatenate([grad_att[:, 4 * LANES :], pad], 1)
                out = jnp.concatenate([att[rows, 4 * LANES :].astype(F32), pad], 1)
            if head % 2:
                do, out = roll(do, HD), roll(out, HD)
            do = jnp.where(low, do, 0.0)
            delta = -jnp.sum(do * out, -1, keepdims=True)
            high = delta.astype(BF16).astype(F32)
            do = jnp.where(lane == HD, high, jnp.where(lane == HD + 1, delta - high, do))
            do_heads[head, rows, :] = do.astype(BF16)
    gain_out[...] = grad_gain


def attend_back_kernel(geometry, where, docs, *refs):
    q_aug, do_heads, own, other, cos, sin = refs[:6]
    dq_out, kept, sent = refs[6:9]
    kz, vz, dq, dk, dv = refs[9:]
    core, wagon = where[0], where[4]
    place_keys(core, own, other, kz, vz)
    attend_back(geometry, core, wagon, docs, q_aug, do_heads, kz, vz, dq, dk, dv)
    for start, count in tiles_of(q_aug.shape[1], ROW_STEP):
        rows = pl.ds(start, count)
        for tile in range(5):
            value = pack_heads(dq, rows, tile) * SCALE
            value = value * cos[rows, :] - halves(value) * sin[rows, :]
            dq_out[rows, tile * LANES : (tile + 1) * LANES] = value.astype(BF16)
    _, blocks, _, half, _ = dk.shape
    low = low_half((blocks, half, LANES))
    for target, index in ((kept, core), (sent, 1 - core)):

        def pick(ref, group):
            return ref[group, :, pl.ds(index, 1)].reshape(blocks, half, LANES)

        def join(first, second):
            return jnp.where(low, first, roll(second, HD)).astype(target.dtype)

        target[:, :, 0:LANES] = join(pick(dk, 0), pick(dk, 1))
        target[:, :, LANES : 2 * LANES] = join(pick(dk, 2), pick(dv, 0))
        target[:, :, 2 * LANES :] = join(pick(dv, 1), pick(dv, 2))


def input_back_kernel(layer, geometry, where, *refs):
    rows_in, tokens_in, chips = geometry
    dm_ref, att, x_ref, dq, dkv, dkv2, gain_mlp, wq, wq2, cos, sin = refs[:11]
    dx_ref, blocks_refs, refs = refs[11], refs[12 : 12 + rows_in], refs[12 + rows_in :]
    kept, sent, blocks_ref, dqkv, normed, da, wq_v, lines, sems = refs
    core, row, place = where[0], where[1], where[2]
    weights = Weights(
        layer, core, {"qkv": wq}, {"qkv": wq2}, {"qkv": wq_v, "gains": lines}, sems
    )
    weights.wait("qkv", "gains")
    gain = gain_row(lines, 0)
    tokens = x_ref.shape[0]
    half = tokens_in // 2
    grad_gain = jnp.zeros((1, D), F32)
    for start, count in tiles_of(tokens, max(ROW_STEP, half)):
        rows = pl.ds(start, count)
        low = low_half((count, LANES))
        grads = [
            dkv[rows, t * LANES : (t + 1) * LANES]
            + dkv2[rows, t * LANES : (t + 1) * LANES].astype(F32)
            for t in range(3)
        ]
        for tile in range(4):
            lanes = slice(tile * LANES, (tile + 1) * LANES)
            dqkv[rows, lanes] = dq[rows, lanes]
        turned = roll(grads[0], HD)

        def unrotate(value):
            return value * cos[rows, :] - halves(value) * sin[rows, :]

        last = dq[rows, 4 * LANES :].astype(F32)
        dqkv[rows, 4 * LANES : 5 * LANES] = jnp.where(low, last, unrotate(turned)).astype(BF16)
        keys = unrotate(jnp.where(low, turned, roll(grads[1], HD)))
        dqkv[rows, 5 * LANES : 6 * LANES] = keys.astype(BF16)
        dqkv[rows, 6 * LANES : 7 * LANES] = jnp.where(low, 0.0, grads[1]).astype(BF16)
        dqkv[rows, 7 * LANES :] = grads[2].astype(BF16)
        stream = x_ref[rows, :].astype(F32)
        inverse = norm_inverse(stream)
        normed[rows, :] = (stream * inverse * gain).astype(BF16)
        grad_normed = mm_nt(dqkv[rows, :], wq_v[...])
        back, more = norm_back(grad_normed, stream, inverse, gain)
        grad_gain = grad_gain + more
        dm = dm_ref[rows, :]
        dx = (dm + back).astype(BF16)
        dx_ref[rows, :] = dx
        store_blocks(geometry, where, blocks_ref, start, dx)
        da[rows, 0:D] = dm.astype(BF16)
        da[rows, D:] = jnp.zeros((count, 2 * TILE - D), BF16)
    for step, block in enumerate(blocks_refs):
        block[...] = blocks_ref[step]
    pad = jnp.zeros((1, 2 * TILE - D), F32)
    lines = []
    for vector in (grad_gain, gain_mlp[...]):
        wide = jnp.concatenate([vector, pad], 1)
        lines += [wide[:, :TILE], wide[:, TILE:]]
    lines = jnp.concatenate(lines + [jnp.zeros((4, TILE), F32)], 0)
    for h in range(2):
        for f in range(2):
            if h == 0:
                value = mm_tn(normed[...], dqkv[:, f * TILE : (f + 1) * TILE])
            else:
                value = mm_tn(att[...], da[:, f * TILE : (f + 1) * TILE])
            if h == 1 and f == 1:
                more = mm_tn(normed[...], dqkv[:, 6 * LANES :])
                value = jnp.concatenate(
                    [
                        value[:, :LANES],
                        value[:, LANES : 2 * LANES] + more[:, :LANES],
                        more[:, LANES:],
                    ],
                    1,
                )
            for g in range(2):
                for chunk in range(CHUNKS):
                    part = value[(2 * chunk + g) * SUB : (2 * chunk + g + 1) * SUB]
                    part = jnp.concatenate([part, lines], 0)
                    store_piece(place, chips == 1, core, row, h, f, g, chunk, part, kept, sent)


def owners_kernel(geometry, where, *refs):
    rows, tokens, _ = geometry
    half = tokens // 2
    core, member = where[0], where[3]
    sets = [refs[i : i + rows + 1] for i in range(0, len(refs) - 2, rows + 1)]
    out, sems = refs[-2:]

    def move(blocks):
        copies = []
        for step in range(rows):
            target = member ^ step
            for side, index in ((0, core), (1, 1 - core)):
                lanes = pl.ds(pl.multiple_of(index * half, half), half)
                source = blocks[rows].at[step] if side else blocks[step]
                if len(sets) == 1:
                    source = source.at[side]
                sem = sems.at[2 * step + side]
                copies.append(pltpu.make_async_copy(source, out.at[target, :, lanes], sem))
        for copy in copies:
            copy.start()
        for copy in copies:
            copy.wait()

    if len(sets) == 1:
        move(sets[0])
    else:
        for number in range(2):

            @pl.when(core == number)
            def _():
                move(sets[number])


def gather_kernel(where, *refs):
    mlp0, mlp1, attn = refs[:2], refs[2:4], refs[4:6]
    wq, wk, wv, wo, wg, wu, wd, g1, g2 = refs[6:15]
    wide, share = refs[15:]
    core, row, place = where[0], where[1], where[2]
    for step in range(4):
        peer = row ^ step
        x_bit, y_bit = peer & 1, peer >> 1
        for kind in range(2):
            h = core if kind == 0 else 1 - core
            f = jnp.where(h == 0, x_bit, y_bit)
            g = jnp.where(h == 0, y_bit, x_bit)

            @pl.when(core == 0)
            def _():
                share[...] = mlp0[kind][step]

            @pl.when(core == 1)
            def _():
                share[...] = mlp1[1 - kind][step]

            part = share[...].astype(F32)
            rows = pl.ds(pl.multiple_of(g * SUB, 8), SUB)
            tile = 2 * h + f
            columns = pl.ds(pl.multiple_of(tile * TILE, LANES), TILE)
            wg[0, rows, columns] = part[:SUB]
            wu[0, rows, columns] = part[SUB : 2 * SUB]
            wd[0, pl.ds(pl.multiple_of((2 * tile + g) * SUB, 8), SUB), :] = part[2 * SUB :]
            part = attn[kind][step, core].astype(F32)
            wide[rows, columns] = part[:SUB]
    wq[0] = wide[:, :D]
    wk[0] = wide[:, D : D + KVW]
    wo[0] = wide[:, 2 * TILE : 2 * TILE + D]
    wv[0] = wide[:, 2 * TILE + D :]
    lines = attn[0][0, core].astype(F32)[SUB:]
    for kind, out in ((0, g1), (1, g2)):
        whole = jnp.concatenate(
            [lines[2 * kind : 2 * kind + 1], lines[2 * kind + 1 : 2 * kind + 2]], 1
        )
        for chunk in range(CHUNKS):

            @pl.when(place == chunk)
            def _():
                out[...] = whole[:, chunk * 2 * SUB : (chunk + 1) * 2 * SUB]


def rotary(place):
    frequency = 10000.0 ** (-jnp.arange(HD // 2, dtype=F32) * 2.0 / HD)
    angles = place.astype(F32)[:, None] * frequency[None, :]
    cosine, sine = jnp.cos(angles), jnp.sin(angles)
    return jnp.concatenate([cosine] * 4, 1), jnp.concatenate([-sine, sine] * 2, 1)


def on_device(
    inputs,
    cotangent,
    group_ids,
    w_query,
    w_key,
    w_value,
    w_out,
    w_gate,
    w_up,
    w_down,
    gain_attn,
    gain_mlp,
):
    core = lax.axis_index("section")
    row = lax.axis_index("row")
    place = lax.axis_index("seq")
    spans = lax.axis_size("seq")
    rows, tokens, _ = inputs.shape
    half = tokens // 2
    chips = spans // rows
    member, wagon = place % rows, place // rows
    own = rows * half
    blocks = chips * rows
    length = blocks * tokens
    geometry = (rows, tokens, chips)
    flipped = half % LANES == 0
    where = jnp.stack([core, row, place, member, wagon]).astype(jnp.int32)
    clans = [[b + rows * j for j in range(chips)] for b in range(rows)]

    def turn(step):
        return [(s, s ^ step) for s in range(spans)]

    def sems(count):
        return pltpu.SemaphoreType.DMA((count,))

    def vmem(*dims, kind=BF16):
        return pltpu.VMEM(dims, kind)

    def flip(array):
        return jnp.swapaxes(array, -1, -2)

    pack_ins = [
        where,
        flip(inputs),
        flip(cotangent),
        group_ids,
        w_query[0],
        flip(w_key[0]),
        flip(w_value[0]),
        gain_attn,
        gain_mlp,
    ]
    if flipped:
        packed = call(
            functools.partial(pack_kernel, geometry),
            pack_ins,
            [SMEM] + [ANY] * 2 + [VMEM] * 6,
            [shape((D + PACK, half))] * rows + [shape((D, half))] * rows + [shape((D + PACK, QKV))],
            [vmem(rows, PACK, half), sems(3 * rows)],
            0,
            room=56 * 1024 * 1024,
        )
        packets, shares, w_qkv = packed[:rows], packed[rows : 2 * rows], packed[-1]
    else:
        packets, shares = [], []
        below = [jnp.sum((group_ids < i).astype(F32), 1) for i in (1, 2)]
        counts = jnp.pad(jnp.stack(below, 1), ((0, 0), (0, D - 2))).astype(BF16)
        counts = jnp.pad(counts[:, None], ((0, 0), (0, PACK - 1), (0, 0)))
        for step in range(rows):
            target = member ^ step
            for array, outs in ((inputs, packets), (cotangent, shares)):
                part = lax.dynamic_index_in_dim(array, target, 0, False)
                part = lax.dynamic_slice_in_dim(part, core * half, half, 0)
                outs.append(part)
            line = lax.dynamic_index_in_dim(counts, target, 0, False)
            packets[-1] = jnp.concatenate([packets[-1], line], 0)
        w_qkv = jnp.concatenate(
            [w_query[0], w_key[0], jnp.zeros((D, HD), BF16), w_value[0]], 1
        )
        parts, rest = [], jnp.concatenate([gain_attn, gain_mlp], 0)
        for _ in range(3):
            parts.append(rest.astype(BF16))
            rest = rest - parts[-1].astype(F32)
        lines = jnp.stack(parts, 1).reshape(6, D)
        w_qkv = jnp.concatenate([w_qkv, jnp.pad(lines, ((0, PACK - 6), (0, QKV - D)))], 0)
    packets = [packets[0]] + [
        lax.ppermute(packets[step], "seq", turn(step)) for step in range(1, rows)
    ]
    w_qkv = [w_qkv, lax.ppermute(w_qkv, "section", SWAP)]
    mine = {"gate": w_gate[0], "up": w_up[0], "down": flip(w_down[0]), "out": w_out[0]}
    gates = dict(zip(mine, [w_qkv[1], *packets[1:4]]))
    pairs = {
        name: (value, lax.ppermute(hold(value, gates[name]), "section", SWAP))
        for name, value in mine.items()
    }
    pairs["qkv"] = w_qkv

    def weights_of(*names):
        return [side for name in names for side in pairs[name]]

    if flipped:
        docs = sum(packet[D, :2].astype(F32) for packet in packets)
    else:
        docs = sum(packet[half, :2].astype(F32) for packet in packets)
    if chips > 1:
        docs = lax.psum(docs, "seq", axis_index_groups=clans)
    docs = docs.astype(jnp.int32)
    local = jnp.arange(own, dtype=jnp.int32)
    tables = rotary((wagon * rows + local // half) * tokens + core * half + local % half)

    x_in, query, kv = call(
        functools.partial(project_kernel, geometry),
        [where, *packets, *w_qkv, *tables],
        [SMEM] + [VMEM] * rows + [ANY] * 2 + [VMEM] * 2,
        [shape((rows, half, D)), shape((HQ, own, LANES)), shape((own, 2 * KVW))],
        [vmem(D, QKV), vmem(PACK, QKV), sems(2)],
        2 * own * D * QKV,
    )
    x_in = x_in.reshape(own, D)

    def exchange(kv):
        kv = kv.reshape(rows, half, 2 * KVW)
        if chips > 1:
            kv = lax.all_gather(kv, "seq", axis=0, tiled=True, axis_index_groups=clans)
        return kv, lax.ppermute(kv, "section", SWAP)

    key_scratch = [vmem(KVH, blocks, 2, half, LANES)] * 2
    head_scratch = [vmem(HQ, own, LANES, kind=F32)]
    weight = {"gate": vmem(D, FF), "up": vmem(D, FF), "down": vmem(D, FF), "out": vmem(D, D)}
    lines_scratch = vmem(PACK, QKV)
    attn_flops = 4 * HQ * own * length * LANES
    feed_flops = 2 * own * D * (D + 3 * FF)
    flat = shape((own, D))
    wide = shape((own, FF))
    heads = shape((HQ, own, LANES))
    sent_blocks = shape((rows, D, half) if flipped else (rows, half, D))

    def forward(layer, x, query, kv, *earlier):
        outs = [heads, flat, shape((own, D), F32), wide, wide, flat, sent_blocks]
        scratch = key_scratch + head_scratch
        scratch += [weight["out"], weight["gate"], weight["up"], weight["down"]]
        scratch += [lines_scratch, sems(5)]
        if layer == 0:
            outs += [heads, shape((own, 2 * KVW))]
            scratch += [vmem(D, QKV), lines_scratch, sems(2)]
        else:
            scratch = [vmem(*sent_blocks.shape)] + scratch
            outs = outs[:-1] + [shape((2,) + sent_blocks.shape[1:])] * rows
        return call(
            functools.partial(forward_kernel, layer, geometry),
            [where, docs, x, query, *kv, *tables]
            + weights_of("gate", "up", "down", "out", "qkv")
            + list(earlier),
            [SMEM] * 2 + [VMEM] * 6 + [ANY] * 10 + [VMEM] * len(earlier),
            outs,
            scratch,
            attn_flops + feed_flops,
        )

    kv0 = exchange(kv)
    q0, att0, middle0, gate0, up0, y0, blocks0, query, kv = forward(0, x_in, query, kv0)
    shares = [shares[0]] + [
        lax.ppermute(shares[step], "seq", turn(step)) for step in range(1, rows)
    ]
    kv1 = exchange(kv)
    outs = forward(1, y0, query, kv1, blocks0)
    q1, att1, middle1, gate1, up1, y1, *pair_blocks = hold(outs, shares)
    mlp_pieces = shape((2, 2, CHUNKS, 3 * SUB, TILE))
    attn_pieces = shape((2, 2, CHUNKS, SUB + 8, TILE))

    def feed(layer, where, grads, middle, gate, up, **order):
        outs = [shape((rows, half, D))] if layer == 1 else []
        return call(
            functools.partial(feed_kernel, layer, geometry),
            [where, *grads, middle, gate, up] + weights_of("down", "qkv"),
            [SMEM] + [VMEM] * (len(grads) + 3) + [ANY] * 4,
            outs + [wide, wide, mlp_pieces, mlp_pieces],
            [vmem(own, D), vmem(D, own), vmem(own, FF), vmem(CHUNKS, D, TILE, kind=F32)]
            + [weight["down"], lines_scratch, sems(2)],
            8 * own * D * FF,
            **order,
        )

    def spread(layer, where, grad, middle, dgate, dup, att, **order):
        return call(
            functools.partial(middle_kernel, layer, geometry),
            [where, grad, middle, dgate, dup, att] + weights_of("gate", "up", "out", "qkv"),
            [SMEM] + [VMEM] * 5 + [ANY] * 8,
            [shape((own, D), F32), shape((1, D), F32), heads],
            [weight["gate"], weight["up"], weight["out"], lines_scratch, sems(4)],
            2 * own * D * (D + 2 * FF),
            **order,
        )

    def attention_back(where, q_aug, do_heads, kv, **order):
        return call(
            functools.partial(attend_back_kernel, geometry),
            [where, docs, q_aug, do_heads, *kv, *tables],
            [SMEM] * 2 + [VMEM] * 6,
            [
                shape((own, 5 * LANES)),
                shape((blocks, half, 2 * KVW), F32),
                shape((blocks, half, 2 * KVW)),
            ],
            key_scratch
            + head_scratch
            + [vmem(KVH, blocks, 2, half, LANES, kind=F32)] * 2,
            3 * attn_flops,
            **order,
        )

    def trade_keys(dq, dkv, dkv_sent):
        dkv_got = lax.ppermute(dkv_sent, "section", SWAP)
        if chips > 1:
            dkv = lax.psum_scatter(
                (dkv + dkv_got).astype(BF16),
                "seq",
                scatter_dimension=0,
                tiled=True,
                axis_index_groups=clans,
            ).astype(F32)
            dkv_got = jnp.zeros(dkv.shape, BF16)
        return dq, dkv.reshape(own, 2 * KVW), dkv_got.reshape(own, 2 * KVW)

    def input_back(layer, where, dm, att, x, dq, dkv, dkv_got, gain_grad, **order):
        return call(
            functools.partial(input_back_kernel, layer, geometry),
            [where, dm, att, x, dq, dkv, dkv_got, gain_grad, *w_qkv, *tables],
            [SMEM] + [VMEM] * 7 + [ANY] * 2 + [VMEM] * 2,
            [flat]
            + [shape(sent_blocks.shape[1:])] * rows
            + [attn_pieces, attn_pieces],
            [vmem(*sent_blocks.shape), vmem(own, QKV), vmem(own, D), vmem(own, 2 * TILE), vmem(D, QKV)]
            + [lines_scratch, sems(2)],
            4 * own * D * QKV + 2 * own * D * D,
            **order,
        )

    def line(section, r):
        return section * 4 + r

    first_pairs = [(line(0, r), line(0, r ^ 1)) for r in range(4)]
    first_pairs += [(line(1, r), line(1, r ^ 2)) for r in range(4)]
    second_pairs = [(line(0, r), line(0, r ^ 2)) for r in range(4)]
    second_pairs += [(line(1, r), line(1, r ^ 1)) for r in range(4)]

    def to_core(sent):
        return lax.ppermute(sent, "section", SWAP)

    def sum_cores(kept, got):
        return (kept[1].astype(F32) + got[1]).astype(BF16)

    def to_first(out):
        return lax.ppermute(out, ("section", "row"), first_pairs)

    def sum_first(kept, got, near):
        return (kept[0, 1].astype(F32) + got[0, 1] + near[1]).astype(BF16)

    def to_second(out):
        return lax.ppermute(out, ("section", "row"), second_pairs)

    def sum_second(kept, got, near, far):
        return (kept[0, 0].astype(F32) + got[0, 0] + near[0] + far).astype(BF16)

    def to_seq(total):
        if chips > 1:
            return [lax.psum(total, "seq")]
        return [total[0]] + [
            lax.ppermute(total[spot], "seq", turn(step)) for spot, step in ((2, 1), (1, 2), (3, 3))
        ]

    def halve(total, step):
        count = total.shape[0] // 2
        got = lax.ppermute(total[count:], "seq", turn(step))
        return got, (total[:count].astype(F32) + got).astype(BF16)

    def sum_seq(first, others):
        return sum((part.astype(F32) for part in others), first.astype(F32)).astype(BF16)

    def to_rows(blocks):
        return list(blocks[:1]) + [
            lax.ppermute(blocks[step], "seq", turn(step)) for step in range(1, rows)
        ]

    def to_owners(sets):
        if flipped:
            return call(
                functools.partial(owners_kernel, geometry),
                [where, *sum(sets, [])],
                [SMEM] + [ANY] * ((rows + 1) * len(sets)),
                [shape((rows, D, tokens))],
                [sems(2 * rows)],
                0,
            )[0]
        out = jnp.zeros((rows, 2, half, D), BF16)
        for step in range(rows):
            if len(sets) == 1:
                pair = [sets[0][step][0], sets[0][rows][step][1]]
            else:
                pair = [
                    jnp.where(core == 0, sets[0][step], sets[1][step]),
                    jnp.where(core == 0, sets[0][rows][step], sets[1][rows][step]),
                ]
            pair = jnp.where(core == 0, jnp.stack(pair), jnp.stack(pair[::-1]))
            out = lax.dynamic_update_index_in_dim(out, pair, member ^ step, 0)
        return flip(out.reshape(rows, tokens, D))

    def to_all(piece):
        return [piece] + [
            lax.ppermute(piece, "row", [(r, r ^ step) for r in range(4)]) for step in range(1, 4)
        ]

    ys = to_rows(pair_blocks)
    grad1, dgate, dup, kept_m1, sent = hold(feed(1, where, shares, middle1, gate1, up1), ys[2])
    grad1 = grad1.reshape(own, D)
    got_m1 = to_core(sent)

    dm, gain_grad, do_heads = hold(
        spread(1, where, grad1, middle1, dgate, dup, att1), ys[1], got_m1
    )

    out = sum_cores(hold(kept_m1, dm), got_m1)
    near_m1 = to_first(out)
    kept_m1, *outs = hold(
        (kept_m1, *attention_back(where, q1, do_heads, kv1)), ys[3], near_m1
    )
    dq, dkv, dkv_got = trade_keys(*outs)

    out = sum_first(kept_m1, got_m1, near_m1)
    far_m1 = to_second(out)
    outs = input_back(
        1, hold(where, out), dm, att1, y0, dq, dkv, dkv_got, gain_grad, stack=ys
    )
    kept_m1, pile, dx1, *blocks1, kept_a1, sent = hold((kept_m1, *outs), far_m1)
    got_a1 = to_core(sent)
    ys.append(to_core(pile))

    total = sum_second(kept_m1, got_m1, near_m1, far_m1)
    parts_m1 = to_seq(total)
    outs = feed(0, hold(where, total), [dx1], middle0, gate0, up0)
    dgate, dup, kept_m0, sent = hold(outs, ys[rows], got_a1, parts_m1)
    got_m0 = to_core(sent)

    mlp1 = to_all(sum_seq(hold(parts_m1[0], dgate), parts_m1[1:]))
    out = sum_cores(hold(kept_a1, dgate), got_a1)
    near_a1 = to_first(out)
    activations = to_owners([ys])
    outs = spread(0, hold(where, out, mlp1[0]), dx1, middle0, dgate, dup, att0)
    dm, gain_grad, do_heads = hold(outs, activations, mlp1, near_a1, got_m0)

    out_a1 = sum_first(hold(kept_a1, dm), got_a1, near_a1)
    far_a1 = to_second(out_a1)
    out_m0 = sum_cores(hold(kept_m0, dm), got_m0)
    near_m0 = to_first(out_m0)
    dxs1 = to_rows(hold(blocks1, dm))
    pile, *outs = attention_back(hold(where, out_a1, out_m0), q0, do_heads, kv0, stack=mlp1)
    kept_a1, kept_m0, pile, *outs = hold(
        (kept_a1, kept_m0, pile, *outs), far_a1, near_m0, dxs1
    )
    mlp1 = lax.ppermute(pile, "section", [(0, 1)]), pile
    dq, dkv, dkv_got = trade_keys(*outs)

    total_a1 = sum_second(kept_a1, got_a1, near_a1, far_a1)
    parts_a1 = to_seq(total_a1)
    out = sum_first(kept_m0, got_m0, near_m0)
    far_m0 = to_second(out)
    outs = input_back(
        0, hold(where, out, total_a1), dm, att0, x_in, dq, dkv, dkv_got, gain_grad, stack=dxs1
    )
    kept_m0, pile, dx0, *blocks0, kept_a0, sent = hold(
        (kept_m0, *outs), far_m0, parts_a1, mlp1[0]
    )

    got_a0 = to_core(sent)
    total = sum_second(kept_m0, got_m0, near_m0, far_m0)
    out = sum_cores(hold(kept_a0, total), got_a0)
    near_a0 = to_first(out)
    if chips == 1:
        got, total = halve(total, 1)
        kept_a0 = hold(kept_a0, got, near_a0)
        got, total = halve(total, 2)
        piece = total[0]
    else:
        piece = lax.psum(total, "seq")
    out = sum_first(kept_a0, got_a0, near_a0)
    far_a0 = to_second(out)
    mlp0 = to_all(piece)
    total = sum_second(hold(kept_a0, piece), got_a0, near_a0, far_a0)
    parts_a0 = to_seq(total)
    blocks0, pile = hold((blocks0, pile), total)
    dxs1.append(lax.ppermute(pile, "section", [(0, 1)]))
    dxs0 = to_rows(blocks0)
    attn = jnp.stack([sum_seq(p[0], p[1:]) for p in (parts_a0, parts_a1)])
    mlp0 = hold(mlp0, attn)
    attn = to_all(attn)
    mlp0 = jnp.stack(mlp0)
    mlp0 = mlp0, lax.ppermute(mlp0, "section", [(1, 0)])
    dxs0 = hold(dxs0, attn)
    attn = jnp.stack(attn)
    attn = attn, to_core(attn)
    dxs0.append(lax.ppermute(hold(jnp.stack(dxs0), attn[0]), "section", [(1, 0)]))
    input_grads = to_owners([dxs0, dxs1])
    input_grads = flip(input_grads)[None]
    activations = flip(activations)[None]
    share = D // spans
    if chips == 1:
        grads = call(
            gather_kernel,
            [where, *mlp0, *mlp1, *attn],
            [SMEM] + [VMEM] * 6,
            [shape((1, share, width), F32) for width in (D, KVW, KVW, D, FF, FF)]
            + [shape((1, D, TILE), F32)]
            + [shape((1, share), F32)] * 2,
            [vmem(2 * SUB, FF, kind=F32), vmem(3 * SUB, TILE)],
            0,
        )
        grads = list(grads)
        grads[6] = flip(grads[6])
        return (activations, input_grads) + tuple(grads)

    def ordered(parts):
        parts = parts.reshape(2, 4, *parts.shape[1:]).swapaxes(0, 1).astype(F32)
        parts = jnp.take(parts, jnp.arange(4) ^ row, axis=0)
        parts = jnp.take(parts, jnp.arange(2) ^ core, axis=1)
        parts = parts.reshape((2, 2) + parts.shape[1:])
        return jnp.stack([parts[:, :, 0].swapaxes(0, 1), parts[:, :, 1]])

    def rows_of(part):
        full = part.transpose(3, 2, 4, 0, 1, 5).reshape(D, FF)
        return lax.dynamic_slice_in_dim(full, place * share, share, 0)[None]

    mlp1 = jnp.concatenate([mlp1[1], mlp1[0]], 0)
    mlp = ordered(jnp.where(core == 0, jnp.concatenate(mlp0, 0), mlp1))
    attn = ordered(lax.dynamic_index_in_dim(jnp.concatenate(attn, 0), core, 1, False))
    downs = mlp[..., 2 * SUB :, :].transpose(0, 1, 2, 4, 3, 5).reshape(D, FF)
    downs = lax.dynamic_slice_in_dim(downs, place * (FF // spans), FF // spans, 1).T[None]
    full = rows_of(attn[..., :SUB, :])
    lines = attn[0, 0, 0, 0, SUB : SUB + 4].reshape(2, 2 * TILE)[:, :D]
    lines = lax.dynamic_slice_in_dim(lines, place * share, share, 1)
    return (
        activations,
        input_grads,
        full[..., :D],
        full[..., D : D + KVW],
        full[..., 2 * TILE + D :],
        full[..., 2 * TILE : 2 * TILE + D],
        rows_of(mlp[..., :SUB, :]),
        rows_of(mlp[..., SUB : 2 * SUB, :]),
        downs,
        lines[:1],
        lines[1:],
    )


def solution(mesh):
    weights = P("section", None, None)
    shares = P("section", "seq", None)
    return jax.shard_map(
        on_device,
        mesh=mesh,
        in_specs=(P("row", "seq", None), P("row", "seq", None), P("row", "seq"))
        + (weights,) * 7
        + (P("section", None),) * 2,
        out_specs=(P("section", "row", "seq", None),) * 2
        + (shares,) * 7
        + (P("section", "seq"),) * 2,
        check_vma=False,
    )
```

```python
import functools

import jax
import jax.numpy as jnp
from jax import lax
from jax.experimental import pallas as pl
from jax.experimental.pallas import tpu as pltpu
from jax.sharding import PartitionSpec as P

D = 576
HQ = 9
KVH = 3
HD = 64
GROUPS = HQ // KVH
KVW = KVH * HD
LANES = 128
QKV = 1024
FF = 1536
CHUNKS = 4
SUB = D // CHUNKS // 2
TILE = FF // 4
PACK = 16
ROW_STEP = 256
KEY_STEP = 256
SCALE = HD**-0.5
SPARE = 4 * 1024 * 1024
EPSILON = 1e-05
MASKED = -1e30
F32 = jnp.float32
BF16 = jnp.bfloat16
VMEM = pl.BlockSpec(memory_space=pltpu.VMEM)
SMEM = pl.BlockSpec(memory_space=pltpu.SMEM)
ANY = pl.BlockSpec(memory_space=pl.ANY)
SWAP = [(0, 1), (1, 0)]


def mm(a, b):
    return jnp.dot(a, b, preferred_element_type=F32)


def mm_nt(a, b):
    return lax.dot_general(a, b, (((1,), (1,)), ((), ())), preferred_element_type=F32)


def mm_tn(a, b):
    return lax.dot_general(a, b, (((0,), (0,)), ((), ())), preferred_element_type=F32)


def shape(dims, kind=BF16):
    return jax.ShapeDtypeStruct(tuple(dims), kind)


def size_of(array):
    if not jnp.issubdtype(array.dtype, jnp.number):
        return 0
    *lead, rows, columns = (1, 1, *array.shape)
    size = -(-rows // 16) * 16 * -(-columns // LANES) * LANES * array.dtype.itemsize
    for dim in lead:
        size *= dim
    return size


def call(body, ins, specs, outs, scratch, flops, stack=(), room=None, light=False, far=()):
    moved = sum(a.size * a.dtype.itemsize for a in list(ins) + list(outs))
    inner, piled = len(ins), len(stack)
    held = [a for a, spec in zip(ins, specs) if spec is VMEM] + list(outs) + list(scratch)
    if room is None:
        room = sum(size_of(a) for a in held) + SPARE
        room += sum(size_of(a) for a in stack)
    piles = [shape((piled, *stack[0].shape), stack[0].dtype)] if piled else []

    def strip(*refs):
        mid = piled + inner
        if not piled:
            return body(*refs)
        pile, sems = refs[mid], refs[-1]
        copies = [
            pltpu.make_async_copy(source, pile.at[i], sems.at[i])
            for i, source in enumerate(refs[:piled])
        ]
        for copy in copies:
            copy.start()
        body(*refs[piled:mid], *refs[mid + 1 : -1])
        for copy in copies:
            copy.wait()

    return pl.pallas_call(
        strip,
        out_shape=tuple(piles) + tuple(
            pltpu.HBM(a.shape, a.dtype) if i in far else a for i, a in enumerate(outs)
        ),
        in_specs=[ANY] * piled + list(specs),
        out_specs=tuple([VMEM] * len(piles) + [ANY if i in far else VMEM for i in range(len(outs))]),
        scratch_shapes=list(scratch) + [pltpu.SemaphoreType.DMA((piled,))] * len(piles),
        compiler_params=pltpu.CompilerParams(vmem_limit_bytes=min(room, 56 * 1024 * 1024)),
        cost_estimate=pl.CostEstimate(
            flops=0 if light else int(flops),
            bytes_accessed=0 if light else int(moved),
            transcendentals=0,
        ),
    )(*stack, *ins)


def hold(value, *others):
    return lax.optimization_barrier((value, others))[0]


def lane_of(dims):
    return lax.broadcasted_iota(jnp.int32, dims, len(dims) - 1)


def roll(value, by):
    return pltpu.roll(value, by, value.ndim - 1)


def low_half(dims):
    return lane_of(dims) < HD


def halves(value):
    first = (lane_of(value.shape) & (HD - 1)) < HD // 2
    return jnp.where(first, roll(value, LANES - HD // 2), roll(value, HD // 2))


def tiles_of(count, step):
    step = min(count, step)
    return [(start, step) for start in range(0, count, step)]


def norm_inverse(stream):
    return lax.rsqrt(jnp.mean(stream * stream, -1, keepdims=True) + EPSILON)


def norm_back(incoming, stream, inverse, gain):
    weighted = incoming * gain
    slope = jnp.mean(weighted * stream, -1, keepdims=True)
    grad_gain = jnp.sum(incoming * (stream * inverse), 0, keepdims=True)
    return inverse * (weighted - stream * (inverse * inverse * slope)), grad_gain


def start_copy(layer, core, mine, theirs, target, sem):
    @pl.when(core == layer)
    def _():
        pltpu.make_async_copy(mine, target, sem).start()

    @pl.when(core != layer)
    def _():
        pltpu.make_async_copy(theirs, target, sem).start()


class Weights:
    def __init__(self, layer, core, mine, theirs, targets, sems):
        self.pending = {}
        for number, (name, target) in enumerate(targets.items()):
            if name in ("qkv", "gains"):
                lines = pl.ds(0, D) if name == "qkv" else pl.ds(D, PACK)
                pair = mine["qkv"].at[lines], theirs["qkv"].at[lines]
            else:
                pair = mine[name], theirs[name]
            start_copy(layer, core, *pair, target, sems.at[number])
            self.pending[name] = (pair[0], target, sems.at[number])

    def wait(self, *names):
        for name in names:
            pltpu.make_async_copy(*self.pending.pop(name)).wait()


def gain_row(lines, kind):
    parts = lines[...].astype(F32)
    parts = [parts[3 * kind + i : 3 * kind + i + 1, :D] for i in range(3)]
    return parts[0] + parts[1] + parts[2]


def project_rows(stream, gain, w_ref, cos, sin, q_ref, kv_ref, start, count):
    normed = (stream * norm_inverse(stream) * gain).astype(BF16)
    raw = mm(normed, w_ref[...])
    low = low_half((count, LANES))
    tiles = []
    for t in range(6):
        tile = raw[:, t * LANES : (t + 1) * LANES]
        tiles.append(tile * cos + halves(tile) * sin)
    rows = pl.ds(start, count)
    for head in range(HQ):
        tile = tiles[head // 2]
        tile = roll(tile, HD) if head % 2 else tile
        q_ref[head, rows, :] = jnp.where(low, tile * SCALE, 0.0).astype(BF16)
    kv_ref[rows, 0:LANES] = jnp.where(low, roll(tiles[4], HD), roll(tiles[5], HD)).astype(BF16)
    kv_ref[rows, LANES : 2 * LANES] = jnp.where(
        low, roll(tiles[5], HD), raw[:, 6 * LANES : 7 * LANES]
    ).astype(BF16)
    kv_ref[rows, 2 * LANES :] = raw[:, 7 * LANES :].astype(BF16)


def place_keys(core, own, other, kz, vz):
    for part, index in ((own, core), (other, 1 - core)):
        blocks, half, _ = part.shape
        low = low_half((blocks, half, LANES))
        tiles = [part[:, :, t * LANES : (t + 1) * LANES].astype(F32) for t in range(3)]
        turned = [roll(tile, HD) for tile in tiles]
        for target, heads in (
            (kz, (tiles[0], turned[0], tiles[1])),
            (vz, (turned[1], tiles[2], turned[2])),
        ):
            for group in range(KVH):
                value = jnp.where(low, heads[group], 1.0).astype(BF16)
                target[group, :, pl.ds(index, 1)] = value[:, None]


def key_rows(ref, group, start, count):
    _, _, _, half, _ = ref.shape
    span = 2 * half
    part = ref[group, start // span : (start + count) // span]
    return part.reshape(count, LANES)


def places(core, wagon, rows, tokens, start, dims, axis):
    half = tokens // 2
    local = lax.broadcasted_iota(jnp.int32, dims, axis) + start
    block, inside = local // half, local % half
    return (wagon * rows + block) * tokens + core * half + inside


def opening(place, docs):
    first, second = docs[0], docs[1]
    return jnp.where(place < first, 0, jnp.where(place < second, first, second))


def query_blocks(geometry):
    rows, tokens, chips = geometry
    half = tokens // 2
    if chips == 1:
        return [(b * half, half, (b + 1) * tokens) for b in range(rows)]
    return [(0, rows * half, chips * rows * tokens)]


def ahead(tasks, first, second):
    ready = first(*tasks[0])
    for number, task in enumerate(tasks):
        following = first(*tasks[number + 1]) if number + 1 < len(tasks) else None
        second(*task, ready)
        ready = following


def attend(geometry, core, wagon, docs, q_ref, kz, vz, heads_out, q_out):
    rows, tokens, _ = geometry
    biases = {}

    def rows_of(ref, start, count, group):
        heads = slice(group * GROUPS, (group + 1) * GROUPS)
        return ref[heads, start : start + count, :].reshape(GROUPS * count, LANES)

    def scores_of(start, count, keys, group):
        if start not in biases:
            place = places(core, wagon, rows, tokens, start, (count, 1), 0)
            key_place = lane_of((1, keys))
            allowed = (key_place <= place) & (key_place >= opening(place, docs))
            biases[start] = jnp.where(allowed, 0.0, MASKED)
        scores = mm_nt(rows_of(q_ref, start, count, group), key_rows(kz, group, 0, keys))
        scores = scores.reshape(GROUPS, count, keys) + biases[start][None]
        return scores.reshape(GROUPS * count, keys)

    def finish(start, count, keys, group, scores):
        heads = slice(group * GROUPS, (group + 1) * GROUPS)
        low = low_half((GROUPS * count, LANES))
        lane = lane_of((GROUPS * count, LANES))
        top = jnp.max(scores, -1, keepdims=True)
        weights = jnp.exp(scores - top).astype(BF16)
        out = mm(weights, key_rows(vz, group, 0, keys))
        total = jnp.where(low, 1.0, out)
        lse = -(top + jnp.log(total))
        high = lse.astype(BF16).astype(F32)
        rest = lse - high
        middle = rest.astype(BF16).astype(F32)
        tail = jnp.where(
            lane == HD,
            high,
            jnp.where(lane == HD + 1, middle, jnp.where(lane == HD + 2, rest - middle, 0.0)),
        )
        q = rows_of(q_ref, start, count, group).astype(F32)
        q_aug = jnp.where(low, q, tail).astype(BF16)
        q_out[heads, start : start + count, :] = q_aug.reshape(GROUPS, count, LANES)
        out = jnp.where(low, out / jnp.where(low, roll(out, HD), 1.0), 0.0)
        heads_out[heads, start : start + count, :] = out.reshape(GROUPS, count, LANES)

    blocks = query_blocks(geometry)
    ahead([(*block, group) for block in blocks for group in range(KVH)], scores_of, finish)


def attend_back(geometry, core, wagon, docs, q_ref, do_ref, kz, vz, dq, dk, dv):
    rows, tokens, _ = geometry
    span, half = tokens, tokens // 2
    dk[...] = jnp.zeros_like(dk)
    dv[...] = jnp.zeros_like(dv)
    masks = {}

    def rows_of(ref, start, count, group):
        heads = slice(group * GROUPS, (group + 1) * GROUPS)
        return ref[heads, start : start + count, :].reshape(GROUPS * count, LANES)

    def products(start, count, key_start, key_count, group):
        if (start, key_start) not in masks:
            local = lane_of((1, GROUPS * count)) % count + start
            place = (wagon * rows + local // half) * tokens + core * half + local % half
            key_place = key_start + lax.broadcasted_iota(jnp.int32, (key_count, 1), 0)
            masks[start, key_start] = (key_place <= place) & (key_place >= opening(place, docs))
        scores = mm_nt(
            key_rows(kz, group, key_start, key_count), rows_of(q_ref, start, count, group)
        )
        grads = mm_nt(
            key_rows(vz, group, key_start, key_count), rows_of(do_ref, start, count, group)
        )
        return scores, grads

    def finish(start, count, key_start, key_count, group, ready):
        heads = slice(group * GROUPS, (group + 1) * GROUPS)
        blocks = slice(key_start // span, (key_start + key_count) // span)
        scores, grads = ready
        probs = jnp.where(masks[start, key_start], jnp.exp(scores), 0.0)
        slopes = (probs * grads).astype(BF16)
        part = (key_count // span, 2, half, LANES)
        do = rows_of(do_ref, start, count, group)
        dv[group, blocks] += mm(probs.astype(BF16), do).reshape(part)
        dk[group, blocks] += mm(slopes, rows_of(q_ref, start, count, group)).reshape(part)
        back = mm_tn(slopes, key_rows(kz, group, key_start, key_count))
        back = back.reshape(GROUPS, count, LANES)
        if key_start == 0:
            dq[heads, start : start + count, :] = back
        else:
            dq[heads, start : start + count, :] += back

    tasks = [
        (start, count, key_start, key_count, group)
        for start, count, keys in query_blocks(geometry)
        for key_start, key_count in tiles_of(keys, KEY_STEP)
        for group in range(KVH)
    ]
    ahead(tasks, products, finish)


def pack_heads(ref, rows, tile):
    count = rows.size
    low = low_half((count, LANES))
    first = ref[2 * tile, rows, :]
    if 2 * tile + 1 == HQ:
        return jnp.where(low, first, 0.0)
    return jnp.where(low, first, roll(ref[2 * tile + 1, rows, :], HD))


def piece_bits(h, row):
    x_bit, y_bit = row & 1, row >> 1
    return (x_bit, y_bit) if h == 0 else (y_bit, x_bit)


def store_piece(place, turned, core, row, h, f, g, chunk, value, kept, sent):
    f_bit, g_bit = piece_bits(h, row)
    spot = chunk ^ place if turned else chunk
    spot = (spot & 1) * 2 + spot // 2 if turned else spot
    value = value.astype(BF16)

    @pl.when(core == h)
    def _():
        kept[f ^ f_bit, g ^ g_bit, spot] = value

    @pl.when(core != h)
    def _():
        sent[f ^ f_bit, g ^ g_bit, spot] = value


def pack_kernel(geometry, inputs, cotangent, ids, wq, wk, wv, gain1, gain2, *refs):
    rows, tokens, _ = geometry
    half = tokens // 2
    core, member = lax.axis_index("section"), lax.rem(lax.axis_index("seq"), rows)
    outs, w_ref, (counts, sems) = refs[: 2 * rows], refs[2 * rows], refs[2 * rows + 1 :]
    mine = pl.ds(pl.multiple_of(core * half, half), half)
    copies = []
    for step in range(rows):
        target = member ^ step
        docs = ids[pl.ds(target, 1), :]
        first = jnp.sum((docs < 1).astype(F32), -1, keepdims=True)
        second = jnp.sum((docs < 2).astype(F32), -1, keepdims=True)
        lane = lane_of((PACK, half))
        value = jnp.where(lane == 0, first, jnp.where(lane == 1, second, 0.0))
        counts[step] = value.astype(BF16)
        copies += [
            (inputs.at[target, :, mine], outs[step].at[pl.ds(0, D)]),
            (counts.at[step], outs[step].at[pl.ds(D, PACK)]),
            (cotangent.at[target, :, mine], outs[rows + step]),
        ]
    copies = [pltpu.make_async_copy(a, b, sems.at[i]) for i, (a, b) in enumerate(copies)]
    for copy in copies:
        copy.start()
    one = lax.broadcasted_iota(jnp.int32, (KVW, KVW), 0) == lane_of((KVW, KVW))
    one = jnp.where(one, 1.0, 0.0).astype(BF16)
    keys, values = mm_tn(wk[...], one), mm_tn(wv[...], one)
    queries = wq[...].astype(F32)
    zeros = jnp.zeros((D, HD), F32)
    w_ref[:D] = jnp.concatenate([queries, keys, zeros, values], 1).astype(BF16)
    lines = []
    for gain in (gain1, gain2):
        rest = gain[...]
        for _ in range(3):
            part = rest.astype(BF16).astype(F32)
            lines.append(part)
            rest = rest - part
    lines = jnp.concatenate(lines + [jnp.zeros((PACK - 6, D), F32)], 0)
    lines = jnp.concatenate([lines, jnp.zeros((PACK, QKV - D), F32)], 1)
    w_ref[D:] = lines.astype(BF16)
    for copy in copies:
        copy.wait()


def unpack(block, half):
    return block[:D].T if half % LANES == 0 else block[:half]


def project_kernel(geometry, where, *refs):
    rows, tokens, _ = geometry
    half = tokens // 2
    packets, refs = refs[:rows], refs[rows:]
    mine, theirs, cos, sin, x_ref, q_ref, kv_ref, w_ref, lines, sems = refs
    core, member = where[0], where[3]
    weights = Weights(
        0, core, {"qkv": mine}, {"qkv": theirs}, {"qkv": w_ref, "gains": lines}, sems
    )
    for step in range(rows):
        x_ref[member ^ step] = unpack(packets[step][...], half)
    weights.wait("qkv", "gains")
    gain = gain_row(lines, 0)
    for start, count in tiles_of(rows * half, max(ROW_STEP, half)):
        stream = x_ref[start // half : (start + count) // half].reshape(count, D).astype(F32)
        rows_of = slice(start, start + count)
        project_rows(
            stream, gain, w_ref, cos[rows_of], sin[rows_of], q_ref, kv_ref, start, count
        )


def store_blocks(geometry, where, target, start, value):
    rows, tokens, _ = geometry
    half = tokens // 2
    for block in range(start // half, (start + value.shape[0]) // half):
        part = value[block * half - start : (block + 1) * half - start]
        part = part.T if half % LANES == 0 else part
        target[block ^ where[3]] = part


def forward_kernel(layer, geometry, where, docs, *refs):
    x_ref, q_ref, own, other, cos, sin = refs[:6]
    wg, wg2, wu, wu2, wd, wd2, wo, wo2, wq, wq2 = refs[6:16]
    refs = refs[16:]
    if layer == 1:
        earlier, refs = refs[0], refs[1:]
    q_aug, att, middle_ref, gate_ref, up_ref, y_ref = refs[:6]
    outs = refs[6:]
    if layer == 0:
        blocks_ref, q_next, kv_next = outs[:3]
        outs, parts, away = outs[3:-5], outs[-5:-1], outs[-1]
        saved = list(zip((q_aug, middle_ref, gate_ref, up_ref), parts))
        q_aug, middle_ref, gate_ref, up_ref = parts
    else:
        pair_refs, blocks_ref = outs[: geometry[0]], outs[geometry[0]]
        outs = outs[geometry[0] + 1 :]
    kz, vz, heads, wo_v, wg_v, wu_v, wd_v, lines, sems = outs[:9]
    core, wagon = where[0], where[4]
    mine = {"gate": wg, "up": wu, "down": wd, "out": wo, "qkv": wq}
    theirs = {"gate": wg2, "up": wu2, "down": wd2, "out": wo2, "qkv": wq2}
    names = {"out": wo_v, "gains": lines, "gate": wg_v, "up": wu_v, "down": wd_v}
    weights = Weights(layer, core, mine, theirs, names, sems)
    if layer == 0:
        wq_v, lines_next, sems_next = outs[9:]
        following = Weights(1, core, mine, theirs, {"qkv": wq_v, "gains": lines_next}, sems_next)
    place_keys(core, own, other, kz, vz)
    attend(geometry, core, wagon, docs, q_ref, kz, vz, heads, q_aug)
    leaving = []

    def leave(target, part, rows=None):
        if rows is not None:
            target, part = target.at[rows], part.at[rows]
        leaving.append(pltpu.make_async_copy(part, target, away.at[len(leaving)]))
        leaving[-1].start()

    if layer == 0:
        leave(*saved[0])
    weights.wait("out", "gains", "gate", "up", "down")
    gain_mlp = gain_row(lines, 1)
    if layer == 0:
        following.wait("qkv", "gains")
        gain_next = gain_row(lines_next, 0)
    tokens = x_ref.shape[0]
    half = geometry[1] // 2
    for start, count in tiles_of(tokens, max(ROW_STEP, half)):
        rows = pl.ds(start, count)
        for tile in range(4):
            att[rows, tile * LANES : (tile + 1) * LANES] = pack_heads(heads, rows, tile).astype(
                BF16
            )
        att[rows, 4 * LANES :] = heads[HQ - 1, rows, :HD].astype(BF16)
        middle = x_ref[rows, :].astype(F32) + mm(att[rows, :], wo_v[...])
        normed = (middle * norm_inverse(middle) * gain_mlp).astype(BF16)
        gate, up = mm(normed, wg_v[...]), mm(normed, wu_v[...])
        middle_ref[rows, :] = middle
        gate_ref[rows, :] = gate.astype(BF16)
        up_ref[rows, :] = up.astype(BF16)
        if layer == 0:
            for target, part in saved[1:]:
                leave(target, part, rows)
        hidden = (gate * jax.nn.sigmoid(gate) * up).astype(BF16)
        result = (middle + mm_nt(hidden, wd_v[...])).astype(BF16)
        y_ref[rows, :] = result
        store_blocks(geometry, where, blocks_ref, start, result)
        if layer == 0:
            project_rows(
                result.astype(F32),
                gain_next,
                wq_v,
                cos[rows, :],
                sin[rows, :],
                q_next,
                kv_next,
                start,
                count,
            )
    for copy in leaving:
        copy.wait()
    if layer == 1:
        for step, pair in enumerate(pair_refs):
            pair[pl.ds(core, 1)] = earlier[pl.ds(step, 1)]
            pair[pl.ds(1 - core, 1)] = blocks_ref[pl.ds(step, 1)]


def feed_kernel(layer, geometry, where, *refs):
    rows_in, tokens_in, chips = geometry
    half = tokens_in // 2
    core, row, place, member = where[0], where[1], where[2], where[3]
    if layer == 1:
        packets, refs = refs[:rows_in], refs[rows_in:]
    else:
        grad_ref, refs = refs[0], refs[1:]
    middle_ref, gate_ref, up_ref, wd, wd2, wq, wq2 = refs[:7]
    refs = refs[7:]
    if layer == 1:
        grad_ref, refs = refs[0], refs[1:]
    dgate, dup, kept, sent, normed, turned, hidden, downs, wd_v, lines, sems = refs
    weights = Weights(
        layer,
        core,
        {"down": wd, "qkv": wq},
        {"down": wd2, "qkv": wq2},
        {"down": wd_v, "gains": lines},
        sems,
    )
    if layer == 1:
        for step in range(rows_in):
            grad_ref[member ^ step] = unpack(packets[step][...], half)
    weights.wait("down", "gains")
    gain_mlp = gain_row(lines, 1)
    tokens = middle_ref.shape[0]
    for start, count in tiles_of(tokens, max(ROW_STEP, half)):
        rows = pl.ds(start, count)
        if layer == 1:
            branch = grad_ref[start // half : (start + count) // half].reshape(count, D)
        else:
            branch = grad_ref[rows, :]
        middle = middle_ref[rows, :]
        normed[rows, :] = (middle * norm_inverse(middle) * gain_mlp).astype(BF16)
        gate, up = gate_ref[rows, :].astype(F32), up_ref[rows, :].astype(F32)
        sig = jax.nn.sigmoid(gate)
        lifted = gate * sig
        grad_hidden = mm(branch, wd_v[...])
        hidden[rows, :] = (lifted * up).astype(BF16)
        dgate[rows, :] = (grad_hidden * up * (sig + lifted * (1.0 - sig))).astype(BF16)
        dup[rows, :] = (grad_hidden * lifted).astype(BF16)
    turned[...] = grad_ref[...].reshape(tokens, D).T
    for chunk in range(CHUNKS):
        downs[chunk] = mm(turned[...], hidden[:, chunk * TILE : (chunk + 1) * TILE])
    turned[...] = normed[...].T
    for h in range(2):
        for f in range(2):
            columns = slice((2 * h + f) * TILE, (2 * h + f + 1) * TILE)
            gates = mm(turned[...], dgate[:, columns])
            ups = mm(turned[...], dup[:, columns])
            for g in range(2):
                for chunk in range(CHUNKS):
                    lines_of = slice((2 * chunk + g) * SUB, (2 * chunk + g + 1) * SUB)
                    spots = pl.ds(((2 * h + f) * 2 + g) * SUB, SUB)
                    value = jnp.concatenate(
                        [gates[lines_of], ups[lines_of], downs[chunk, spots, :]], 0
                    )
                    store_piece(place, chips == 1, core, row, h, f, g, chunk, value, kept, sent)


def middle_kernel(layer, geometry, where, *refs):
    grad_ref, middle_ref, dgate, dup, att, wg, wg2, wu, wu2, wo, wo2, wq, wq2 = refs[:13]
    dm_ref, gain_out, do_heads, wg_v, wu_v, wo_v, lines, sems = refs[13:]
    weights = Weights(
        layer,
        where[0],
        {"gate": wg, "up": wu, "out": wo, "qkv": wq},
        {"gate": wg2, "up": wu2, "out": wo2, "qkv": wq2},
        {"gate": wg_v, "up": wu_v, "out": wo_v, "gains": lines},
        sems,
    )
    weights.wait("gate", "up", "out", "gains")
    gain_mlp = gain_row(lines, 1)
    tokens = middle_ref.shape[0]
    grad_gain = jnp.zeros((1, D), F32)
    for start, count in tiles_of(tokens, ROW_STEP):
        rows = pl.ds(start, count)
        middle = middle_ref[rows, :]
        grad_normed = mm_nt(dgate[rows, :], wg_v[...]) + mm_nt(dup[rows, :], wu_v[...])
        back, more = norm_back(grad_normed, middle, norm_inverse(middle), gain_mlp)
        grad_gain = grad_gain + more
        dm = grad_ref[rows, :].astype(F32) + back
        dm_ref[rows, :] = dm
        grad_att = mm_nt(dm.astype(BF16), wo_v[...]).astype(BF16).astype(F32)
        low = low_half((count, LANES))
        lane = lane_of((count, LANES))
        for head in range(HQ):
            if head < HQ - 1:
                tile = slice(head // 2 * LANES, (head // 2 + 1) * LANES)
                do = grad_att[:, tile]
                out = att[rows, tile].astype(F32)
            else:
                pad = jnp.zeros((count, HD), F32)
                do = jnp.concatenate([grad_att[:, 4 * LANES :], pad], 1)
                out = jnp.concatenate([att[rows, 4 * LANES :].astype(F32), pad], 1)
            if head % 2:
                do, out = roll(do, HD), roll(out, HD)
            do = jnp.where(low, do, 0.0)
            delta = -jnp.sum(do * out, -1, keepdims=True)
            high = delta.astype(BF16).astype(F32)
            do = jnp.where(lane == HD, high, jnp.where(lane == HD + 1, delta - high, do))
            do_heads[head, rows, :] = do.astype(BF16)
    gain_out[...] = grad_gain


def attend_back_kernel(geometry, where, docs, *refs):
    q_aug, do_heads, own, other, cos, sin = refs[:6]
    dq_out, kept, sent = refs[6:9]
    kz, vz, dq, dk, dv = refs[9:]
    core, wagon = where[0], where[4]
    place_keys(core, own, other, kz, vz)
    attend_back(geometry, core, wagon, docs, q_aug, do_heads, kz, vz, dq, dk, dv)
    for start, count in tiles_of(q_aug.shape[1], ROW_STEP):
        rows = pl.ds(start, count)
        for tile in range(5):
            value = pack_heads(dq, rows, tile) * SCALE
            value = value * cos[rows, :] - halves(value) * sin[rows, :]
            dq_out[rows, tile * LANES : (tile + 1) * LANES] = value.astype(BF16)
    _, blocks, _, half, _ = dk.shape
    low = low_half((blocks, half, LANES))
    for target, index in ((kept, core), (sent, 1 - core)):

        def pick(ref, group):
            return ref[group, :, pl.ds(index, 1)].reshape(blocks, half, LANES)

        def join(first, second):
            return jnp.where(low, first, roll(second, HD)).astype(target.dtype)

        target[:, :, 0:LANES] = join(pick(dk, 0), pick(dk, 1))
        target[:, :, LANES : 2 * LANES] = join(pick(dk, 2), pick(dv, 0))
        target[:, :, 2 * LANES :] = join(pick(dv, 1), pick(dv, 2))


def input_back_kernel(layer, geometry, where, *refs):
    rows_in, tokens_in, chips = geometry
    dm_ref, att, x_ref, dq, dkv, dkv2, gain_mlp, wq, wq2, cos, sin = refs[:11]
    dx_ref, blocks_refs, refs = refs[11], refs[12 : 12 + rows_in], refs[12 + rows_in :]
    kept, sent, blocks_ref, dqkv, normed, da, wq_v, lines, sems = refs
    core, row, place = where[0], where[1], where[2]
    weights = Weights(
        layer, core, {"qkv": wq}, {"qkv": wq2}, {"qkv": wq_v, "gains": lines}, sems
    )
    weights.wait("qkv", "gains")
    gain = gain_row(lines, 0)
    tokens = x_ref.shape[0]
    half = tokens_in // 2
    grad_gain = jnp.zeros((1, D), F32)
    for start, count in tiles_of(tokens, max(ROW_STEP, half)):
        rows = pl.ds(start, count)
        low = low_half((count, LANES))
        grads = [
            dkv[rows, t * LANES : (t + 1) * LANES]
            + dkv2[rows, t * LANES : (t + 1) * LANES].astype(F32)
            for t in range(3)
        ]
        for tile in range(4):
            lanes = slice(tile * LANES, (tile + 1) * LANES)
            dqkv[rows, lanes] = dq[rows, lanes]
        turned = roll(grads[0], HD)

        def unrotate(value):
            return value * cos[rows, :] - halves(value) * sin[rows, :]

        last = dq[rows, 4 * LANES :].astype(F32)
        dqkv[rows, 4 * LANES : 5 * LANES] = jnp.where(low, last, unrotate(turned)).astype(BF16)
        keys = unrotate(jnp.where(low, turned, roll(grads[1], HD)))
        dqkv[rows, 5 * LANES : 6 * LANES] = keys.astype(BF16)
        dqkv[rows, 6 * LANES : 7 * LANES] = jnp.where(low, 0.0, grads[1]).astype(BF16)
        dqkv[rows, 7 * LANES :] = grads[2].astype(BF16)
        stream = x_ref[rows, :].astype(F32)
        inverse = norm_inverse(stream)
        normed[rows, :] = (stream * inverse * gain).astype(BF16)
        grad_normed = mm_nt(dqkv[rows, :], wq_v[...])
        back, more = norm_back(grad_normed, stream, inverse, gain)
        grad_gain = grad_gain + more
        dm = dm_ref[rows, :]
        dx = (dm + back).astype(BF16)
        dx_ref[rows, :] = dx
        store_blocks(geometry, where, blocks_ref, start, dx)
        da[rows, 0:D] = dm.astype(BF16)
        da[rows, D:] = jnp.zeros((count, 2 * TILE - D), BF16)
    for step, block in enumerate(blocks_refs):
        block[...] = blocks_ref[step]
    pad = jnp.zeros((1, 2 * TILE - D), F32)
    lines = []
    for vector in (grad_gain, gain_mlp[...]):
        wide = jnp.concatenate([vector, pad], 1)
        lines += [wide[:, :TILE], wide[:, TILE:]]
    lines = jnp.concatenate(lines + [jnp.zeros((4, TILE), F32)], 0)
    for h in range(2):
        for f in range(2):
            if h == 0:
                value = mm_tn(normed[...], dqkv[:, f * TILE : (f + 1) * TILE])
            else:
                value = mm_tn(att[...], da[:, f * TILE : (f + 1) * TILE])
            if h == 1 and f == 1:
                more = mm_tn(normed[...], dqkv[:, 6 * LANES :])
                value = jnp.concatenate(
                    [
                        value[:, :LANES],
                        value[:, LANES : 2 * LANES] + more[:, :LANES],
                        more[:, LANES:],
                    ],
                    1,
                )
            for g in range(2):
                for chunk in range(CHUNKS):
                    part = value[(2 * chunk + g) * SUB : (2 * chunk + g + 1) * SUB]
                    part = jnp.concatenate([part, lines], 0)
                    store_piece(place, chips == 1, core, row, h, f, g, chunk, part, kept, sent)


def owners_kernel(geometry, where, *refs):
    rows, tokens, _ = geometry
    half = tokens // 2
    core, member = where[0], where[3]
    sets = [refs[i : i + rows + 1] for i in range(0, len(refs) - 2, rows + 1)]
    out, sems = refs[-2:]

    def move(blocks):
        copies = []
        for step in range(rows):
            target = member ^ step
            for side, index in ((0, core), (1, 1 - core)):
                lanes = pl.ds(pl.multiple_of(index * half, half), half)
                source = blocks[rows].at[step] if side else blocks[step]
                if len(sets) == 1:
                    source = source.at[side]
                sem = sems.at[2 * step + side]
                copies.append(pltpu.make_async_copy(source, out.at[target, :, lanes], sem))
        for copy in copies:
            copy.start()
        for copy in copies:
            copy.wait()

    if len(sets) == 1:
        move(sets[0])
    else:
        for number in range(2):

            @pl.when(core == number)
            def _():
                move(sets[number])


def gather_kernel(where, *refs):
    mlp0, mlp1, attn = refs[:2], refs[2:4], refs[4:6]
    wq, wk, wv, wo, wg, wu, wd, g1, g2 = refs[6:15]
    wide, share = refs[15:]
    core, row, place = where[0], where[1], where[2]
    for step in range(4):
        peer = row ^ step
        x_bit, y_bit = peer & 1, peer >> 1
        for kind in range(2):
            h = core if kind == 0 else 1 - core
            f = jnp.where(h == 0, x_bit, y_bit)
            g = jnp.where(h == 0, y_bit, x_bit)

            @pl.when(core == 0)
            def _():
                share[...] = mlp0[kind][step]

            @pl.when(core == 1)
            def _():
                share[...] = mlp1[1 - kind][step]

            part = share[...].astype(F32)
            rows = pl.ds(pl.multiple_of(g * SUB, 8), SUB)
            tile = 2 * h + f
            columns = pl.ds(pl.multiple_of(tile * TILE, LANES), TILE)
            wg[0, rows, columns] = part[:SUB]
            wu[0, rows, columns] = part[SUB : 2 * SUB]
            wd[0, pl.ds(pl.multiple_of((2 * tile + g) * SUB, 8), SUB), :] = part[2 * SUB :]
            part = attn[kind][step, core].astype(F32)
            wide[rows, columns] = part[:SUB]
    wq[0] = wide[:, :D]
    wk[0] = wide[:, D : D + KVW]
    wo[0] = wide[:, 2 * TILE : 2 * TILE + D]
    wv[0] = wide[:, 2 * TILE + D :]
    lines = attn[0][0, core].astype(F32)[SUB:]
    for kind, out in ((0, g1), (1, g2)):
        whole = jnp.concatenate(
            [lines[2 * kind : 2 * kind + 1], lines[2 * kind + 1 : 2 * kind + 2]], 1
        )
        for chunk in range(CHUNKS):

            @pl.when(place == chunk)
            def _():
                out[...] = whole[:, chunk * 2 * SUB : (chunk + 1) * 2 * SUB]


def rotary(place):
    frequency = 10000.0 ** (-jnp.arange(HD // 2, dtype=F32) * 2.0 / HD)
    angles = place.astype(F32)[:, None] * frequency[None, :]
    cosine, sine = jnp.cos(angles), jnp.sin(angles)
    return jnp.concatenate([cosine] * 4, 1), jnp.concatenate([-sine, sine] * 2, 1)


def on_device(
    inputs,
    cotangent,
    group_ids,
    w_query,
    w_key,
    w_value,
    w_out,
    w_gate,
    w_up,
    w_down,
    gain_attn,
    gain_mlp,
):
    core = lax.axis_index("section")
    row = lax.axis_index("row")
    place = lax.axis_index("seq")
    spans = lax.axis_size("seq")
    rows, tokens, _ = inputs.shape
    half = tokens // 2
    chips = spans // rows
    member, wagon = place % rows, place // rows
    own = rows * half
    blocks = chips * rows
    length = blocks * tokens
    geometry = (rows, tokens, chips)
    flipped = half % LANES == 0
    where = jnp.stack([core, row, place, member, wagon]).astype(jnp.int32)
    whole = 0 if chips == 1 else slice(None)
    clans = [[b + rows * j for j in range(chips)] for b in range(rows)]

    def turn(step):
        return [(s, s ^ step) for s in range(spans)]

    def sems(count):
        return pltpu.SemaphoreType.DMA((count,))

    def vmem(*dims, kind=BF16):
        return pltpu.VMEM(dims, kind)

    def flip(array):
        return jnp.swapaxes(array, -1, -2)

    pack_ins = [
        flip(inputs),
        flip(cotangent),
        group_ids,
        w_query[0],
        flip(w_key[0]),
        flip(w_value[0]),
        gain_attn,
        gain_mlp,
    ]
    if flipped:
        packed = call(
            functools.partial(pack_kernel, geometry),
            pack_ins,
            [ANY] * 2 + [VMEM] * 6,
            [shape((D + PACK, half))] * rows + [shape((D, half))] * rows + [shape((D + PACK, QKV))],
            [vmem(rows, PACK, half), sems(3 * rows)],
            0,
            room=56 * 1024 * 1024,
        )
        packets, shares, w_qkv = packed[:rows], packed[rows : 2 * rows], packed[-1]
    else:
        packets, shares = [], []
        below = [jnp.sum((group_ids < i).astype(F32), 1) for i in (1, 2)]
        counts = jnp.pad(jnp.stack(below, 1), ((0, 0), (0, D - 2))).astype(BF16)
        counts = jnp.pad(counts[:, None], ((0, 0), (0, PACK - 1), (0, 0)))
        for step in range(rows):
            target = member ^ step
            for array, outs in ((inputs, packets), (cotangent, shares)):
                part = lax.dynamic_index_in_dim(array, target, 0, False)
                part = lax.dynamic_slice_in_dim(part, core * half, half, 0)
                outs.append(part)
            line = lax.dynamic_index_in_dim(counts, target, 0, False)
            packets[-1] = jnp.concatenate([packets[-1], line], 0)
        w_qkv = jnp.concatenate(
            [w_query[0], w_key[0], jnp.zeros((D, HD), BF16), w_value[0]], 1
        )
        parts, rest = [], jnp.concatenate([gain_attn, gain_mlp], 0)
        for _ in range(3):
            parts.append(rest.astype(BF16))
            rest = rest - parts[-1].astype(F32)
        lines = jnp.stack(parts, 1).reshape(6, D)
        w_qkv = jnp.concatenate([w_qkv, jnp.pad(lines, ((0, PACK - 6), (0, QKV - D)))], 0)
    packets = [packets[0]] + [
        lax.ppermute(packets[step], "seq", turn(step)) for step in range(1, rows)
    ]
    w_qkv = [w_qkv, lax.ppermute(w_qkv, "section", SWAP)]
    mine = {"gate": w_gate[0], "up": w_up[0], "down": flip(w_down[0]), "out": w_out[0]}
    gates = dict(zip(mine, [*packets[1:4], w_qkv[1]]))
    pairs = {
        name: (value, lax.ppermute(hold(value, gates[name]), "section", SWAP))
        for name, value in mine.items()
    }
    pairs["qkv"] = w_qkv

    def weights_of(*names):
        return [side for name in names for side in pairs[name]]

    if flipped:
        docs = sum(packet[D, :2].astype(F32) for packet in packets)
    else:
        docs = sum(packet[half, :2].astype(F32) for packet in packets)
    if chips > 1:
        docs = lax.psum(docs, "seq", axis_index_groups=clans)
    docs = docs.astype(jnp.int32)
    local = jnp.arange(own, dtype=jnp.int32)
    tables = rotary((wagon * rows + local // half) * tokens + core * half + local % half)

    x_in, query, kv = call(
        functools.partial(project_kernel, geometry),
        [where, *packets, *w_qkv, *tables],
        [SMEM] + [VMEM] * rows + [ANY] * 2 + [VMEM] * 2,
        [shape((rows, half, D)), shape((HQ, own, LANES)), shape((own, 2 * KVW))],
        [vmem(D, QKV), vmem(PACK, QKV), sems(2)],
        2 * own * D * QKV,
    )
    x_in = x_in.reshape(own, D)

    def exchange(kv):
        kv = kv.reshape(rows, half, 2 * KVW)
        if chips > 1:
            kv = lax.all_gather(kv, "seq", axis=0, tiled=True, axis_index_groups=clans)
        return kv, lax.ppermute(kv, "section", SWAP)

    key_scratch = [vmem(KVH, blocks, 2, half, LANES)] * 2
    head_scratch = [vmem(HQ, own, LANES, kind=F32)]
    weight = {"gate": vmem(D, FF), "up": vmem(D, FF), "down": vmem(D, FF), "out": vmem(D, D)}
    lines_scratch = vmem(PACK, QKV)
    attn_flops = 4 * HQ * own * length * LANES
    feed_flops = 2 * own * D * (D + 3 * FF)
    flat = shape((own, D))
    wide = shape((own, FF))
    heads = shape((HQ, own, LANES))
    sent_blocks = shape((rows, D, half) if flipped else (rows, half, D))

    def forward(layer, x, query, kv, *earlier):
        outs = [heads, flat, shape((own, D), F32), wide, wide, flat, sent_blocks]
        scratch = key_scratch + head_scratch
        scratch += [weight["out"], weight["gate"], weight["up"], weight["down"]]
        scratch += [lines_scratch, sems(5)]
        if layer == 0:
            outs += [heads, shape((own, 2 * KVW))]
            scratch += [vmem(D, QKV), lines_scratch, sems(2)]
            scratch += [vmem(HQ, own, LANES), vmem(own, D, kind=F32), vmem(own, FF)]
            scratch += [vmem(own, FF), sems(16)]
        else:
            scratch = [vmem(*sent_blocks.shape)] + scratch
            outs = outs[:-1] + [shape((2,) + sent_blocks.shape[1:])] * rows
        return call(
            functools.partial(forward_kernel, layer, geometry),
            [where, docs, x, query, *kv, *tables]
            + weights_of("gate", "up", "down", "out", "qkv")
            + list(earlier),
            [SMEM] * 2 + [VMEM] * 6 + [ANY] * 10 + [VMEM] * len(earlier),
            outs,
            scratch,
            attn_flops + feed_flops,
            far=(0, 2, 3, 4) if layer == 0 else (),
        )

    kv0 = exchange(kv)
    q0, att0, middle0, gate0, up0, y0, blocks0, query, kv = forward(0, x_in, query, kv0)
    shares = [shares[0]] + [
        lax.ppermute(shares[step], "seq", turn(step)) for step in range(1, rows)
    ]
    kv1 = exchange(kv)
    outs = forward(1, y0, query, kv1, blocks0)
    q1, att1, middle1, gate1, up1, y1, *pair_blocks = hold(outs, shares)
    mlp_pieces = shape((2, 2, CHUNKS, 3 * SUB, TILE))
    attn_pieces = shape((2, 2, CHUNKS, SUB + 8, TILE))

    def feed(layer, where, grads, middle, gate, up, **order):
        outs = [shape((rows, half, D))] if layer == 1 else []
        return call(
            functools.partial(feed_kernel, layer, geometry),
            [where, *grads, middle, gate, up] + weights_of("down", "qkv"),
            [SMEM] + [VMEM] * (len(grads) + 3) + [ANY] * 4,
            outs + [wide, wide, mlp_pieces, mlp_pieces],
            [vmem(own, D), vmem(D, own), vmem(own, FF), vmem(CHUNKS, D, TILE, kind=F32)]
            + [weight["down"], lines_scratch, sems(2)],
            8 * own * D * FF,
            **order,
        )

    def spread(layer, where, grad, middle, dgate, dup, att, **order):
        return call(
            functools.partial(middle_kernel, layer, geometry),
            [where, grad, middle, dgate, dup, att] + weights_of("gate", "up", "out", "qkv"),
            [SMEM] + [VMEM] * 5 + [ANY] * 8,
            [shape((own, D), F32), shape((1, D), F32), heads],
            [weight["gate"], weight["up"], weight["out"], lines_scratch, sems(4)],
            2 * own * D * (D + 2 * FF),
            light=layer == 1,
            **order,
        )

    def attention_back(where, q_aug, do_heads, kv, **order):
        return call(
            functools.partial(attend_back_kernel, geometry),
            [where, docs, q_aug, do_heads, *kv, *tables],
            [SMEM] * 2 + [VMEM] * 6,
            [
                shape((own, 5 * LANES)),
                shape((blocks, half, 2 * KVW), F32),
                shape((blocks, half, 2 * KVW)),
            ],
            key_scratch
            + head_scratch
            + [vmem(KVH, blocks, 2, half, LANES, kind=F32)] * 2,
            3 * attn_flops,
            **order,
        )

    def trade_keys(dq, dkv, dkv_sent):
        dkv_got = lax.ppermute(dkv_sent, "section", SWAP)
        if chips > 1:
            dkv = lax.psum_scatter(
                (dkv + dkv_got).astype(BF16),
                "seq",
                scatter_dimension=0,
                tiled=True,
                axis_index_groups=clans,
            ).astype(F32)
            dkv_got = jnp.zeros(dkv.shape, BF16)
        return dq, dkv.reshape(own, 2 * KVW), dkv_got.reshape(own, 2 * KVW)

    def input_back(layer, where, dm, att, x, dq, dkv, dkv_got, gain_grad, **order):
        return call(
            functools.partial(input_back_kernel, layer, geometry),
            [where, dm, att, x, dq, dkv, dkv_got, gain_grad, *w_qkv, *tables],
            [SMEM] + [VMEM] * 7 + [ANY] * 2 + [VMEM] * 2,
            [flat]
            + [shape(sent_blocks.shape[1:])] * rows
            + [attn_pieces, attn_pieces],
            [vmem(*sent_blocks.shape), vmem(own, QKV), vmem(own, D), vmem(own, 2 * TILE), vmem(D, QKV)]
            + [lines_scratch, sems(2)],
            4 * own * D * QKV + 2 * own * D * D,
            **order,
        )

    def line(section, r):
        return section * 4 + r

    first_pairs = [(line(0, r), line(0, r ^ 1)) for r in range(4)]
    first_pairs += [(line(1, r), line(1, r ^ 2)) for r in range(4)]
    second_pairs = [(line(0, r), line(0, r ^ 2)) for r in range(4)]
    second_pairs += [(line(1, r), line(1, r ^ 1)) for r in range(4)]

    def to_core(sent):
        return lax.ppermute(sent, "section", SWAP)

    def sum_cores(kept, got):
        return (kept[1].astype(F32) + got[1]).astype(BF16)

    def to_first(out):
        return lax.ppermute(out, ("section", "row"), first_pairs)

    def sum_first(kept, got, near):
        return (kept[0, 1].astype(F32) + got[0, 1] + near[1]).astype(BF16)

    def to_second(out):
        return lax.ppermute(out, ("section", "row"), second_pairs)

    def sum_second(kept, got, near, far):
        return (kept[0, 0].astype(F32) + got[0, 0] + near[0] + far).astype(BF16)

    def to_seq(total):
        if chips > 1:
            return [lax.psum(total, "seq")]
        return [total[0]] + [
            lax.ppermute(total[spot], "seq", turn(step)) for spot, step in ((2, 1), (1, 2), (3, 3))
        ]

    def part_of(total, step):
        if chips > 1:
            return (total, total) if step == 1 else (lax.psum(total, "seq"),) * 2
        count = total.shape[0] // 2
        return total[:count], lax.ppermute(total[count:], "seq", turn(step))

    def sum_two(low, got):
        return low if chips > 1 else (low.astype(F32) + got).astype(BF16)

    def sum_seq(first, others):
        return sum((part.astype(F32) for part in others), first.astype(F32)).astype(BF16)

    def to_rows(blocks):
        return list(blocks[:1]) + [
            lax.ppermute(blocks[step], "seq", turn(step)) for step in range(1, rows)
        ]

    def to_owners(sets):
        if flipped:
            return call(
                functools.partial(owners_kernel, geometry),
                [where, *sum(sets, [])],
                [SMEM] + [ANY] * ((rows + 1) * len(sets)),
                [shape((rows, D, tokens))],
                [sems(2 * rows)],
                0,
            )[0]
        out = jnp.zeros((rows, 2, half, D), BF16)
        for step in range(rows):
            if len(sets) == 1:
                pair = [sets[0][step][0], sets[0][rows][step][1]]
            else:
                pair = [
                    jnp.where(core == 0, sets[0][step], sets[1][step]),
                    jnp.where(core == 0, sets[0][rows][step], sets[1][rows][step]),
                ]
            pair = jnp.where(core == 0, jnp.stack(pair), jnp.stack(pair[::-1]))
            out = lax.dynamic_update_index_in_dim(out, pair, member ^ step, 0)
        return flip(out.reshape(rows, tokens, D))

    def to_all(piece):
        return [piece] + [
            lax.ppermute(piece, "row", [(r, r ^ step) for r in range(4)]) for step in range(1, 4)
        ]

    ys = to_rows(pair_blocks)
    grad1, dgate, dup, kept_m1, sent = feed(1, where, shares, middle1, gate1, up1)
    grad1 = grad1.reshape(own, D)
    got_m1 = to_core(sent)

    dm, gain_grad, do_heads = hold(
        spread(1, where, grad1, middle1, dgate, dup, att1), ys[1], ys[2], got_m1
    )

    out = sum_cores(hold(kept_m1, dm), got_m1)
    near_m1 = to_first(out)
    kept_m1, *outs = hold(
        (kept_m1, *attention_back(where, q1, do_heads, kv1)), ys[3], near_m1
    )
    dq, dkv, dkv_got = trade_keys(*outs)

    out = sum_first(kept_m1, got_m1, near_m1)
    far_m1 = to_second(out)
    outs = input_back(
        1, hold(where, out), dm, att1, y0, dq, dkv, dkv_got, gain_grad, stack=ys
    )
    kept_m1, pile, dx1, *blocks1, kept_a1, sent = hold((kept_m1, *outs), far_m1)
    got_a1 = to_core(sent)
    ys.append(to_core(pile))

    total = sum_second(kept_m1, got_m1, near_m1, far_m1)
    low_m1, got = part_of(total, 1)
    outs = feed(0, hold(where, total), [dx1], middle0, gate0, up0)
    dgate, dup, kept_m0, sent = hold(outs, ys[rows], got_a1, got)
    got_m0 = to_core(sent)

    low_m1, got = part_of(sum_two(hold(low_m1, dgate), got), 2)
    out = sum_cores(hold(kept_a1, dgate), got_a1)
    near_a1 = to_first(out)
    activations = to_owners([ys])
    outs = spread(0, hold(where, out, low_m1), dx1, middle0, dgate, dup, att0)
    dm, gain_grad, do_heads, low_m1 = hold((*outs, low_m1), activations, near_a1, got_m0, got)
    piece_m1 = sum_two(low_m1, got)[whole]

    out_a1 = sum_first(hold(kept_a1, dm), got_a1, near_a1)
    far_a1 = to_second(out_a1)
    out_m0 = sum_cores(hold(kept_m0, dm), got_m0)
    near_m0 = to_first(out_m0)
    dxs1 = to_rows(hold(blocks1, dm))
    outs = attention_back(hold(where, out_a1, out_m0), q0, do_heads, kv0)
    kept_a1, kept_m0, *outs = hold((kept_a1, kept_m0, *outs), far_a1, near_m0, dxs1)
    dq, dkv, dkv_got = trade_keys(*outs)

    total_a1 = sum_second(kept_a1, got_a1, near_a1, far_a1)
    low_a1, got = part_of(total_a1, 1)
    out = sum_first(kept_m0, got_m0, near_m0)
    far_m0 = to_second(out)
    outs = input_back(
        0, hold(where, out, total_a1), dm, att0, x_in, dq, dkv, dkv_got, gain_grad, stack=dxs1
    )
    mlp1 = to_all(hold(piece_m1, out))
    kept_m0, low_a1, pile, dx0, *blocks0, kept_a0, sent = hold(
        (kept_m0, low_a1, *outs), far_m0, got, mlp1
    )

    got_a0 = to_core(sent)
    total = sum_second(kept_m0, got_m0, near_m0, far_m0)
    low_m0, got_low = part_of(total, 1)
    out = sum_cores(hold(kept_a0, total), got_a0)
    near_a0 = to_first(out)
    kept_a0, low_m0 = hold((kept_a0, low_m0), got_low, near_a0)
    low_m0, got_low = part_of(sum_two(low_m0, got_low), 2)
    low_a1, got_a1 = part_of(sum_two(hold(low_a1, kept_a0), got), 2)
    out = sum_first(kept_a0, got_a0, near_a0)
    far_a0 = to_second(out)
    total = sum_second(hold(kept_a0, got_low), got_a0, near_a0, far_a0)
    parts_a0 = to_seq(total)
    low_m0, low_a1, blocks0, pile, mlp1 = hold((low_m0, low_a1, blocks0, pile, mlp1), total)
    mlp0 = to_all(sum_two(low_m0, got_low)[whole])
    mlp1 = jnp.stack(mlp1)
    mlp1 = lax.ppermute(mlp1, "section", [(0, 1)]), mlp1
    dxs1.append(lax.ppermute(pile, "section", [(0, 1)]))
    dxs0 = to_rows(blocks0)
    attn = jnp.stack([sum_seq(parts_a0[0], parts_a0[1:]), sum_two(low_a1, got_a1)[whole]])
    mlp0 = hold(mlp0, attn)
    attn = to_all(attn)
    mlp0 = jnp.stack(mlp0)
    mlp0 = mlp0, lax.ppermute(mlp0, "section", [(1, 0)])
    dxs0 = hold(dxs0, attn)
    attn = jnp.stack(attn)
    attn = attn, to_core(attn)
    dxs0.append(lax.ppermute(hold(jnp.stack(dxs0), attn[0]), "section", [(1, 0)]))
    input_grads = to_owners([dxs0, dxs1])
    input_grads = flip(input_grads)[None]
    activations = flip(activations)[None]
    share = D // spans
    if chips == 1:
        grads = call(
            gather_kernel,
            [where, *mlp0, *mlp1, *attn],
            [SMEM] + [VMEM] * 6,
            [shape((1, share, width), F32) for width in (D, KVW, KVW, D, FF, FF)]
            + [shape((1, D, TILE), F32)]
            + [shape((1, share), F32)] * 2,
            [vmem(2 * SUB, FF, kind=F32), vmem(3 * SUB, TILE)],
            0,
        )
        grads = list(grads)
        grads[6] = flip(grads[6])
        return (activations, input_grads) + tuple(grads)

    def ordered(parts):
        parts = parts.reshape(2, 4, *parts.shape[1:]).swapaxes(0, 1).astype(F32)
        parts = jnp.take(parts, jnp.arange(4) ^ row, axis=0)
        parts = jnp.take(parts, jnp.arange(2) ^ core, axis=1)
        parts = parts.reshape((2, 2) + parts.shape[1:])
        return jnp.stack([parts[:, :, 0].swapaxes(0, 1), parts[:, :, 1]])

    def rows_of(part):
        full = part.transpose(3, 2, 4, 0, 1, 5).reshape(D, FF)
        return lax.dynamic_slice_in_dim(full, place * share, share, 0)[None]

    mlp1 = jnp.concatenate([mlp1[1], mlp1[0]], 0)
    mlp = ordered(jnp.where(core == 0, jnp.concatenate(mlp0, 0), mlp1))
    attn = ordered(lax.dynamic_index_in_dim(jnp.concatenate(attn, 0), core, 1, False))
    downs = mlp[..., 2 * SUB :, :].transpose(0, 1, 2, 4, 3, 5).reshape(D, FF)
    downs = lax.dynamic_slice_in_dim(downs, place * (FF // spans), FF // spans, 1).T[None]
    full = rows_of(attn[..., :SUB, :])
    lines = attn[0, 0, 0, 0, SUB : SUB + 4].reshape(2, 2 * TILE)[:, :D]
    lines = lax.dynamic_slice_in_dim(lines, place * share, share, 1)
    return (
        activations,
        input_grads,
        full[..., :D],
        full[..., D : D + KVW],
        full[..., 2 * TILE + D :],
        full[..., 2 * TILE : 2 * TILE + D],
        rows_of(mlp[..., :SUB, :]),
        rows_of(mlp[..., SUB : 2 * SUB, :]),
        downs,
        lines[:1],
        lines[1:],
    )


def solution(mesh):
    weights = P("section", None, None)
    shares = P("section", "seq", None)
    return jax.shard_map(
        on_device,
        mesh=mesh,
        in_specs=(P("row", "seq", None), P("row", "seq", None), P("row", "seq"))
        + (weights,) * 7
        + (P("section", None),) * 2,
        out_specs=(P("section", "row", "seq", None),) * 2
        + (shares,) * 7
        + (P("section", "seq"),) * 2,
        check_vma=False,
    )
```

```python
import functools

import jax
import jax.numpy as jnp
from jax import lax
from jax.experimental import pallas as pl
from jax.experimental.pallas import tpu as pltpu
from jax.sharding import PartitionSpec as P

D = 576
HQ = 9
KVH = 3
HD = 64
GROUPS = HQ // KVH
KVW = KVH * HD
LANES = 128
QKV = 1024
FF = 1536
CHUNKS = 4
SUB = D // CHUNKS // 2
TILE = FF // 4
PACK = 16
ROW_STEP = 256
KEY_STEP = 256
SCALE = HD**-0.5
SPARE = 4 * 1024 * 1024
EPSILON = 1e-05
MASKED = -1e30
F32 = jnp.float32
BF16 = jnp.bfloat16
VMEM = pl.BlockSpec(memory_space=pltpu.VMEM)
SMEM = pl.BlockSpec(memory_space=pltpu.SMEM)
ANY = pl.BlockSpec(memory_space=pl.ANY)
SWAP = [(0, 1), (1, 0)]


def mm(a, b):
    return jnp.dot(a, b, preferred_element_type=F32)


def mm_nt(a, b):
    return lax.dot_general(a, b, (((1,), (1,)), ((), ())), preferred_element_type=F32)


def mm_tn(a, b):
    return lax.dot_general(a, b, (((0,), (0,)), ((), ())), preferred_element_type=F32)


def shape(dims, kind=BF16):
    return jax.ShapeDtypeStruct(tuple(dims), kind)


def size_of(array):
    if not jnp.issubdtype(array.dtype, jnp.number):
        return 0
    *lead, rows, columns = (1, 1, *array.shape)
    size = -(-rows // 16) * 16 * -(-columns // LANES) * LANES * array.dtype.itemsize
    for dim in lead:
        size *= dim
    return size


def call(body, ins, specs, outs, scratch, flops, stack=(), room=None, light=False, far=()):
    moved = sum(a.size * a.dtype.itemsize for a in list(ins) + list(outs))
    inner, piled = len(ins), len(stack)
    held = [a for a, spec in zip(ins, specs) if spec is VMEM] + list(outs) + list(scratch)
    if room is None:
        room = sum(size_of(a) for a in held) + SPARE
        room += sum(size_of(a) for a in stack)
    piles = [shape((piled, *stack[0].shape), stack[0].dtype)] if piled else []

    def strip(*refs):
        mid = piled + inner
        if not piled:
            return body(*refs)
        pile, sems = refs[mid], refs[-1]
        copies = [
            pltpu.make_async_copy(source, pile.at[i], sems.at[i])
            for i, source in enumerate(refs[:piled])
        ]
        for copy in copies:
            copy.start()
        body(*refs[piled:mid], *refs[mid + 1 : -1])
        for copy in copies:
            copy.wait()

    return pl.pallas_call(
        strip,
        out_shape=tuple(piles) + tuple(
            pltpu.HBM(a.shape, a.dtype) if i in far else a for i, a in enumerate(outs)
        ),
        in_specs=[ANY] * piled + list(specs),
        out_specs=tuple([VMEM] * len(piles) + [ANY if i in far else VMEM for i in range(len(outs))]),
        scratch_shapes=list(scratch) + [pltpu.SemaphoreType.DMA((piled,))] * len(piles),
        compiler_params=pltpu.CompilerParams(vmem_limit_bytes=min(room, 56 * 1024 * 1024)),
        cost_estimate=pl.CostEstimate(
            flops=0 if light else int(flops),
            bytes_accessed=0 if light else int(moved),
            transcendentals=0,
        ),
    )(*stack, *ins)


def hold(value, *others):
    return lax.optimization_barrier((value, others))[0]


def lane_of(dims):
    return lax.broadcasted_iota(jnp.int32, dims, len(dims) - 1)


def roll(value, by):
    return pltpu.roll(value, by, value.ndim - 1)


def low_half(dims):
    return lane_of(dims) < HD


def halves(value):
    first = (lane_of(value.shape) & (HD - 1)) < HD // 2
    return jnp.where(first, roll(value, LANES - HD // 2), roll(value, HD // 2))


def tiles_of(count, step):
    step = min(count, step)
    return [(start, step) for start in range(0, count, step)]


def norm_inverse(stream):
    return lax.rsqrt(jnp.mean(stream * stream, -1, keepdims=True) + EPSILON)


def norm_back(incoming, stream, inverse, gain):
    weighted = incoming * gain
    slope = jnp.mean(weighted * stream, -1, keepdims=True)
    grad_gain = jnp.sum(incoming * (stream * inverse), 0, keepdims=True)
    return inverse * (weighted - stream * (inverse * inverse * slope)), grad_gain


def start_copy(layer, core, mine, theirs, target, sem):
    @pl.when(core == layer)
    def _():
        pltpu.make_async_copy(mine, target, sem).start()

    @pl.when(core != layer)
    def _():
        pltpu.make_async_copy(theirs, target, sem).start()


class Weights:
    def __init__(self, layer, core, mine, theirs, targets, sems):
        self.pending = {}
        for number, (name, target) in enumerate(targets.items()):
            if name in ("qkv", "gains"):
                lines = pl.ds(0, D) if name == "qkv" else pl.ds(D, PACK)
                pair = mine["qkv"].at[lines], theirs["qkv"].at[lines]
            else:
                pair = mine[name], theirs[name]
            start_copy(layer, core, *pair, target, sems.at[number])
            self.pending[name] = (pair[0], target, sems.at[number])

    def wait(self, *names):
        for name in names:
            pltpu.make_async_copy(*self.pending.pop(name)).wait()


def gain_row(lines, kind):
    parts = lines[...].astype(F32)
    parts = [parts[3 * kind + i : 3 * kind + i + 1, :D] for i in range(3)]
    return parts[0] + parts[1] + parts[2]


def project_rows(stream, gain, w_ref, cos, sin, q_ref, kv_ref, start, count):
    normed = (stream * norm_inverse(stream) * gain).astype(BF16)
    raw = mm(normed, w_ref[...])
    low = low_half((count, LANES))
    tiles = []
    for t in range(6):
        tile = raw[:, t * LANES : (t + 1) * LANES]
        tiles.append(tile * cos + halves(tile) * sin)
    rows = pl.ds(start, count)
    for head in range(HQ):
        tile = tiles[head // 2]
        tile = roll(tile, HD) if head % 2 else tile
        q_ref[head, rows, :] = jnp.where(low, tile * SCALE, 0.0).astype(BF16)
    kv_ref[rows, 0:LANES] = jnp.where(low, roll(tiles[4], HD), roll(tiles[5], HD)).astype(BF16)
    kv_ref[rows, LANES : 2 * LANES] = jnp.where(
        low, roll(tiles[5], HD), raw[:, 6 * LANES : 7 * LANES]
    ).astype(BF16)
    kv_ref[rows, 2 * LANES :] = raw[:, 7 * LANES :].astype(BF16)


def place_keys(core, own, other, kz, vz):
    for part, index in ((own, core), (other, 1 - core)):
        blocks, half, _ = part.shape
        low = low_half((blocks, half, LANES))
        tiles = [part[:, :, t * LANES : (t + 1) * LANES].astype(F32) for t in range(3)]
        turned = [roll(tile, HD) for tile in tiles]
        for target, heads in (
            (kz, (tiles[0], turned[0], tiles[1])),
            (vz, (turned[1], tiles[2], turned[2])),
        ):
            for group in range(KVH):
                value = jnp.where(low, heads[group], 1.0).astype(BF16)
                target[group, :, pl.ds(index, 1)] = value[:, None]


def key_rows(ref, group, start, count):
    _, _, _, half, _ = ref.shape
    span = 2 * half
    part = ref[group, start // span : (start + count) // span]
    return part.reshape(count, LANES)


def places(core, wagon, rows, tokens, start, dims, axis):
    half = tokens // 2
    local = lax.broadcasted_iota(jnp.int32, dims, axis) + start
    block, inside = local // half, local % half
    return (wagon * rows + block) * tokens + core * half + inside


def opening(place, docs):
    first, second = docs[0], docs[1]
    return jnp.where(place < first, 0, jnp.where(place < second, first, second))


def query_blocks(geometry):
    rows, tokens, chips = geometry
    half = tokens // 2
    if chips == 1:
        return [(b * half, half, (b + 1) * tokens) for b in range(rows)]
    return [(0, rows * half, chips * rows * tokens)]


def ahead(tasks, first, second):
    ready = first(*tasks[0])
    for number, task in enumerate(tasks):
        following = first(*tasks[number + 1]) if number + 1 < len(tasks) else None
        second(*task, ready)
        ready = following


def attend(geometry, core, wagon, docs, q_ref, kz, vz, heads_out, q_out):
    rows, tokens, _ = geometry
    biases = {}

    def rows_of(ref, start, count, group):
        heads = slice(group * GROUPS, (group + 1) * GROUPS)
        return ref[heads, start : start + count, :].reshape(GROUPS * count, LANES)

    def scores_of(start, count, keys, group):
        if start not in biases:
            place = places(core, wagon, rows, tokens, start, (count, 1), 0)
            key_place = lane_of((1, keys))
            allowed = (key_place <= place) & (key_place >= opening(place, docs))
            biases[start] = jnp.where(allowed, 0.0, MASKED)
        scores = mm_nt(rows_of(q_ref, start, count, group), key_rows(kz, group, 0, keys))
        scores = scores.reshape(GROUPS, count, keys) + biases[start][None]
        return scores.reshape(GROUPS * count, keys)

    def finish(start, count, keys, group, scores):
        heads = slice(group * GROUPS, (group + 1) * GROUPS)
        low = low_half((GROUPS * count, LANES))
        lane = lane_of((GROUPS * count, LANES))
        top = jnp.max(scores, -1, keepdims=True)
        weights = jnp.exp(scores - top).astype(BF16)
        out = mm(weights, key_rows(vz, group, 0, keys))
        total = jnp.where(low, 1.0, out)
        lse = -(top + jnp.log(total))
        high = lse.astype(BF16).astype(F32)
        rest = lse - high
        middle = rest.astype(BF16).astype(F32)
        tail = jnp.where(
            lane == HD,
            high,
            jnp.where(lane == HD + 1, middle, jnp.where(lane == HD + 2, rest - middle, 0.0)),
        )
        q = rows_of(q_ref, start, count, group).astype(F32)
        q_aug = jnp.where(low, q, tail).astype(BF16)
        q_out[heads, start : start + count, :] = q_aug.reshape(GROUPS, count, LANES)
        out = jnp.where(low, out / jnp.where(low, roll(out, HD), 1.0), 0.0)
        heads_out[heads, start : start + count, :] = out.reshape(GROUPS, count, LANES)

    blocks = query_blocks(geometry)
    ahead([(*block, group) for block in blocks for group in range(KVH)], scores_of, finish)


def attend_back(geometry, core, wagon, docs, q_ref, do_ref, kz, vz, dq, dk, dv):
    rows, tokens, _ = geometry
    span, half = tokens, tokens // 2
    dk[...] = jnp.zeros_like(dk)
    dv[...] = jnp.zeros_like(dv)
    masks = {}

    def rows_of(ref, start, count, group):
        heads = slice(group * GROUPS, (group + 1) * GROUPS)
        return ref[heads, start : start + count, :].reshape(GROUPS * count, LANES)

    def products(start, count, key_start, key_count, group):
        if (start, key_start) not in masks:
            local = lane_of((1, GROUPS * count)) % count + start
            place = (wagon * rows + local // half) * tokens + core * half + local % half
            key_place = key_start + lax.broadcasted_iota(jnp.int32, (key_count, 1), 0)
            masks[start, key_start] = (key_place <= place) & (key_place >= opening(place, docs))
        scores = mm_nt(
            key_rows(kz, group, key_start, key_count), rows_of(q_ref, start, count, group)
        )
        grads = mm_nt(
            key_rows(vz, group, key_start, key_count), rows_of(do_ref, start, count, group)
        )
        return scores, grads

    def finish(start, count, key_start, key_count, group, ready):
        heads = slice(group * GROUPS, (group + 1) * GROUPS)
        blocks = slice(key_start // span, (key_start + key_count) // span)
        scores, grads = ready
        probs = jnp.where(masks[start, key_start], jnp.exp(scores), 0.0)
        slopes = (probs * grads).astype(BF16)
        part = (key_count // span, 2, half, LANES)
        do = rows_of(do_ref, start, count, group)
        dv[group, blocks] += mm(probs.astype(BF16), do).reshape(part)
        dk[group, blocks] += mm(slopes, rows_of(q_ref, start, count, group)).reshape(part)
        back = mm_tn(slopes, key_rows(kz, group, key_start, key_count))
        back = back.reshape(GROUPS, count, LANES)
        if key_start == 0:
            dq[heads, start : start + count, :] = back
        else:
            dq[heads, start : start + count, :] += back

    tasks = [
        (start, count, key_start, key_count, group)
        for start, count, keys in query_blocks(geometry)
        for key_start, key_count in tiles_of(keys, KEY_STEP)
        for group in range(KVH)
    ]
    ahead(tasks, products, finish)


def pack_heads(ref, rows, tile):
    count = rows.size
    low = low_half((count, LANES))
    first = ref[2 * tile, rows, :]
    if 2 * tile + 1 == HQ:
        return jnp.where(low, first, 0.0)
    return jnp.where(low, first, roll(ref[2 * tile + 1, rows, :], HD))


def piece_bits(h, row):
    x_bit, y_bit = row & 1, row >> 1
    return (x_bit, y_bit) if h == 0 else (y_bit, x_bit)


def store_piece(place, turned, core, row, h, f, g, chunk, value, kept, sent):
    f_bit, g_bit = piece_bits(h, row)
    spot = chunk ^ place if turned else chunk
    spot = (spot & 1) * 2 + spot // 2 if turned else spot
    value = value.astype(BF16)

    @pl.when(core == h)
    def _():
        kept[f ^ f_bit, g ^ g_bit, spot] = value

    @pl.when(core != h)
    def _():
        sent[f ^ f_bit, g ^ g_bit, spot] = value


def pack_kernel(geometry, inputs, cotangent, ids, wq, wk, wv, gain1, gain2, *refs):
    rows, tokens, _ = geometry
    half = tokens // 2
    core, member = lax.axis_index("section"), lax.rem(lax.axis_index("seq"), rows)
    outs, w_ref, (counts, sems) = refs[: 2 * rows], refs[2 * rows], refs[2 * rows + 1 :]
    mine = pl.ds(pl.multiple_of(core * half, half), half)
    copies = []
    for step in range(rows):
        target = member ^ step
        docs = ids[pl.ds(target, 1), :]
        first = jnp.sum((docs < 1).astype(F32), -1, keepdims=True)
        second = jnp.sum((docs < 2).astype(F32), -1, keepdims=True)
        lane = lane_of((PACK, half))
        value = jnp.where(lane == 0, first, jnp.where(lane == 1, second, 0.0))
        counts[step] = value.astype(BF16)
        copies += [
            (inputs.at[target, :, mine], outs[step].at[pl.ds(0, D)]),
            (counts.at[step], outs[step].at[pl.ds(D, PACK)]),
            (cotangent.at[target, :, mine], outs[rows + step]),
        ]
    copies = [pltpu.make_async_copy(a, b, sems.at[i]) for i, (a, b) in enumerate(copies)]
    for copy in copies:
        copy.start()
    one = lax.broadcasted_iota(jnp.int32, (KVW, KVW), 0) == lane_of((KVW, KVW))
    one = jnp.where(one, 1.0, 0.0).astype(BF16)
    keys, values = mm_tn(wk[...], one), mm_tn(wv[...], one)
    queries = wq[...].astype(F32)
    zeros = jnp.zeros((D, HD), F32)
    w_ref[:D] = jnp.concatenate([queries, keys, zeros, values], 1).astype(BF16)
    lines = []
    for gain in (gain1, gain2):
        rest = gain[...]
        for _ in range(3):
            part = rest.astype(BF16).astype(F32)
            lines.append(part)
            rest = rest - part
    lines = jnp.concatenate(lines + [jnp.zeros((PACK - 6, D), F32)], 0)
    lines = jnp.concatenate([lines, jnp.zeros((PACK, QKV - D), F32)], 1)
    w_ref[D:] = lines.astype(BF16)
    for copy in copies:
        copy.wait()


def unpack(block, half):
    return block[:D].T if half % LANES == 0 else block[:half]


def project_kernel(geometry, where, *refs):
    rows, tokens, _ = geometry
    half = tokens // 2
    packets, refs = refs[:rows], refs[rows:]
    mine, theirs, cos, sin, x_ref, q_ref, kv_ref, w_ref, lines, sems = refs
    core, member = where[0], where[3]
    weights = Weights(
        0, core, {"qkv": mine}, {"qkv": theirs}, {"qkv": w_ref, "gains": lines}, sems
    )
    for step in range(rows):
        x_ref[member ^ step] = unpack(packets[step][...], half)
    weights.wait("qkv", "gains")
    gain = gain_row(lines, 0)
    for start, count in tiles_of(rows * half, max(ROW_STEP, half)):
        stream = x_ref[start // half : (start + count) // half].reshape(count, D).astype(F32)
        rows_of = slice(start, start + count)
        project_rows(
            stream, gain, w_ref, cos[rows_of], sin[rows_of], q_ref, kv_ref, start, count
        )


def store_blocks(geometry, where, target, start, value):
    rows, tokens, _ = geometry
    half = tokens // 2
    for block in range(start // half, (start + value.shape[0]) // half):
        part = value[block * half - start : (block + 1) * half - start]
        part = part.T if half % LANES == 0 else part
        target[block ^ where[3]] = part


def forward_kernel(layer, geometry, where, docs, *refs):
    x_ref, q_ref, own, other, cos, sin = refs[:6]
    wg, wg2, wu, wu2, wd, wd2, wo, wo2, wq, wq2 = refs[6:16]
    refs = refs[16:]
    if layer == 1:
        earlier, refs = refs[0], refs[1:]
    q_aug, att, middle_ref, gate_ref, up_ref, y_ref = refs[:6]
    outs = refs[6:]
    if layer == 0:
        blocks_ref, q_next, kv_next = outs[:3]
        outs, parts, away = outs[3:-5], outs[-5:-1], outs[-1]
        saved = list(zip((q_aug, middle_ref, gate_ref, up_ref), parts))
        q_aug, middle_ref, gate_ref, up_ref = parts
    else:
        pair_refs, blocks_ref = outs[: geometry[0]], outs[geometry[0]]
        outs = outs[geometry[0] + 1 :]
    kz, vz, heads, wo_v, wg_v, wu_v, wd_v, lines, sems = outs[:9]
    core, wagon = where[0], where[4]
    mine = {"gate": wg, "up": wu, "down": wd, "out": wo, "qkv": wq}
    theirs = {"gate": wg2, "up": wu2, "down": wd2, "out": wo2, "qkv": wq2}
    names = {"out": wo_v, "gains": lines, "gate": wg_v, "up": wu_v, "down": wd_v}
    weights = Weights(layer, core, mine, theirs, names, sems)
    if layer == 0:
        wq_v, lines_next, sems_next = outs[9:]
        following = Weights(1, core, mine, theirs, {"qkv": wq_v, "gains": lines_next}, sems_next)
    place_keys(core, own, other, kz, vz)
    attend(geometry, core, wagon, docs, q_ref, kz, vz, heads, q_aug)
    leaving = []

    def leave(target, part, rows=None):
        if rows is not None:
            target, part = target.at[rows], part.at[rows]
        leaving.append(pltpu.make_async_copy(part, target, away.at[len(leaving)]))
        leaving[-1].start()

    if layer == 0:
        leave(*saved[0])
    weights.wait("out", "gains", "gate", "up", "down")
    gain_mlp = gain_row(lines, 1)
    if layer == 0:
        following.wait("qkv", "gains")
        gain_next = gain_row(lines_next, 0)
    tokens = x_ref.shape[0]
    half = geometry[1] // 2
    for start, count in tiles_of(tokens, max(ROW_STEP, half)):
        rows = pl.ds(start, count)
        for tile in range(4):
            att[rows, tile * LANES : (tile + 1) * LANES] = pack_heads(heads, rows, tile).astype(
                BF16
            )
        att[rows, 4 * LANES :] = heads[HQ - 1, rows, :HD].astype(BF16)
        middle = x_ref[rows, :].astype(F32) + mm(att[rows, :], wo_v[...])
        normed = (middle * norm_inverse(middle) * gain_mlp).astype(BF16)
        gate, up = mm(normed, wg_v[...]), mm(normed, wu_v[...])
        middle_ref[rows, :] = middle
        gate_ref[rows, :] = gate.astype(BF16)
        up_ref[rows, :] = up.astype(BF16)
        if layer == 0:
            for target, part in saved[1:]:
                leave(target, part, rows)
        hidden = (gate * jax.nn.sigmoid(gate) * up).astype(BF16)
        result = (middle + mm_nt(hidden, wd_v[...])).astype(BF16)
        y_ref[rows, :] = result
        store_blocks(geometry, where, blocks_ref, start, result)
        if layer == 0:
            project_rows(
                result.astype(F32),
                gain_next,
                wq_v,
                cos[rows, :],
                sin[rows, :],
                q_next,
                kv_next,
                start,
                count,
            )
    for copy in leaving:
        copy.wait()
    if layer == 1:
        for step, pair in enumerate(pair_refs):
            pair[pl.ds(core, 1)] = earlier[pl.ds(step, 1)]
            pair[pl.ds(1 - core, 1)] = blocks_ref[pl.ds(step, 1)]


def feed_kernel(layer, geometry, where, *refs):
    rows_in, tokens_in, chips = geometry
    half = tokens_in // 2
    core, row, place, member = where[0], where[1], where[2], where[3]
    if layer == 1:
        packets, refs = refs[:rows_in], refs[rows_in:]
    else:
        grad_ref, refs = refs[0], refs[1:]
    middle_ref, gate_ref, up_ref, wd, wd2, wq, wq2 = refs[:7]
    refs = refs[7:]
    if layer == 1:
        grad_ref, refs = refs[0], refs[1:]
    dgate, dup, kept, sent, normed, turned, hidden, downs, wd_v, lines, sems = refs
    weights = Weights(
        layer,
        core,
        {"down": wd, "qkv": wq},
        {"down": wd2, "qkv": wq2},
        {"down": wd_v, "gains": lines},
        sems,
    )
    if layer == 1:
        for step in range(rows_in):
            grad_ref[member ^ step] = unpack(packets[step][...], half)
    weights.wait("down", "gains")
    gain_mlp = gain_row(lines, 1)
    tokens = middle_ref.shape[0]
    for start, count in tiles_of(tokens, max(ROW_STEP, half)):
        rows = pl.ds(start, count)
        if layer == 1:
            branch = grad_ref[start // half : (start + count) // half].reshape(count, D)
        else:
            branch = grad_ref[rows, :]
        middle = middle_ref[rows, :]
        normed[rows, :] = (middle * norm_inverse(middle) * gain_mlp).astype(BF16)
        gate, up = gate_ref[rows, :].astype(F32), up_ref[rows, :].astype(F32)
        sig = jax.nn.sigmoid(gate)
        lifted = gate * sig
        grad_hidden = mm(branch, wd_v[...])
        hidden[rows, :] = (lifted * up).astype(BF16)
        dgate[rows, :] = (grad_hidden * up * (sig + lifted * (1.0 - sig))).astype(BF16)
        dup[rows, :] = (grad_hidden * lifted).astype(BF16)
    turned[...] = grad_ref[...].reshape(tokens, D).T
    for chunk in range(CHUNKS):
        downs[chunk] = mm(turned[...], hidden[:, chunk * TILE : (chunk + 1) * TILE])
    turned[...] = normed[...].T
    for h in range(2):
        for f in range(2):
            columns = slice((2 * h + f) * TILE, (2 * h + f + 1) * TILE)
            gates = mm(turned[...], dgate[:, columns])
            ups = mm(turned[...], dup[:, columns])
            for g in range(2):
                for chunk in range(CHUNKS):
                    lines_of = slice((2 * chunk + g) * SUB, (2 * chunk + g + 1) * SUB)
                    spots = pl.ds(((2 * h + f) * 2 + g) * SUB, SUB)
                    value = jnp.concatenate(
                        [gates[lines_of], ups[lines_of], downs[chunk, spots, :]], 0
                    )
                    store_piece(place, chips == 1, core, row, h, f, g, chunk, value, kept, sent)


def middle_kernel(layer, geometry, where, *refs):
    grad_ref, middle_ref, dgate, dup, att, wg, wg2, wu, wu2, wo, wo2, wq, wq2 = refs[:13]
    dm_ref, gain_out, do_heads, wg_v, wu_v, wo_v, lines, sems = refs[13:]
    weights = Weights(
        layer,
        where[0],
        {"gate": wg, "up": wu, "out": wo, "qkv": wq},
        {"gate": wg2, "up": wu2, "out": wo2, "qkv": wq2},
        {"gate": wg_v, "up": wu_v, "out": wo_v, "gains": lines},
        sems,
    )
    weights.wait("gate", "up", "out", "gains")
    gain_mlp = gain_row(lines, 1)
    tokens = middle_ref.shape[0]
    grad_gain = jnp.zeros((1, D), F32)
    for start, count in tiles_of(tokens, ROW_STEP):
        rows = pl.ds(start, count)
        middle = middle_ref[rows, :]
        grad_normed = mm_nt(dgate[rows, :], wg_v[...]) + mm_nt(dup[rows, :], wu_v[...])
        back, more = norm_back(grad_normed, middle, norm_inverse(middle), gain_mlp)
        grad_gain = grad_gain + more
        dm = grad_ref[rows, :].astype(F32) + back
        dm_ref[rows, :] = dm
        grad_att = mm_nt(dm.astype(BF16), wo_v[...]).astype(BF16).astype(F32)
        low = low_half((count, LANES))
        lane = lane_of((count, LANES))
        for head in range(HQ):
            if head < HQ - 1:
                tile = slice(head // 2 * LANES, (head // 2 + 1) * LANES)
                do = grad_att[:, tile]
                out = att[rows, tile].astype(F32)
            else:
                pad = jnp.zeros((count, HD), F32)
                do = jnp.concatenate([grad_att[:, 4 * LANES :], pad], 1)
                out = jnp.concatenate([att[rows, 4 * LANES :].astype(F32), pad], 1)
            if head % 2:
                do, out = roll(do, HD), roll(out, HD)
            do = jnp.where(low, do, 0.0)
            delta = -jnp.sum(do * out, -1, keepdims=True)
            high = delta.astype(BF16).astype(F32)
            do = jnp.where(lane == HD, high, jnp.where(lane == HD + 1, delta - high, do))
            do_heads[head, rows, :] = do.astype(BF16)
    gain_out[...] = grad_gain


def attend_back_kernel(geometry, where, docs, *refs):
    q_aug, do_heads, own, other, cos, sin = refs[:6]
    dq_out, kept, sent = refs[6:9]
    kz, vz, dq, dk, dv = refs[9:]
    core, wagon = where[0], where[4]
    place_keys(core, own, other, kz, vz)
    attend_back(geometry, core, wagon, docs, q_aug, do_heads, kz, vz, dq, dk, dv)
    for start, count in tiles_of(q_aug.shape[1], ROW_STEP):
        rows = pl.ds(start, count)
        for tile in range(5):
            value = pack_heads(dq, rows, tile) * SCALE
            value = value * cos[rows, :] - halves(value) * sin[rows, :]
            dq_out[rows, tile * LANES : (tile + 1) * LANES] = value.astype(BF16)
    _, blocks, _, half, _ = dk.shape
    low = low_half((blocks, half, LANES))
    for target, index in ((kept, core), (sent, 1 - core)):

        def pick(ref, group):
            return ref[group, :, pl.ds(index, 1)].reshape(blocks, half, LANES)

        def join(first, second):
            return jnp.where(low, first, roll(second, HD)).astype(target.dtype)

        target[:, :, 0:LANES] = join(pick(dk, 0), pick(dk, 1))
        target[:, :, LANES : 2 * LANES] = join(pick(dk, 2), pick(dv, 0))
        target[:, :, 2 * LANES :] = join(pick(dv, 1), pick(dv, 2))


def input_back_kernel(layer, geometry, where, *refs):
    rows_in, tokens_in, chips = geometry
    dm_ref, att, x_ref, dq, dkv, dkv2, gain_mlp, wq, wq2, cos, sin = refs[:11]
    dx_ref, blocks_refs, refs = refs[11], refs[12 : 12 + rows_in], refs[12 + rows_in :]
    kept, sent, blocks_ref, dqkv, normed, da, wq_v, lines, sems = refs
    core, row, place = where[0], where[1], where[2]
    weights = Weights(
        layer, core, {"qkv": wq}, {"qkv": wq2}, {"qkv": wq_v, "gains": lines}, sems
    )
    weights.wait("qkv", "gains")
    gain = gain_row(lines, 0)
    tokens = x_ref.shape[0]
    half = tokens_in // 2
    grad_gain = jnp.zeros((1, D), F32)
    for start, count in tiles_of(tokens, max(ROW_STEP, half)):
        rows = pl.ds(start, count)
        low = low_half((count, LANES))
        grads = [
            dkv[rows, t * LANES : (t + 1) * LANES]
            + dkv2[rows, t * LANES : (t + 1) * LANES].astype(F32)
            for t in range(3)
        ]
        for tile in range(4):
            lanes = slice(tile * LANES, (tile + 1) * LANES)
            dqkv[rows, lanes] = dq[rows, lanes]
        turned = roll(grads[0], HD)

        def unrotate(value):
            return value * cos[rows, :] - halves(value) * sin[rows, :]

        last = dq[rows, 4 * LANES :].astype(F32)
        dqkv[rows, 4 * LANES : 5 * LANES] = jnp.where(low, last, unrotate(turned)).astype(BF16)
        keys = unrotate(jnp.where(low, turned, roll(grads[1], HD)))
        dqkv[rows, 5 * LANES : 6 * LANES] = keys.astype(BF16)
        dqkv[rows, 6 * LANES : 7 * LANES] = jnp.where(low, 0.0, grads[1]).astype(BF16)
        dqkv[rows, 7 * LANES :] = grads[2].astype(BF16)
        stream = x_ref[rows, :].astype(F32)
        inverse = norm_inverse(stream)
        normed[rows, :] = (stream * inverse * gain).astype(BF16)
        grad_normed = mm_nt(dqkv[rows, :], wq_v[...])
        back, more = norm_back(grad_normed, stream, inverse, gain)
        grad_gain = grad_gain + more
        dm = dm_ref[rows, :]
        dx = (dm + back).astype(BF16)
        dx_ref[rows, :] = dx
        store_blocks(geometry, where, blocks_ref, start, dx)
        da[rows, 0:D] = dm.astype(BF16)
        da[rows, D:] = jnp.zeros((count, 2 * TILE - D), BF16)
    for step, block in enumerate(blocks_refs):
        block[...] = blocks_ref[step]
    pad = jnp.zeros((1, 2 * TILE - D), F32)
    lines = []
    for vector in (grad_gain, gain_mlp[...]):
        wide = jnp.concatenate([vector, pad], 1)
        lines += [wide[:, :TILE], wide[:, TILE:]]
    lines = jnp.concatenate(lines + [jnp.zeros((4, TILE), F32)], 0)
    for h in range(2):
        for f in range(2):
            if h == 0:
                value = mm_tn(normed[...], dqkv[:, f * TILE : (f + 1) * TILE])
            else:
                value = mm_tn(att[...], da[:, f * TILE : (f + 1) * TILE])
            if h == 1 and f == 1:
                more = mm_tn(normed[...], dqkv[:, 6 * LANES :])
                value = jnp.concatenate(
                    [
                        value[:, :LANES],
                        value[:, LANES : 2 * LANES] + more[:, :LANES],
                        more[:, LANES:],
                    ],
                    1,
                )
            for g in range(2):
                for chunk in range(CHUNKS):
                    part = value[(2 * chunk + g) * SUB : (2 * chunk + g + 1) * SUB]
                    part = jnp.concatenate([part, lines], 0)
                    store_piece(place, chips == 1, core, row, h, f, g, chunk, part, kept, sent)


def owners_kernel(geometry, where, *refs):
    rows, tokens, _ = geometry
    half = tokens // 2
    core, member = where[0], where[3]
    sets = [refs[i : i + rows + 1] for i in range(0, len(refs) - 2, rows + 1)]
    out, sems = refs[-2:]

    def move(blocks):
        copies = []
        for step in range(rows):
            target = member ^ step
            for side, index in ((0, core), (1, 1 - core)):
                lanes = pl.ds(pl.multiple_of(index * half, half), half)
                source = blocks[rows].at[step] if side else blocks[step]
                if len(sets) == 1:
                    source = source.at[side]
                sem = sems.at[2 * step + side]
                copies.append(pltpu.make_async_copy(source, out.at[target, :, lanes], sem))
        for copy in copies:
            copy.start()
        for copy in copies:
            copy.wait()

    if len(sets) == 1:
        move(sets[0])
    else:
        for number in range(2):

            @pl.when(core == number)
            def _():
                move(sets[number])


def gather_kernel(where, *refs):
    mlp0, mlp1, attn = refs[:2], refs[2:4], refs[4:6]
    wq, wk, wv, wo, wg, wu, wd, g1, g2 = refs[6:15]
    wide, share = refs[15:]
    core, row, place = where[0], where[1], where[2]
    for step in range(4):
        peer = row ^ step
        x_bit, y_bit = peer & 1, peer >> 1
        for kind in range(2):
            h = core if kind == 0 else 1 - core
            f = jnp.where(h == 0, x_bit, y_bit)
            g = jnp.where(h == 0, y_bit, x_bit)

            @pl.when(core == 0)
            def _():
                share[...] = mlp0[kind][step]

            @pl.when(core == 1)
            def _():
                share[...] = mlp1[1 - kind][step]

            part = share[...].astype(F32)
            rows = pl.ds(pl.multiple_of(g * SUB, 8), SUB)
            tile = 2 * h + f
            columns = pl.ds(pl.multiple_of(tile * TILE, LANES), TILE)
            wg[0, rows, columns] = part[:SUB]
            wu[0, rows, columns] = part[SUB : 2 * SUB]
            wd[0, pl.ds(pl.multiple_of((2 * tile + g) * SUB, 8), SUB), :] = part[2 * SUB :]
            part = attn[kind][step, core].astype(F32)
            wide[rows, columns] = part[:SUB]
    wq[0] = wide[:, :D]
    wk[0] = wide[:, D : D + KVW]
    wo[0] = wide[:, 2 * TILE : 2 * TILE + D]
    wv[0] = wide[:, 2 * TILE + D :]
    lines = attn[0][0, core].astype(F32)[SUB:]
    for kind, out in ((0, g1), (1, g2)):
        whole = jnp.concatenate(
            [lines[2 * kind : 2 * kind + 1], lines[2 * kind + 1 : 2 * kind + 2]], 1
        )
        for chunk in range(CHUNKS):

            @pl.when(place == chunk)
            def _():
                out[...] = whole[:, chunk * 2 * SUB : (chunk + 1) * 2 * SUB]


def rotary(place):
    frequency = 10000.0 ** (-jnp.arange(HD // 2, dtype=F32) * 2.0 / HD)
    angles = place.astype(F32)[:, None] * frequency[None, :]
    cosine, sine = jnp.cos(angles), jnp.sin(angles)
    return jnp.concatenate([cosine] * 4, 1), jnp.concatenate([-sine, sine] * 2, 1)


def on_device(
    inputs,
    cotangent,
    group_ids,
    w_query,
    w_key,
    w_value,
    w_out,
    w_gate,
    w_up,
    w_down,
    gain_attn,
    gain_mlp,
):
    core = lax.axis_index("section")
    row = lax.axis_index("row")
    place = lax.axis_index("seq")
    spans = lax.axis_size("seq")
    rows, tokens, _ = inputs.shape
    half = tokens // 2
    chips = spans // rows
    member, wagon = place % rows, place // rows
    own = rows * half
    blocks = chips * rows
    length = blocks * tokens
    geometry = (rows, tokens, chips)
    flipped = half % LANES == 0
    where = jnp.stack([core, row, place, member, wagon]).astype(jnp.int32)
    whole = 0 if chips == 1 else slice(None)
    clans = [[b + rows * j for j in range(chips)] for b in range(rows)]

    def turn(step):
        return [(s, s ^ step) for s in range(spans)]

    def sems(count):
        return pltpu.SemaphoreType.DMA((count,))

    def vmem(*dims, kind=BF16):
        return pltpu.VMEM(dims, kind)

    def flip(array):
        return jnp.swapaxes(array, -1, -2)

    pack_ins = [
        flip(inputs),
        flip(cotangent),
        group_ids,
        w_query[0],
        flip(w_key[0]),
        flip(w_value[0]),
        gain_attn,
        gain_mlp,
    ]
    if flipped:
        packed = call(
            functools.partial(pack_kernel, geometry),
            pack_ins,
            [ANY] * 2 + [VMEM] * 6,
            [shape((D + PACK, half))] * rows + [shape((D, half))] * rows + [shape((D + PACK, QKV))],
            [vmem(rows, PACK, half), sems(3 * rows)],
            0,
            room=56 * 1024 * 1024,
        )
        packets, shares, w_qkv = packed[:rows], packed[rows : 2 * rows], packed[-1]
    else:
        packets, shares = [], []
        below = [jnp.sum((group_ids < i).astype(F32), 1) for i in (1, 2)]
        counts = jnp.pad(jnp.stack(below, 1), ((0, 0), (0, D - 2))).astype(BF16)
        counts = jnp.pad(counts[:, None], ((0, 0), (0, PACK - 1), (0, 0)))
        for step in range(rows):
            target = member ^ step
            for array, outs in ((inputs, packets), (cotangent, shares)):
                part = lax.dynamic_index_in_dim(array, target, 0, False)
                part = lax.dynamic_slice_in_dim(part, core * half, half, 0)
                outs.append(part)
            line = lax.dynamic_index_in_dim(counts, target, 0, False)
            packets[-1] = jnp.concatenate([packets[-1], line], 0)
        w_qkv = jnp.concatenate(
            [w_query[0], w_key[0], jnp.zeros((D, HD), BF16), w_value[0]], 1
        )
        parts, rest = [], jnp.concatenate([gain_attn, gain_mlp], 0)
        for _ in range(3):
            parts.append(rest.astype(BF16))
            rest = rest - parts[-1].astype(F32)
        lines = jnp.stack(parts, 1).reshape(6, D)
        w_qkv = jnp.concatenate([w_qkv, jnp.pad(lines, ((0, PACK - 6), (0, QKV - D)))], 0)
    packets = [packets[0]] + [
        lax.ppermute(packets[step], "seq", turn(step)) for step in range(1, rows)
    ]
    w_qkv = [w_qkv, lax.ppermute(w_qkv, "section", SWAP)]
    mine = {"gate": w_gate[0], "up": w_up[0], "down": flip(w_down[0]), "out": w_out[0]}
    gates = dict(zip(mine, [*packets[1:4], w_qkv[1]]))
    pairs = {
        name: (value, lax.ppermute(hold(value, gates[name]), "section", SWAP))
        for name, value in mine.items()
    }
    pairs["qkv"] = w_qkv

    def weights_of(*names):
        return [side for name in names for side in pairs[name]]

    if flipped:
        docs = sum(packet[D, :2].astype(F32) for packet in packets)
    else:
        docs = sum(packet[half, :2].astype(F32) for packet in packets)
    if chips > 1:
        docs = lax.psum(docs, "seq", axis_index_groups=clans)
    docs = docs.astype(jnp.int32)
    local = jnp.arange(own, dtype=jnp.int32)
    tables = rotary((wagon * rows + local // half) * tokens + core * half + local % half)

    x_in, query, kv = call(
        functools.partial(project_kernel, geometry),
        [where, *packets, *w_qkv, *tables],
        [SMEM] + [VMEM] * rows + [ANY] * 2 + [VMEM] * 2,
        [shape((rows, half, D)), shape((HQ, own, LANES)), shape((own, 2 * KVW))],
        [vmem(D, QKV), vmem(PACK, QKV), sems(2)],
        2 * own * D * QKV,
    )
    x_in = x_in.reshape(own, D)

    def exchange(kv):
        kv = kv.reshape(rows, half, 2 * KVW)
        if chips > 1:
            kv = lax.all_gather(kv, "seq", axis=0, tiled=True, axis_index_groups=clans)
        return kv, lax.ppermute(kv, "section", SWAP)

    key_scratch = [vmem(KVH, blocks, 2, half, LANES)] * 2
    head_scratch = [vmem(HQ, own, LANES, kind=F32)]
    weight = {"gate": vmem(D, FF), "up": vmem(D, FF), "down": vmem(D, FF), "out": vmem(D, D)}
    lines_scratch = vmem(PACK, QKV)
    attn_flops = 4 * HQ * own * length * LANES
    feed_flops = 2 * own * D * (D + 3 * FF)
    flat = shape((own, D))
    wide = shape((own, FF))
    heads = shape((HQ, own, LANES))
    sent_blocks = shape((rows, D, half) if flipped else (rows, half, D))

    def forward(layer, x, query, kv, *earlier):
        outs = [heads, flat, shape((own, D), F32), wide, wide, flat, sent_blocks]
        scratch = key_scratch + head_scratch
        scratch += [weight["out"], weight["gate"], weight["up"], weight["down"]]
        scratch += [lines_scratch, sems(5)]
        if layer == 0:
            outs += [heads, shape((own, 2 * KVW))]
            scratch += [vmem(D, QKV), lines_scratch, sems(2)]
            scratch += [vmem(HQ, own, LANES), vmem(own, D, kind=F32), vmem(own, FF)]
            scratch += [vmem(own, FF), sems(16)]
        else:
            scratch = [vmem(*sent_blocks.shape)] + scratch
            outs = outs[:-1] + [shape((2,) + sent_blocks.shape[1:])] * rows
        return call(
            functools.partial(forward_kernel, layer, geometry),
            [where, docs, x, query, *kv, *tables]
            + weights_of("gate", "up", "down", "out", "qkv")
            + list(earlier),
            [SMEM] * 2 + [VMEM] * 6 + [ANY] * 10 + [VMEM] * len(earlier),
            outs,
            scratch,
            attn_flops + feed_flops,
            far=(0, 2, 3, 4) if layer == 0 else (),
        )

    kv0 = exchange(kv)
    q0, att0, middle0, gate0, up0, y0, blocks0, query, kv = forward(0, x_in, query, kv0)
    shares = [shares[0]] + [
        lax.ppermute(shares[step], "seq", turn(step)) for step in range(1, rows)
    ]
    kv1 = exchange(kv)
    outs = forward(1, y0, query, kv1, blocks0)
    q1, att1, middle1, gate1, up1, y1, *pair_blocks = hold(outs, shares)
    mlp_pieces = shape((2, 2, CHUNKS, 3 * SUB, TILE))
    attn_pieces = shape((2, 2, CHUNKS, SUB + 8, TILE))

    def feed(layer, where, grads, middle, gate, up, **order):
        outs = [shape((rows, half, D))] if layer == 1 else []
        return call(
            functools.partial(feed_kernel, layer, geometry),
            [where, *grads, middle, gate, up] + weights_of("down", "qkv"),
            [SMEM] + [VMEM] * (len(grads) + 3) + [ANY] * 4,
            outs + [wide, wide, mlp_pieces, mlp_pieces],
            [vmem(own, D), vmem(D, own), vmem(own, FF), vmem(CHUNKS, D, TILE, kind=F32)]
            + [weight["down"], lines_scratch, sems(2)],
            8 * own * D * FF,
            **order,
        )

    def spread(layer, where, grad, middle, dgate, dup, att, **order):
        return call(
            functools.partial(middle_kernel, layer, geometry),
            [where, grad, middle, dgate, dup, att] + weights_of("gate", "up", "out", "qkv"),
            [SMEM] + [VMEM] * 5 + [ANY] * 8,
            [shape((own, D), F32), shape((1, D), F32), heads],
            [weight["gate"], weight["up"], weight["out"], lines_scratch, sems(4)],
            2 * own * D * (D + 2 * FF),
            light=layer == 1,
            **order,
        )

    def attention_back(where, q_aug, do_heads, kv, **order):
        return call(
            functools.partial(attend_back_kernel, geometry),
            [where, docs, q_aug, do_heads, *kv, *tables],
            [SMEM] * 2 + [VMEM] * 6,
            [
                shape((own, 5 * LANES)),
                shape((blocks, half, 2 * KVW), F32),
                shape((blocks, half, 2 * KVW)),
            ],
            key_scratch
            + head_scratch
            + [vmem(KVH, blocks, 2, half, LANES, kind=F32)] * 2,
            3 * attn_flops,
            **order,
        )

    def trade_keys(dq, dkv, dkv_sent):
        dkv_got = lax.ppermute(dkv_sent, "section", SWAP)
        if chips > 1:
            dkv = lax.psum_scatter(
                (dkv + dkv_got).astype(BF16),
                "seq",
                scatter_dimension=0,
                tiled=True,
                axis_index_groups=clans,
            ).astype(F32)
            dkv_got = jnp.zeros(dkv.shape, BF16)
        return dq, dkv.reshape(own, 2 * KVW), dkv_got.reshape(own, 2 * KVW)

    def input_back(layer, where, dm, att, x, dq, dkv, dkv_got, gain_grad, **order):
        return call(
            functools.partial(input_back_kernel, layer, geometry),
            [where, dm, att, x, dq, dkv, dkv_got, gain_grad, *w_qkv, *tables],
            [SMEM] + [VMEM] * 7 + [ANY] * 2 + [VMEM] * 2,
            [flat]
            + [shape(sent_blocks.shape[1:])] * rows
            + [attn_pieces, attn_pieces],
            [vmem(*sent_blocks.shape), vmem(own, QKV), vmem(own, D), vmem(own, 2 * TILE), vmem(D, QKV)]
            + [lines_scratch, sems(2)],
            4 * own * D * QKV + 2 * own * D * D,
            **order,
        )

    def line(section, r):
        return section * 4 + r

    first_pairs = [(line(0, r), line(0, r ^ 1)) for r in range(4)]
    first_pairs += [(line(1, r), line(1, r ^ 2)) for r in range(4)]
    second_pairs = [(line(0, r), line(0, r ^ 2)) for r in range(4)]
    second_pairs += [(line(1, r), line(1, r ^ 1)) for r in range(4)]

    def to_core(sent):
        return lax.ppermute(sent, "section", SWAP)

    def sum_cores(kept, got):
        return (kept[1].astype(F32) + got[1]).astype(BF16)

    def to_first(out):
        return lax.ppermute(out, ("section", "row"), first_pairs)

    def sum_first(kept, got, near):
        return (kept[0, 1].astype(F32) + got[0, 1] + near[1]).astype(BF16)

    def to_second(out):
        return lax.ppermute(out, ("section", "row"), second_pairs)

    def sum_second(kept, got, near, far):
        return (kept[0, 0].astype(F32) + got[0, 0] + near[0] + far).astype(BF16)

    def to_seq(total):
        if chips > 1:
            return [lax.psum(total, "seq")]
        return [total[0]] + [
            lax.ppermute(total[spot], "seq", turn(step)) for spot, step in ((2, 1), (1, 2), (3, 3))
        ]

    def part_of(total, step):
        if chips > 1:
            return (total, total) if step == 1 else (lax.psum(total, "seq"),) * 2
        count = total.shape[0] // 2
        return total[:count], lax.ppermute(total[count:], "seq", turn(step))

    def sum_two(low, got):
        return low if chips > 1 else (low.astype(F32) + got).astype(BF16)

    def sum_seq(first, others):
        return sum((part.astype(F32) for part in others), first.astype(F32)).astype(BF16)

    def to_rows(blocks):
        return list(blocks[:1]) + [
            lax.ppermute(blocks[step], "seq", turn(step)) for step in range(1, rows)
        ]

    def to_owners(sets):
        if flipped:
            return call(
                functools.partial(owners_kernel, geometry),
                [where, *sum(sets, [])],
                [SMEM] + [ANY] * ((rows + 1) * len(sets)),
                [shape((rows, D, tokens))],
                [sems(2 * rows)],
                0,
            )[0]
        out = jnp.zeros((rows, 2, half, D), BF16)
        for step in range(rows):
            if len(sets) == 1:
                pair = [sets[0][step][0], sets[0][rows][step][1]]
            else:
                pair = [
                    jnp.where(core == 0, sets[0][step], sets[1][step]),
                    jnp.where(core == 0, sets[0][rows][step], sets[1][rows][step]),
                ]
            pair = jnp.where(core == 0, jnp.stack(pair), jnp.stack(pair[::-1]))
            out = lax.dynamic_update_index_in_dim(out, pair, member ^ step, 0)
        return flip(out.reshape(rows, tokens, D))

    def to_all(piece):
        return [piece] + [
            lax.ppermute(piece, "row", [(r, r ^ step) for r in range(4)]) for step in range(1, 4)
        ]

    ys = to_rows(pair_blocks)
    grad1, dgate, dup, kept_m1, sent = feed(1, where, shares, middle1, gate1, up1)
    grad1 = grad1.reshape(own, D)
    got_m1 = to_core(sent)

    dm, gain_grad, do_heads = hold(
        spread(1, where, grad1, middle1, dgate, dup, att1), ys[1], ys[2], got_m1
    )

    out = sum_cores(hold(kept_m1, dm), got_m1)
    near_m1 = to_first(out)
    kept_m1, *outs = hold(
        (kept_m1, *attention_back(where, q1, do_heads, kv1)), ys[3], near_m1
    )
    dq, dkv, dkv_got = trade_keys(*outs)

    out = sum_first(kept_m1, got_m1, near_m1)
    far_m1 = to_second(out)
    outs = input_back(
        1, hold(where, out), dm, att1, y0, dq, dkv, dkv_got, gain_grad, stack=ys
    )
    kept_m1, pile, dx1, *blocks1, kept_a1, sent = hold((kept_m1, *outs), far_m1)
    got_a1 = to_core(sent)
    ys.append(to_core(pile))

    total = sum_second(kept_m1, got_m1, near_m1, far_m1)
    low_m1, got = part_of(total, 1)
    outs = feed(0, hold(where, total), [dx1], middle0, gate0, up0)
    dgate, dup, kept_m0, sent = hold(outs, ys[rows], got_a1, got)
    got_m0 = to_core(sent)

    low_m1, got = part_of(sum_two(hold(low_m1, dgate), got), 2)
    out = sum_cores(hold(kept_a1, dgate), got_a1)
    near_a1 = to_first(out)
    activations = to_owners([ys])
    outs = spread(0, hold(where, out, low_m1), dx1, middle0, dgate, dup, att0)
    dm, gain_grad, do_heads, low_m1 = hold((*outs, low_m1), activations, near_a1, got_m0, got)
    piece_m1 = sum_two(low_m1, got)[whole]

    out_a1 = sum_first(hold(kept_a1, dm), got_a1, near_a1)
    far_a1 = to_second(out_a1)
    out_m0 = sum_cores(hold(kept_m0, dm), got_m0)
    near_m0 = to_first(out_m0)
    dxs1 = to_rows(hold(blocks1, dm))
    outs = attention_back(hold(where, out_a1, out_m0), q0, do_heads, kv0)
    kept_a1, kept_m0, *outs = hold((kept_a1, kept_m0, *outs), far_a1, near_m0, dxs1)
    dq, dkv, dkv_got = trade_keys(*outs)

    total_a1 = sum_second(kept_a1, got_a1, near_a1, far_a1)
    low_a1, got = part_of(total_a1, 1)
    out = sum_first(kept_m0, got_m0, near_m0)
    far_m0 = to_second(out)
    outs = input_back(
        0, hold(where, out, total_a1), dm, att0, x_in, dq, dkv, dkv_got, gain_grad, stack=dxs1
    )
    mlp1 = to_all(hold(piece_m1, out))
    kept_m0, low_a1, pile, dx0, *blocks0, kept_a0, sent = hold(
        (kept_m0, low_a1, *outs), far_m0, got, mlp1[1]
    )

    got_a0 = to_core(sent)
    total = sum_second(kept_m0, got_m0, near_m0, far_m0)
    low_m0, got_low = part_of(total, 1)
    out = sum_cores(hold(kept_a0, total), got_a0)
    near_a0 = to_first(out)
    kept_a0, low_m0 = hold((kept_a0, low_m0), got_low, near_a0)
    low_m0, got_low = part_of(sum_two(low_m0, got_low), 2)
    low_a1, got_a1 = part_of(sum_two(hold(low_a1, kept_a0), got), 2)
    out = sum_first(kept_a0, got_a0, near_a0)
    far_a0 = to_second(out)
    nearest = lax.ppermute(hold(blocks0[1], kept_a0), "seq", turn(1))
    total = sum_second(hold(kept_a0, got_low, nearest), got_a0, near_a0, far_a0)
    parts_a0 = to_seq(total)
    low_m0, low_a1, blocks0, pile, mlp1 = hold((low_m0, low_a1, blocks0, pile, mlp1), total)
    mlp0 = to_all(sum_two(low_m0, got_low)[whole])
    mlp1 = jnp.stack(mlp1)
    mlp1 = lax.ppermute(mlp1, "section", [(0, 1)]), mlp1
    dxs1.append(lax.ppermute(pile, "section", [(0, 1)]))
    dxs0 = [blocks0[0], nearest] + [
        lax.ppermute(blocks0[step], "seq", turn(step)) for step in range(2, rows)
    ]
    attn = jnp.stack([sum_seq(parts_a0[0], parts_a0[1:]), sum_two(low_a1, got_a1)[whole]])
    attn = hold(attn, mlp1[0], dxs1[rows])
    mlp0 = hold(mlp0, attn)
    attn = to_all(attn)
    mlp0 = jnp.stack(mlp0)
    mlp0 = mlp0, lax.ppermute(mlp0, "section", [(1, 0)])
    dxs0 = hold(dxs0, attn)
    attn = jnp.stack(attn)
    attn = attn, to_core(attn)
    dxs0.append(lax.ppermute(hold(jnp.stack(dxs0), attn[0]), "section", [(1, 0)]))
    input_grads = to_owners([dxs0, dxs1])
    input_grads = flip(input_grads)[None]
    activations = flip(activations)[None]
    share = D // spans
    if chips == 1:
        grads = call(
            gather_kernel,
            [where, *mlp0, *mlp1, *attn],
            [SMEM] + [VMEM] * 6,
            [shape((1, share, width), F32) for width in (D, KVW, KVW, D, FF, FF)]
            + [shape((1, D, TILE), F32)]
            + [shape((1, share), F32)] * 2,
            [vmem(2 * SUB, FF, kind=F32), vmem(3 * SUB, TILE)],
            0,
        )
        grads = list(grads)
        grads[6] = flip(grads[6])
        return (activations, input_grads) + tuple(grads)

    def ordered(parts):
        parts = parts.reshape(2, 4, *parts.shape[1:]).swapaxes(0, 1).astype(F32)
        parts = jnp.take(parts, jnp.arange(4) ^ row, axis=0)
        parts = jnp.take(parts, jnp.arange(2) ^ core, axis=1)
        parts = parts.reshape((2, 2) + parts.shape[1:])
        return jnp.stack([parts[:, :, 0].swapaxes(0, 1), parts[:, :, 1]])

    def rows_of(part):
        full = part.transpose(3, 2, 4, 0, 1, 5).reshape(D, FF)
        return lax.dynamic_slice_in_dim(full, place * share, share, 0)[None]

    mlp1 = jnp.concatenate([mlp1[1], mlp1[0]], 0)
    mlp = ordered(jnp.where(core == 0, jnp.concatenate(mlp0, 0), mlp1))
    attn = ordered(lax.dynamic_index_in_dim(jnp.concatenate(attn, 0), core, 1, False))
    downs = mlp[..., 2 * SUB :, :].transpose(0, 1, 2, 4, 3, 5).reshape(D, FF)
    downs = lax.dynamic_slice_in_dim(downs, place * (FF // spans), FF // spans, 1).T[None]
    full = rows_of(attn[..., :SUB, :])
    lines = attn[0, 0, 0, 0, SUB : SUB + 4].reshape(2, 2 * TILE)[:, :D]
    lines = lax.dynamic_slice_in_dim(lines, place * share, share, 1)
    return (
        activations,
        input_grads,
        full[..., :D],
        full[..., D : D + KVW],
        full[..., 2 * TILE + D :],
        full[..., 2 * TILE : 2 * TILE + D],
        rows_of(mlp[..., :SUB, :]),
        rows_of(mlp[..., SUB : 2 * SUB, :]),
        downs,
        lines[:1],
        lines[1:],
    )


def solution(mesh):
    weights = P("section", None, None)
    shares = P("section", "seq", None)
    return jax.shard_map(
        on_device,
        mesh=mesh,
        in_specs=(P("row", "seq", None), P("row", "seq", None), P("row", "seq"))
        + (weights,) * 7
        + (P("section", None),) * 2,
        out_specs=(P("section", "row", "seq", None),) * 2
        + (shares,) * 7
        + (P("section", "seq"),) * 2,
        check_vma=False,
    )
```
